32 devices in a mesh: dp: 2 (over x), rows: 4 (over y, core), cols: 4 (over z).
Axes of the slice: x: 2, y: 2, z: 4, core: 2. Of those that a mesh axis runs over, the one named last changes fastest.
Arguments:
- hidden_in: bfloat16 [4096, 1536], P(('dp', 'rows'), 'cols'), may hold values from -6 to 6
- lengths: int32 [2, 2], P('dp'), may hold values from 128 to 1792, as said below
- norm1_gain: float32 [1536], P('cols'), may hold values from 0.5 to 1.5
- z_weight: bfloat16 [1536, 3072], P('cols', 'rows'), may hold values from -0.15625 to 0.15625
- x_weight: bfloat16 [1536, 3072], P('cols', 'rows'), may hold values from -0.15625 to 0.15625
- bcdt_weight: bfloat16 [1536, 304], P('cols'), may hold values from -0.15625 to 0.15625
- conv_x_weight: float32 [4, 3072], P(None, 'rows'), may hold values from -3 to 3
- conv_x_bias: float32 [3072], P('rows'), may hold values from -3 to 3
- conv_bc_weight: float32 [4, 256], replicated, may hold values from -3 to 3
- conv_bc_bias: float32 [256], replicated, may hold values from -3 to 3
- a_log: float32 [48], P('rows'), may hold values from -1 to 1
- d_skip: float32 [48], P('rows'), may hold values from 0.5 to 1.5
- dt_bias: float32 [48], P('rows'), may hold values from -8 to -2
- gate_gain: float32 [3072], P('rows'), may hold values from 0.5 to 1.5
- mix_out_weight: bfloat16 [3072, 1536], P('rows', 'cols'), may hold values from -0.109375 to 0.109375
- norm2_gain: float32 [1536], P('cols'), may hold values from 0.5 to 1.5
- q_weight: bfloat16 [1536, 1536], P('cols', 'rows'), may hold values from -0.15625 to 0.15625
- k_weight: bfloat16 [1536, 1536], P('cols', 'rows'), may hold values from -0.15625 to 0.15625
- v_weight: bfloat16 [1536, 1536], P('cols', 'rows'), may hold values from -0.15625 to 0.15625
- att_out_weight: bfloat16 [1536, 1536], P('rows', 'cols'), may hold values from -1.25 to 1.25
- norm3_gain: float32 [1536], P('cols'), may hold values from 0.5 to 1.5
- up_weight: bfloat16 [1536, 6144], P('cols', 'rows'), may hold values from -0.15625 to 0.15625
- down_weight: bfloat16 [6144, 1536], P('rows', 'cols'), may hold values from -0.078125 to 0.078125
- grad_output: bfloat16 [4096, 1536], P(('dp', 'rows'), 'cols'), may hold values from -6 to 6
Outputs:
- output: bfloat16 [4096, 1536], P(('dp', 'rows'), 'cols')
- input_grad: float32 [4096, 1536], P(('dp', 'rows'), 'cols')
- norm1_gain_grad: float32 [1536], replicated
- z_weight_grad: float32 [1536, 3072], P('cols', 'rows')
- x_weight_grad: float32 [1536, 3072], P('cols', 'rows')
- bcdt_weight_grad: float32 [1536, 304], replicated
- conv_x_weight_grad: float32 [4, 3072], replicated
- conv_x_bias_grad: float32 [3072], replicated
- conv_bc_weight_grad: float32 [4, 256], replicated
- conv_bc_bias_grad: float32 [256], replicated
- a_log_grad: float32 [48], replicated
- d_skip_grad: float32 [48], replicated
- dt_bias_grad: float32 [48], replicated
- gate_gain_grad: float32 [3072], replicated
- mix_out_weight_grad: float32 [3072, 1536], P('rows', 'cols')
- norm2_gain_grad: float32 [1536], replicated
- q_weight_grad: float32 [1536, 1536], P('cols', 'rows')
- k_weight_grad: float32 [1536, 1536], P('cols', 'rows')
- v_weight_grad: float32 [1536, 1536], P('cols', 'rows')
- att_out_weight_grad: float32 [1536, 1536], P('rows', 'cols')
- norm3_gain_grad: float32 [1536], replicated
- up_weight_grad: float32 [1536, 6144], P('cols', 'rows')
- down_weight_grad: float32 [6144, 1536], P('rows', 'cols')
The draws below stay inside these ranges and needn't reach their ends.
Inputs may be any that keep to these rules, and one draw needn't show every extreme that they name: `lengths`: row g holds the two packed sequences of group g, in order from place 0, then padding: the first is longer than three quarters of 2048, the two together take at most 2048 places.
All inputs are finite; a program needn't handle non-finite values.
Results may differ from the reference program's by a relative error of at most 0.018.
Values may be sent and summed in bfloat16 or wider, within the bound.
A program may use at most 256 MiB of HBM per device.

```python
import jax
import jax.numpy as jnp
from jax import lax

D = 1536
HEADS = 48
HEAD_DIM = 64
STATE = 128
CONV = 4
SPAN = 256
AHEADS = 24
AHEAD_DIM = 64
FF = 6144
TOK_GRP = 2048
INNER = 3072
BCDT = 304
TOKENS = 4096
N_DP = 2


def draw_lengths(key, part):
    key = jax.random.fold_in(key, 11)
    lead_key, second_key, pick_key = jax.random.split(key, 3)
    longest = TOK_GRP - TOK_GRP // 8
    shortest = TOK_GRP // 16
    leading = jax.random.randint(lead_key, (N_DP,), 3 * TOK_GRP // 4 + 1, longest + 1)
    second = jax.random.randint(second_key, (N_DP,), shortest, TOK_GRP - leading + 1)
    chosen = jax.random.randint(pick_key, (), 0, N_DP)
    marked = jnp.arange(N_DP) == chosen
    leading = jnp.where(marked, longest, leading)
    second = jnp.where(marked, shortest, second)
    return jnp.stack([leading, second], axis=1).astype(jnp.int32)


def levels(key, shape, cuts, smallest, largest):
    def one(position, parts):
        steps = jax.random.uniform(jax.random.fold_in(jax.random.fold_in(key, 6), position), (parts,), jnp.float32, smallest / len(cuts), largest / len(cuts))
        return jnp.repeat(jnp.exp(steps), shape[position] // parts).reshape((-1,) + (1,) * (len(shape) - position - 1))

    factor_of = one(*cuts[0])
    for cut in cuts[1:]:
        factor_of = factor_of * one(*cut)
    return factor_of


def normal_values(stream_key, extent, spread, bound, cuts=(), kind=jnp.bfloat16):
    array = jax.random.normal(stream_key, extent, jnp.float32) * spread
    if len(cuts) > 0:
        array = levels(stream_key, extent, cuts, -0.22, 0.18) * array
    return jnp.clip(array, min=-bound, max=bound).astype(kind)


def setup_inputs(seed: int = 0) -> dict:
    splits = jax.random.split(jax.random.key(seed), 25)
    return {
        "hidden_in": normal_values(splits[0], (TOKENS, D), 1.0, 6.0, ((0, 8), (1, 4))),
        "lengths": draw_lengths(jax.random.fold_in(splits[24], 71), 0),
        "norm1_gain": jnp.clip(1.0 + 0.1 * jax.random.normal(splits[2], (D,), jnp.float32), 0.5, 1.5),
        "z_weight": normal_values(splits[3], (D, INNER), D ** -0.5, 0.15625, ((0, 4), (1, 4))),
        "x_weight": normal_values(splits[4], (D, INNER), D ** -0.5, 0.15625, ((0, 4), (1, 4))),
        "bcdt_weight": normal_values(splits[5], (D, BCDT), D ** -0.5, 0.15625, ((0, 4),)),
        "conv_x_weight": normal_values(splits[6], (CONV, INNER), CONV ** -0.5, 3.0, ((1, 4),), jnp.float32),
        "conv_x_bias": normal_values(splits[7], (INNER,), 0.5, 3.0, ((0, 4),), jnp.float32),
        "conv_bc_weight": normal_values(splits[8], (CONV, 2 * STATE), CONV ** -0.5, 3.0, (), jnp.float32),
        "conv_bc_bias": normal_values(splits[9], (2 * STATE,), 0.5, 3.0, (), jnp.float32),
        "a_log": jnp.clip(jax.random.uniform(splits[10], (HEADS,), jnp.float32, -1.0, 1.0) * levels(splits[10], (HEADS,), ((0, 4),), -0.4, 0.0), -1.0, 1.0),
        "d_skip": jnp.clip(0.5 + 1.0 * jax.random.uniform(splits[11], (HEADS,), jnp.float32) ** levels(splits[11], (HEADS,), ((0, 4),), -0.2, 0.2), 0.5, 1.5),
        "dt_bias": jnp.clip(-8.0 + 6.0 * jax.random.uniform(splits[12], (HEADS,), jnp.float32) ** levels(splits[12], (HEADS,), ((0, 4),), -0.2, 0.2), -8.0, -2.0),
        "gate_gain": jnp.clip(1.0 + 0.1 * jax.random.normal(splits[13], (INNER,), jnp.float32), 0.5, 1.5),
        "mix_out_weight": normal_values(splits[14], (INNER, D), INNER ** -0.5, 0.109375, ((0, 4), (1, 4))),
        "norm2_gain": jnp.clip(1.0 + 0.1 * jax.random.normal(splits[15], (D,), jnp.float32), 0.5, 1.5),
        "q_weight": normal_values(splits[16], (D, D), D ** -0.5, 0.15625, ((0, 4), (1, 4))),
        "k_weight": normal_values(splits[17], (D, D), D ** -0.5, 0.15625, ((0, 4), (1, 4))),
        "v_weight": normal_values(splits[18], (D, D), D ** -0.5, 0.15625, ((0, 4), (1, 4))),
        "att_out_weight": normal_values(splits[19], (D, D), (D // 64) ** -0.5, 1.25, ((0, 4), (1, 4))),
        "norm3_gain": jnp.clip(1.0 + 0.1 * jax.random.normal(splits[20], (D,), jnp.float32), 0.5, 1.5),
        "up_weight": normal_values(splits[21], (D, FF), D ** -0.5, 0.15625, ((0, 4), (1, 4))),
        "down_weight": normal_values(splits[22], (FF, D), FF ** -0.5, 0.078125, ((0, 4), (1, 4))),
        "grad_output": normal_values(splits[23], (TOKENS, D), 1.0, 6.0, ((0, 8), (1, 4))),
    }


EPS = 1e-05
HIGH = lax.Precision.HIGHEST

@jax.custom_vjp
def low(v):
    return lax.optimization_barrier(v.astype(jnp.bfloat16)).astype(jnp.float32)

@jax.custom_vjp
def low_back(v):
    return v

def low_keep(v):
    return (low(v), None)

def low_pass(kept, grad):
    return (grad,)

def back_keep(v):
    return (v, None)

def back_low(kept, grad):
    return (low(grad),)
low.defvjp(low_keep, low_pass)
low_back.defvjp(back_keep, back_low)

def exact_dot(left, right):
    return jnp.dot(left, right, precision=HIGH, preferred_element_type=jnp.float32)

def rms_scale(values):
    return lax.rsqrt(lax.optimization_barrier(jnp.mean(values * values, axis=-1, keepdims=True)) + EPS)

def segments_of(places, seq_lens):
    first_part = (places >= seq_lens[0]).astype(jnp.int32)
    second_part = (places >= seq_lens[0] + seq_lens[1]).astype(jnp.int32)
    return jnp.where(places < 0, -1, first_part + second_part).astype(jnp.int32)

def causal_conv(values, weight, conv_bias, segment):
    summed = conv_bias[None, :] + weight[CONV - 1][None, :] * values
    for shift_by in range(1, CONV):
        shifted = jnp.concatenate([jnp.zeros((shift_by, values.shape[1]), jnp.float32), values[:-shift_by]], axis=0)
        shifted_seg = jnp.concatenate([jnp.full((shift_by,), -1, jnp.int32), segment[:-shift_by]])
        keeping = (shifted_seg == segment).astype(jnp.float32)
        summed = summed + weight[CONV - 1 - shift_by][None, :] * shifted * keeping[:, None]
    return summed

def ssd_block(carried, w_block, b_block, c_block, r_block, s_block, prior_seg):
    length = r_block.shape[0]
    cumulative = jnp.cumsum(r_block, axis=0)
    order = jnp.arange(length, dtype=jnp.int32)
    allowed = (order[None, :] <= order[:, None]) & (s_block[None, :] == s_block[:, None])
    gaps = cumulative[:, None, :] - cumulative[None, :, :]
    decay = jnp.where(allowed[:, :, None], jnp.exp(jnp.where(allowed[:, :, None], gaps, 0.0)), 0.0)
    scores = jnp.einsum('pn,qn->pq', c_block, b_block, precision=HIGH)
    mixing = scores[:, :, None] * decay
    result = jnp.einsum('pqh,qhm->phm', mixing, w_block, precision=HIGH)
    reach = (s_block == prior_seg).astype(jnp.float32)[:, None] * jnp.exp(cumulative)
    result = result + jnp.einsum('pn,hmn->phm', c_block, carried, precision=HIGH) * reach[:, :, None]
    tail_decay = jnp.exp(cumulative[-1][None, :] - cumulative) * (s_block == s_block[-1]).astype(jnp.float32)[:, None]
    local_state = jnp.einsum('qh,qhm,qn->hmn', tail_decay, w_block, b_block, precision=HIGH)
    through = jnp.exp(cumulative[-1]) * (s_block[-1] == prior_seg).astype(jnp.float32)
    return (result, through[:, None, None] * carried + local_state)

def ssd_group(signal, b_matrix, c_matrix, step_size, rate, segment):
    blocks = TOK_GRP // SPAN
    priors = jnp.concatenate([jnp.full((1,), -1, jnp.int32), segment[:-1]]).reshape(blocks, SPAN)[:, 0]
    weighted = signal * step_size[:, :, None]
    pieces = (weighted.reshape(blocks, SPAN, HEADS, HEAD_DIM), b_matrix.reshape(blocks, SPAN, STATE), c_matrix.reshape(blocks, SPAN, STATE), rate.reshape(blocks, SPAN, HEADS), segment.reshape(blocks, SPAN), priors)

    def block_step(carried, piece_set):
        w_block, b_block, c_block, r_block, s_block, prior_seg = piece_set
        result, next_state = ssd_block(carried, w_block, b_block, c_block, r_block, s_block, prior_seg)
        return (next_state, result)
    zero_state = jnp.zeros((HEADS, HEAD_DIM, STATE), jnp.float32)
    last_state, y_blocks = lax.scan(jax.checkpoint(block_step), zero_state, pieces)
    return y_blocks.reshape(TOK_GRP, HEADS, HEAD_DIM)

def group_forward(weights, hidden, seq_lens):
    norm1_gain, z_weight, x_weight, bcdt_weight, conv_x_weight, conv_x_bias, conv_bc_weight, conv_bc_bias, a_log, d_skip, dt_bias, gate_gain, mix_out_weight, norm2_gain, q_weight, k_weight, v_weight, att_out_weight, norm3_gain, up_weight, down_weight = weights
    places = jnp.arange(TOK_GRP, dtype=jnp.int32)
    segment = segments_of(places, seq_lens)
    valid = (places < seq_lens[0] + seq_lens[1]).astype(jnp.float32)
    normed = low(hidden * rms_scale(hidden) * norm1_gain)
    gate_pre = low_back(exact_dot(normed, z_weight))
    x_pre = low_back(exact_dot(normed, x_weight))
    bcdt = low_back(exact_dot(normed, bcdt_weight))
    signal = jax.nn.silu(causal_conv(x_pre, conv_x_weight, conv_x_bias, segment)).reshape(TOK_GRP, HEADS, HEAD_DIM)
    bc_act = jax.nn.silu(causal_conv(bcdt[:, :2 * STATE], conv_bc_weight, conv_bc_bias, segment))
    step_size = jax.nn.softplus(bcdt[:, 2 * STATE:] + dt_bias[None, :])
    rate = -jnp.exp(a_log)[None, :] * step_size
    mixed = ssd_group(signal, bc_act[:, :STATE], bc_act[:, STATE:], step_size, rate, segment)
    mixed = mixed + d_skip[None, :, None] * signal
    gated = mixed.reshape(TOK_GRP, INNER) * jax.nn.silu(gate_pre)
    gated = low(gated * rms_scale(gated) * gate_gain)
    hidden = hidden + low_back(exact_dot(gated, mix_out_weight))
    normed = low(hidden * rms_scale(hidden) * norm2_gain)
    queries = low(low_back(exact_dot(normed, q_weight))).reshape(TOK_GRP, AHEADS, AHEAD_DIM).transpose(1, 0, 2)
    keys_all = low(low_back(exact_dot(normed, k_weight))).reshape(TOK_GRP, AHEADS, AHEAD_DIM).transpose(1, 0, 2)
    values_all = low(low_back(exact_dot(normed, v_weight))).reshape(TOK_GRP, AHEADS, AHEAD_DIM).transpose(1, 0, 2)
    allowed = (places[None, :] <= places[:, None]) & (segment[None, :] == segment[:, None])

    def one_head(piece_set):
        q_head, k_head, v_head = piece_set
        scores = low_back(exact_dot(q_head, k_head.T)) * AHEAD_DIM ** (-0.5)
        scores = jnp.where(allowed, scores, -jnp.inf)
        row_top = lax.optimization_barrier(jnp.max(scores, axis=1, keepdims=True))
        powers = jnp.exp(scores - row_top)
        probs = powers / lax.optimization_barrier(jnp.sum(powers, axis=1, keepdims=True))
        return exact_dot(low(probs), v_head)
    heads_out = lax.map(jax.checkpoint(one_head), (queries, keys_all, values_all))
    attended = low(low_back(heads_out.transpose(1, 0, 2).reshape(TOK_GRP, D)))
    hidden = hidden + low_back(exact_dot(attended, att_out_weight))
    normed = low(hidden * rms_scale(hidden) * norm3_gain)
    activated = low_back(exact_dot(normed, up_weight))
    hidden_act = low(jax.nn.gelu(activated, approximate=True))
    hidden = hidden + low_back(exact_dot(hidden_act, down_weight))
    return hidden * valid[:, None]

def reference(hidden_in, lengths, norm1_gain, z_weight, x_weight, bcdt_weight, conv_x_weight, conv_x_bias, conv_bc_weight, conv_bc_bias, a_log, d_skip, dt_bias, gate_gain, mix_out_weight, norm2_gain, q_weight, k_weight, v_weight, att_out_weight, norm3_gain, up_weight, down_weight, grad_output):
    listed = [norm1_gain, z_weight, x_weight, bcdt_weight, conv_x_weight, conv_x_bias, conv_bc_weight, conv_bc_bias, a_log, d_skip, dt_bias, gate_gain, mix_out_weight, norm2_gain, q_weight, k_weight, v_weight, att_out_weight, norm3_gain, up_weight, down_weight]
    params = tuple((tensor.astype(jnp.float32) for tensor in listed))
    hidden = hidden_in.astype(jnp.float32).reshape(N_DP, TOK_GRP, D)

    def forward(hidden_all, weights):

        def per_group(piece_set):
            return group_forward(weights, piece_set[0], piece_set[1])
        return lax.map(jax.checkpoint(per_group), (hidden_all, lengths))
    result, pullback = jax.vjp(forward, hidden, params)
    hidden_grad, weight_grads = pullback(grad_output.astype(jnp.float32).reshape(N_DP, TOK_GRP, D))
    norm1_gain_grad, z_weight_grad, x_weight_grad, bcdt_weight_grad, conv_x_weight_grad, conv_x_bias_grad, conv_bc_weight_grad, conv_bc_bias_grad, a_log_grad, d_skip_grad, dt_bias_grad, gate_gain_grad, mix_out_weight_grad, norm2_gain_grad, q_weight_grad, k_weight_grad, v_weight_grad, att_out_weight_grad, norm3_gain_grad, up_weight_grad, down_weight_grad = weight_grads
    return (result.reshape(TOKENS, D).astype(jnp.bfloat16), hidden_grad.reshape(TOKENS, D), norm1_gain_grad, z_weight_grad, x_weight_grad, bcdt_weight_grad, conv_x_weight_grad, conv_x_bias_grad, conv_bc_weight_grad, conv_bc_bias_grad, a_log_grad, d_skip_grad, dt_bias_grad, gate_gain_grad, mix_out_weight_grad, norm2_gain_grad, q_weight_grad, k_weight_grad, v_weight_grad, att_out_weight_grad, norm3_gain_grad, up_weight_grad, down_weight_grad)
```

```python
import functools
import jax, jax.numpy as jnp
from jax import lax
from jax.experimental import pallas as pl
from jax.experimental.pallas import tpu as pltpu
MESH = pl.DeviceIdType.MESH
NC = 4
F32, BF = jnp.float32, jnp.bfloat16


def copy_to(src, dst, send, recv, dev):
    return pltpu.make_async_remote_copy(src_ref=src, dst_ref=dst, send_sem=send, recv_sem=recv, device_id=dev, device_id_type=MESH)


def greet(r, c):
    barrier = pltpu.get_barrier_semaphore()
    pl.semaphore_signal(barrier, inc=1, device_id={"rows": r ^ 1}, device_id_type=MESH)
    pl.semaphore_signal(barrier, inc=1, device_id={"rows": r ^ 2}, device_id_type=MESH)

    @pl.when(c > 0)
    def _():
        pl.semaphore_signal(barrier, inc=1, device_id={"cols": c - 1}, device_id_type=MESH)

    @pl.when(c < NC - 1)
    def _():
        pl.semaphore_signal(barrier, inc=1, device_id={"cols": c + 1}, device_id_type=MESH)

    count = 2 + jnp.where(c > 0, 1, 0) + jnp.where(c < NC - 1, 1, 0)
    pl.semaphore_wait(barrier, count)


def ag_kernel(native, x_ref, out_ref, recv, zr_s, zl_s, y_s, k_s, loc):
    r, c = lax.axis_index("rows"), lax.axis_index("cols")
    S, W = x_ref.shape
    greet(r, c)

    def slab(rr, cc):
        if native:
            return out_ref.at[pl.ds(pl.multiple_of(rr * S, 16), S), pl.ds(pl.multiple_of(cc * W, 128), W)]
        return out_ref.at[pl.ds(pl.multiple_of((rr * NC + cc) * S, 16), S)]

    def right(cc, src):
        return copy_to(src, slab(r, cc), zr_s.at[cc], recv.at[r * NC + cc], {"cols": c + 1})

    def left(cc, src):
        return copy_to(src, slab(r, cc), zl_s.at[cc], recv.at[r * NC + cc], {"cols": c - 1})

    def ycopy(cc, src):
        return copy_to(src, slab(r, cc), y_s.at[cc], recv.at[r * NC + cc], {"rows": r ^ 2})

    def kcopy(rr, cc, src):
        return copy_to(src, slab(rr, cc), k_s.at[(rr >> 1) * NC + cc], recv.at[rr * NC + cc], {"rows": r ^ 1})

    def got(rr, cc):
        copy_to(slab(rr, cc), slab(rr, cc), k_s.at[0], recv.at[rr * NC + cc], {"rows": r ^ 1}).wait_recv()

    @pl.when(c < NC - 1)
    def _():
        right(c, x_ref).start()

    @pl.when(c > 0)
    def _():
        left(c, x_ref).start()
    ycopy(c, x_ref).start()
    kcopy(r, c, x_ref).start()
    own = pltpu.make_async_copy(x_ref, slab(r, c), loc)
    own.start()

    def from_y(cc):
        got(r ^ 2, cc)
        kcopy(r ^ 2, cc, slab(r ^ 2, cc)).start()

    for d in range(1, NC):
        @pl.when(c >= d)
        def _():
            cc = c - d
            got(r, cc)

            @pl.when(c < NC - 1)
            def _():
                right(cc, slab(r, cc)).start()
            ycopy(cc, slab(r, cc)).start()
            kcopy(r, cc, slab(r, cc)).start()

        @pl.when(c + d < NC)
        def _():
            cc = c + d
            got(r, cc)

            @pl.when(c > 0)
            def _():
                left(cc, slab(r, cc)).start()
            ycopy(cc, slab(r, cc)).start()
            kcopy(r, cc, slab(r, cc)).start()
        if d == 1:
            from_y(c)
        else:
            @pl.when(c >= d - 1)
            def _():
                from_y(c - (d - 1))

            @pl.when(c + d - 1 < NC)
            def _():
                from_y(c + d - 1)
    d = NC

    @pl.when(c >= d - 1)
    def _():
        from_y(c - (d - 1))

    @pl.when(c + d - 1 < NC)
    def _():
        from_y(c + d - 1)
    for cc in range(NC):
        got(r ^ 1, cc)
        got(r ^ 3, cc)
    own.wait()
    for cc in range(NC):
        y_c = ycopy(cc, slab(r, cc))
        y_c.wait_send()
        kcopy(r, cc, slab(r, cc)).wait_send()
        kcopy(r ^ 2, cc, slab(r ^ 2, cc)).wait_send()

        @pl.when((cc <= c) & (c < NC - 1))
        def _():
            right(cc, slab(r, cc)).wait_send()

        @pl.when((cc >= c) & (c > 0))
        def _():
            left(cc, slab(r, cc)).wait_send()


def gather16(x, cid, native):
    S, D = x.shape
    return pl.pallas_call(
        functools.partial(ag_kernel, native),
        out_shape=jax.ShapeDtypeStruct((4 * S, NC * D) if native else (16 * S, D), x.dtype),
        in_specs=[pl.BlockSpec(memory_space=pltpu.VMEM)],
        out_specs=pl.BlockSpec(memory_space=pltpu.VMEM),
        scratch_shapes=[pltpu.SemaphoreType.DMA((16,)), pltpu.SemaphoreType.DMA((NC,)), pltpu.SemaphoreType.DMA((NC,)),
                        pltpu.SemaphoreType.DMA((NC,)), pltpu.SemaphoreType.DMA((2 * NC,)), pltpu.SemaphoreType.DMA],
        compiler_params=pltpu.CompilerParams(collective_id=cid, has_side_effects=True, vmem_limit_bytes=48 << 20),
        cost_estimate=pl.CostEstimate(flops=0, bytes_accessed=64 << 20, transcendentals=0),
    )(x)


def all_gather16(x, cid):
    return gather16(x, cid, False)


def gather_native(x, cid):
    return gather16(x, cid, True)


def rs_kernel(p_ref, o_ref, k_buf, y_buf, l_buf, r_buf, k_out, y_out, zr_out, zl_out,
              k_s, k_r, y_s, y_r, zr_s, zr_r, zl_s, zl_r):
    r, c = lax.axis_index("rows"), lax.axis_index("cols")
    S, D = o_ref.shape
    yy, kk = r >> 1, r & 1
    greet(r, c)

    def mine(rr, cc):
        return p_ref.at[pl.ds(pl.multiple_of((rr * NC + cc) * S, 16), S)]

    def kcopy(y2, cc):
        return copy_to(mine(y2 * 2 + (1 - kk), cc), k_buf.at[y2, cc], k_s.at[y2 * NC + cc], k_r.at[y2 * NC + cc], {"rows": r ^ 1})

    def ycopy(cc):
        return copy_to(y_out.at[cc], y_buf.at[cc], y_s.at[cc], y_r.at[cc], {"rows": r ^ 2})

    def rcopy(cc):
        return copy_to(zr_out.at[cc], r_buf.at[cc], zr_s.at[cc], zr_r.at[cc], {"cols": c + 1})

    def lcopy(cc):
        return copy_to(zl_out.at[cc], l_buf.at[cc], zl_s.at[cc], zl_r.at[cc], {"cols": c - 1})

    def order(f):
        for d in range(NC - 1, 0, -1):
            @pl.when(c + d < NC)
            def _():
                f(c + d)

            @pl.when(c >= d)
            def _():
                f(c - d)
        f(c)

    def start_k(cc):
        kcopy(1 - yy, cc).start()
    order(start_k)

    def start_k2(cc):
        kcopy(yy, cc).start()
    order(start_k2)

    def do_y(cc):
        kcopy(1 - yy, cc).wait_recv()
        y_out[cc] = (mine((1 - yy) * 2 + kk, cc)[...].astype(F32) + k_buf[1 - yy, cc].astype(F32)).astype(BF)
        ycopy(cc).start()
    order(do_y)

    def partial(cc):
        kcopy(yy, cc).wait_recv()
        a = mine(r, cc)[...].astype(F32) + k_buf[yy, cc].astype(F32)
        ycopy(cc).wait_recv()
        return a + y_buf[cc].astype(F32)

    for d in range(NC - 1, 0, -1):
        @pl.when(c + d < NC)
        def _():
            cc = c + d
            a = partial(cc)
            zr_out[cc] = a.astype(BF)

            @pl.when(c > 0)
            def _():
                rcopy(cc).wait_recv()
                zr_out[cc] = (zr_out[cc].astype(F32) + r_buf[cc].astype(F32)).astype(BF)
            rcopy(cc).start()

        @pl.when(c >= d)
        def _():
            cc = c - d
            a = partial(cc)
            zl_out[cc] = a.astype(BF)

            @pl.when(c < NC - 1)
            def _():
                lcopy(cc).wait_recv()
                zl_out[cc] = (zl_out[cc].astype(F32) + l_buf[cc].astype(F32)).astype(BF)
            lcopy(cc).start()
    o_ref[...] = partial(c)

    @pl.when(c > 0)
    def _():
        rcopy(c).wait_recv()
        o_ref[...] += r_buf[c].astype(F32)

    @pl.when(c < NC - 1)
    def _():
        lcopy(c).wait_recv()
        o_ref[...] += l_buf[c].astype(F32)

    def fin(cc):
        kcopy(1 - yy, cc).wait_send()
        kcopy(yy, cc).wait_send()
        ycopy(cc).wait_send()
    order(fin)
    for d in range(NC - 1, 0, -1):
        @pl.when(c + d < NC)
        def _():
            rcopy(c + d).wait_send()

        @pl.when(c >= d)
        def _():
            lcopy(c - d).wait_send()


def reduce_scatter16(p, cid):
    T, D = p.shape
    S = T // 16
    buf = lambda n: pltpu.VMEM((n, S, D), BF)
    sem = lambda n: pltpu.SemaphoreType.DMA((n,))
    return pl.pallas_call(
        rs_kernel,
        out_shape=jax.ShapeDtypeStruct((S, D), F32),
        in_specs=[pl.BlockSpec(memory_space=pltpu.VMEM)],
        out_specs=pl.BlockSpec(memory_space=pltpu.VMEM),
        scratch_shapes=[pltpu.VMEM((2, NC, S, D), BF), buf(NC), buf(NC), buf(NC), buf(NC), buf(NC), buf(NC), buf(NC),
                        sem(8), sem(8), sem(4), sem(4), sem(4), sem(4), sem(4), sem(4)],
        compiler_params=pltpu.CompilerParams(collective_id=cid, has_side_effects=True, vmem_limit_bytes=56 << 20),
        cost_estimate=pl.CostEstimate(flops=0, bytes_accessed=64 << 20, transcendentals=0),
    )(p)


P = jax.sharding.PartitionSpec
HEAD_DIM = 64
STATE = 128
CONV = 4
SPAN = 256
AHEAD_DIM = 64
EPS = 1e-05
HIGH = lax.Precision.HIGHEST


def dot(a, b):
    return jnp.dot(a, b, preferred_element_type=F32)


def dot_t(a, b):
    return lax.dot_general(a, b, (((1,), (1,)), ((), ())), preferred_element_type=F32)


def t_dot(a, b):
    return lax.dot_general(a, b, (((0,), (0,)), ((), ())), preferred_element_type=F32)


def segments_of(places, seq_lens):
    first = (places >= seq_lens[0]).astype(jnp.int32)
    second = (places >= seq_lens[0] + seq_lens[1]).astype(jnp.int32)
    return jnp.where(places < 0, -1, first + second)


def cols_swap(pieces):
    c = lax.axis_index("cols")
    out = jnp.zeros_like(pieces)
    own = lax.dynamic_index_in_dim(pieces, c, 0, True)
    out = lax.dynamic_update_slice_in_dim(out, own, c, 0)
    for s in range(1, NC):
        away = lax.dynamic_index_in_dim(pieces, (c + s) % NC, 0, True)
        came = lax.ppermute(away, "cols", [(i, (i + s) % NC) for i in range(NC)])
        out = lax.dynamic_update_slice_in_dim(out, came, (c - s) % NC, 0)
    return out


def spread_in(w):
    d, n = w.shape
    return cols_swap(w.reshape(d, NC, n // NC).transpose(1, 0, 2)).reshape(d * NC, n // NC)


def spread_pair(w):
    d, n = w.shape
    halves = w.reshape(d, 2, n // 2).transpose(1, 0, 2)
    return cols_swap(jnp.repeat(halves, NC // 2, axis=0)).reshape(d * NC, n // 2)


def spread_out(w):
    n, d = w.shape
    return cols_swap(w.reshape(NC, n // NC, d)).transpose(1, 0, 2).reshape(n // NC, d * NC)


def spread_out_pair(w):
    n, d = w.shape
    halves = jnp.repeat(w.reshape(2, n // 2, d), NC // 2, axis=0)
    return cols_swap(halves).transpose(1, 0, 2).reshape(n // 2, d * NC)


def both_groups(x):
    if lax.axis_size("dp") == 2:
        return x.astype(F32) + lax.ppermute(x, "dp", [(0, 1), (1, 0)]).astype(F32)
    return lax.psum(x, "dp").astype(F32)


def back_in(g):
    d, n = g.shape
    got = both_groups(cols_swap(g.astype(BF).reshape(NC, d // NC, n)))
    return got.transpose(1, 0, 2).reshape(d // NC, NC * n)


def back_in_pair(g):
    d, n = g.shape
    got = both_groups(cols_swap(g.astype(BF).reshape(NC, d // NC, n)))
    got = got.reshape(2, NC // 2, d // NC, n).sum(1)
    return got.transpose(1, 0, 2).reshape(d // NC, 2 * n)


def back_out(g):
    n, d = g.shape
    got = both_groups(cols_swap(g.astype(BF).reshape(n, NC, d // NC).transpose(1, 0, 2)))
    return got.reshape(NC * n, d // NC)


def back_out_pair(g):
    n, d = g.shape
    got = both_groups(cols_swap(g.astype(BF).reshape(n, NC, d // NC).transpose(1, 0, 2)))
    got = got.reshape(2, NC // 2, n, d // NC).sum(1)
    return got.reshape(2 * n, d // NC)


def place_block(piece, start, full_len, axis):
    shape = piece.shape[:axis] + (full_len,) + piece.shape[axis + 1:]
    return lax.dynamic_update_slice_in_dim(jnp.zeros(shape, piece.dtype), piece, start, axis)


def rms_scale(x):
    return lax.rsqrt(jnp.mean(x * x, axis=1, keepdims=True) + EPS)


def norm_back(x, gain, scale, up):
    gain_grad = jnp.sum(x * scale * up, axis=0)
    tilted = up * gain[None, :]
    project = jnp.mean(x * tilted, axis=1, keepdims=True)
    return scale * tilted - x * (scale**3 * project), gain_grad


def depth_conv(masks, x, weight, bias):
    total = bias[None, :] + weight[CONV - 1][None, :] * x
    for s in range(1, CONV):
        shifted = jnp.concatenate([jnp.zeros((s, x.shape[1]), F32), x[:-s]], axis=0)
        total = total + weight[CONV - 1 - s][None, :] * shifted * masks[s - 1][:, None]
    return total


def mixer_pre(masks, x_pre, bc_pre, dt_raw, conv_w, conv_b, bc_w, bc_b, dt_bias, a_log):
    signal = jax.nn.silu(depth_conv(masks, x_pre, conv_w, conv_b))
    bc = jax.nn.silu(depth_conv(masks, bc_pre, bc_w, bc_b))
    step = jax.nn.softplus(dt_raw + dt_bias[None, :])
    rate = -jnp.exp(a_log)[None, :] * step
    return signal, bc[:, :STATE], bc[:, STATE:], step, rate


def ssd(seg, signal, bm, cm, step, rate):
    T, H = rate.shape
    nb = T // SPAN
    sb = seg.reshape(nb, SPAN)
    prior = jnp.concatenate([jnp.full((1,), -1, jnp.int32), sb[:-1, -1]])
    cum = jnp.cumsum(rate.reshape(nb, SPAN, H), axis=1).transpose(0, 2, 1)
    w = (signal.reshape(T, H, HEAD_DIM) * step[:, :, None]).reshape(nb, SPAN, H, HEAD_DIM).transpose(0, 2, 1, 3)
    b = bm.reshape(nb, SPAN, STATE)
    cc = cm.reshape(nb, SPAN, STATE)
    order = jnp.arange(SPAN, dtype=jnp.int32)
    allowed = (order[None, None, :] <= order[None, :, None]) & (sb[:, None, :] == sb[:, :, None])
    gaps = cum[:, :, :, None] - cum[:, :, None, :]
    decay = jnp.exp(jnp.where(allowed[:, None], gaps, -1e30))
    scores = jnp.einsum("bpn,bqn->bpq", cc, b, precision=HIGH)
    y = jnp.einsum("bhpq,bhqm->bhpm", scores[:, None] * decay, w, precision=HIGH)
    last = cum[:, :, -1]
    tail = jnp.exp(last[:, :, None] - cum) * (sb == sb[:, -1:]).astype(F32)[:, None, :]
    local = jnp.einsum("bhqm,bqn->bhmn", tail[..., None] * w, b, precision=HIGH)
    through = jnp.exp(last) * (sb[:, -1] == prior).astype(F32)[:, None]
    reach = jnp.exp(cum) * (sb == prior[:, None]).astype(F32)[:, None, :]
    state = jnp.zeros((H, HEAD_DIM, STATE), F32)
    states = []
    for i in range(nb):
        states.append(state)
        state = through[i][:, None, None] * state + local[i]
    states = jnp.stack(states)
    y = y + jnp.einsum("bpn,bhmn->bhpm", cc, states, precision=HIGH) * reach[..., None]
    return y.transpose(0, 2, 1, 3).reshape(T, H * HEAD_DIM)


def attend_head(allowed, piece):
    q, k, v = piece
    s = jnp.where(allowed, dot_t(q, k) * AHEAD_DIM ** (-0.5), -jnp.inf)
    top = jnp.max(s, axis=1, keepdims=True)
    e = jnp.exp(s - top)
    tot = jnp.sum(e, axis=1, keepdims=True)
    return dot((e / tot).astype(BF), v), (top + jnp.log(tot))[:, 0]


def attend_back(allowed, piece):
    q, k, v, do, lse = piece
    s = jnp.where(allowed, dot_t(q, k) * AHEAD_DIM ** (-0.5), -jnp.inf)
    p = jnp.exp(s - lse[:, None])
    dp = dot_t(do, v)
    ds = (p * (dp - jnp.sum(p * dp, axis=1, keepdims=True)) * AHEAD_DIM ** (-0.5)).astype(BF)
    return dot(ds, k), t_dot(ds, q), t_dot(p.astype(BF), do)


def heads_first(x):
    n, w = x.shape
    return x.reshape(n, w // AHEAD_DIM, AHEAD_DIM).transpose(1, 0, 2)


def heads_last(x):
    h, n, w = x.shape
    return x.transpose(1, 0, 2).reshape(n, h * w)


def per_device(hidden_in, lengths, norm1_gain, z_weight, x_weight, bcdt_weight, conv_x_weight, conv_x_bias,
               conv_bc_weight, conv_bc_bias, a_log, d_skip, dt_bias, gate_gain, mix_out_weight, norm2_gain,
               q_weight, k_weight, v_weight, att_out_weight, norm3_gain, up_weight, down_weight, grad_output):
    r, c = lax.axis_index("rows"), lax.axis_index("cols")
    rows = lax.axis_size("rows")
    tok_rows, feat = hidden_in.shape
    T, D = tok_rows * rows, feat * NC
    S = T // (rows * NC)
    slab = r * NC + c
    inner = z_weight.shape[1] * rows
    wide = z_weight.shape[1] // NC
    heads_row = a_log.shape[0]
    heads = heads_row // NC
    n_heads = heads_row * rows
    seq_lens = lengths[0]
    places = jnp.arange(T, dtype=jnp.int32)
    seg = segments_of(places, seq_lens)
    valid = (places < seq_lens[0] + seq_lens[1]).astype(F32)
    my_valid = lax.dynamic_slice_in_dim(valid, slab * S, S, 0)[:, None]
    pad = 128

    gains = lax.all_gather(jnp.stack([norm1_gain, norm2_gain, norm3_gain]), "cols", axis=1, tiled=True)
    hidden_all = gather_native(hidden_in, 0)
    w_z = spread_in(z_weight)
    w_x = spread_in(x_weight)
    w_bcdt = lax.all_gather(bcdt_weight, "cols", axis=0, tiled=True)
    w_in = jnp.concatenate([w_z, w_x, w_bcdt], axis=1)
    w_mix = spread_out(mix_out_weight)
    w_qkv = jnp.concatenate([spread_pair(q_weight), spread_pair(k_weight), spread_pair(v_weight)], axis=1)
    w_o = spread_out_pair(att_out_weight)
    w_up = spread_in(up_weight)
    w_down = spread_out(down_weight)
    grad_all = gather_native(grad_output, 0)

    hid_all = hidden_all.astype(F32)
    u1 = (hid_all * rms_scale(hid_all) * gains[0][None, :]).astype(BF)
    proj = dot(u1, w_in)
    z_pre, x_pre = proj[:, :wide], proj[:, wide:2 * wide]
    bc_pre = proj[:, 2 * wide:2 * wide + 2 * STATE]
    dt_raw = lax.dynamic_slice_in_dim(proj[:, 2 * wide + 2 * STATE:], slab * heads, heads, 1)
    masks = jnp.stack([(segments_of(places - s, seq_lens) == seg).astype(F32) for s in range(1, CONV)])
    mine = lambda a, n: lax.dynamic_slice_in_dim(a, c * n, n, a.ndim - 1)
    pre_out, pre_back = jax.vjp(
        functools.partial(mixer_pre, masks), x_pre, bc_pre, dt_raw, mine(conv_x_weight, wide), mine(conv_x_bias, wide),
        conv_bc_weight, conv_bc_bias, mine(dt_bias, heads), mine(a_log, heads))
    signal = pre_out[0]
    y_ssd, ssd_back = jax.vjp(functools.partial(ssd, seg), *pre_out)
    skip = jnp.repeat(mine(d_skip, heads), HEAD_DIM)[None, :]
    y = y_ssd + skip * signal
    silu_z, silu_back = jax.vjp(jax.nn.silu, z_pre)
    gated = y * silu_z
    my_gate_gain = mine(gate_gain, wide)[None, :]
    mixg = (gated * my_gate_gain).astype(BF)
    squares = jnp.sum(gated * gated, axis=1, keepdims=True)
    part = jnp.concatenate([dot(mixg, w_mix), jnp.broadcast_to(squares, (T, pad))], axis=1).astype(BF)
    summed = reduce_scatter16(part, 2)
    gate_scale = lax.rsqrt(summed[:, D:D + 1] / inner + EPS)
    mix_out = summed[:, :D] * gate_scale
    h0 = lax.dynamic_slice_in_dim(hidden_all, slab * S, S, 0).astype(F32)
    h1 = h0 + mix_out
    s2 = rms_scale(h1)
    u2 = all_gather16((h1 * s2 * gains[1][None, :]).astype(BF), 1)

    qkv = dot(u2, w_qkv).astype(BF)
    att = w_o.shape[0]
    odd = c % 2
    blk = T // 4
    b0, b1 = jnp.where(odd == 1, 1, 0), jnp.where(odd == 1, 2, 3)

    def pick(x):
        return jnp.concatenate([lax.dynamic_slice_in_dim(x, b0 * blk, blk, 0), lax.dynamic_slice_in_dim(x, b1 * blk, blk, 0)], axis=0)

    def unpick(x):
        out = jnp.zeros((T,) + x.shape[1:], x.dtype)
        out = lax.dynamic_update_slice_in_dim(out, x[:blk], b0 * blk, 0)
        return lax.dynamic_update_slice_in_dim(out, x[blk:], b1 * blk, 0)

    q_h = heads_first(pick(qkv[:, :att]))
    k_h, v_h = heads_first(qkv[:, att:2 * att]), heads_first(qkv[:, 2 * att:])
    q_places, q_seg = pick(places), pick(seg)
    allowed = (places[None, :] <= q_places[:, None]) & (seg[None, :] == q_seg[:, None])
    att_h, lse = lax.map(functools.partial(attend_head, allowed), (q_h, k_h, v_h))
    attended = heads_last(att_h).astype(BF)
    h2 = h1 + reduce_scatter16(unpick(dot(attended, w_o).astype(BF)), 3)
    s3 = rms_scale(h2)
    u3 = all_gather16((h2 * s3 * gains[2][None, :]).astype(BF), 1)

    act, = (dot(u3, w_up),)
    gelu, gelu_back = jax.vjp(functools.partial(jax.nn.gelu, approximate=True), act)
    hid = gelu.astype(BF)
    h3 = h2 + reduce_scatter16(dot(hid, w_down).astype(BF), 3)
    out_slab = (h3 * my_valid).astype(BF)
    output = cols_swap(out_slab.reshape(S, NC, feat).transpose(1, 0, 2)).reshape(NC * S, feat)

    g3 = (grad_all.astype(F32) * valid[:, None]).astype(BF)
    g3_mine = lax.dynamic_slice_in_dim(g3, slab * S, S, 0).astype(F32)
    d_act = gelu_back(dot_t(g3, w_down))[0].astype(BF)
    down_grad = back_out(t_dot(hid, g3))
    up_grad = back_in(t_dot(u3, d_act))
    d_u3 = reduce_scatter16(dot_t(d_act, w_up).astype(BF), 3)
    d_n3, gain3_grad = norm_back(h2, gains[2], s3, d_u3)
    dh2 = g3_mine + d_n3
    g2 = all_gather16(dh2.astype(BF), 1)
    g2_sel = pick(g2)
    d_att = heads_first(dot_t(g2_sel, w_o).astype(BF))
    o_grad = back_out_pair(t_dot(attended, g2_sel))
    dq, dk, dv = lax.map(functools.partial(attend_back, allowed), (q_h, k_h, v_h, d_att, lse))
    d_qkv = jnp.concatenate([unpick(heads_last(dq)), heads_last(dk), heads_last(dv)], axis=1).astype(BF)
    qkv_grad = t_dot(u2, d_qkv)
    q_grad, k_grad, v_grad = (back_in_pair(qkv_grad[:, i * att:(i + 1) * att]) for i in range(3))
    d_u2 = reduce_scatter16(dot_t(d_qkv, w_qkv).astype(BF), 3)
    d_n2, gain2_grad = norm_back(h1, gains[1], s2, d_u2)
    dh1 = dh2 + d_n2
    tilt = gate_scale * gate_scale * jnp.sum(dh1 * mix_out, axis=1, keepdims=True) / inner
    tilt_hi = tilt.astype(BF)
    tilt_lo = (tilt - tilt_hi.astype(F32)).astype(BF)
    tail = jnp.concatenate([jnp.broadcast_to(tilt_hi, (S, pad // 2)), jnp.broadcast_to(tilt_lo, (S, pad // 2))], axis=1)
    g1_ext = all_gather16(jnp.concatenate([(dh1 * gate_scale).astype(BF), tail], axis=1), 4)
    g1 = g1_ext[:, :D]
    tilt_all = g1_ext[:, D:D + 1].astype(F32) + g1_ext[:, D + pad // 2:D + pad // 2 + 1].astype(F32)
    d_mix = dot_t(g1, w_mix)
    mix_grad = back_out(t_dot(mixg, g1))
    gate_gain_grad = jnp.sum(gated * d_mix, axis=0)
    d_gated = d_mix * my_gate_gain - gated * tilt_all
    d_z = silu_back(d_gated * y)[0]
    d_y = d_gated * silu_z
    d_skip_grad = jnp.sum((d_y * signal).reshape(T, heads, HEAD_DIM), axis=(0, 2))
    d_signal, d_b, d_c, d_step, d_rate = ssd_back(d_y)
    pre_grads = pre_back((d_signal + d_y * skip, d_b, d_c, d_step, d_rate))
    d_x, d_bc, d_dt, cxw_grad, cxb_grad, cbw_grad, cbb_grad, dt_bias_grad, a_log_grad = pre_grads
    d_bcdt = jnp.concatenate([d_bc, place_block(d_dt, slab * heads, n_heads, 1)], axis=1)
    d_in = jnp.concatenate([d_z, d_x, d_bcdt], axis=1).astype(BF)
    in_grad = t_dot(u1, d_in)
    z_grad, x_grad = back_in(in_grad[:, :wide]), back_in(in_grad[:, wide:2 * wide])
    d_u1 = reduce_scatter16(dot_t(d_in, w_in).astype(BF), 3)
    d_n1, gain1_grad = norm_back(h0, gains[0], rms_scale(h0), d_u1)
    in_slab = dh1 + d_n1
    input_grad = cols_swap(in_slab.reshape(S, NC, feat).transpose(1, 0, 2)).reshape(NC * S, feat)

    small = lax.psum((
        gain1_grad, in_grad[:, 2 * wide:], place_block(cxw_grad, slab * wide, inner, 1), place_block(cxb_grad, slab * wide, inner, 0),
        cbw_grad, cbb_grad, place_block(a_log_grad, slab * heads, n_heads, 0), place_block(d_skip_grad, slab * heads, n_heads, 0),
        place_block(dt_bias_grad, slab * heads, n_heads, 0), place_block(gate_gain_grad, slab * wide, inner, 0),
        gain2_grad, gain3_grad), ("dp", "rows", "cols"))
    return (output, input_grad, small[0], z_grad, x_grad, small[1], small[2], small[3], small[4], small[5], small[6], small[7],
            small[8], small[9], mix_grad, small[10], q_grad, k_grad, v_grad, o_grad, small[11], up_grad, down_grad)


def solution(mesh):
    assert mesh.shape["rows"] == 4 and mesh.shape["cols"] == NC
    token = P(("dp", "rows"), "cols")
    w_in, w_out = P("cols", "rows"), P("rows", "cols")
    row, col, whole = P("rows"), P("cols"), P()
    placed = (token, P("dp", None), col, w_in, w_in, P("cols", None), P(None, "rows"), row, whole, whole, row, row, row, row,
              w_out, col, w_in, w_in, w_in, w_out, col, w_in, w_out, token)
    given = (token, token, whole, w_in, w_in, whole, whole, whole, whole, whole, whole, whole, whole, whole, w_out, whole,
             w_in, w_in, w_in, w_out, whole, w_in, w_out)
    return jax.shard_map(per_device, mesh=mesh, in_specs=placed, out_specs=given, check_vma=False)
```

```python
import functools
import jax, jax.numpy as jnp
from jax import lax
from jax.experimental import pallas as pl
from jax.experimental.pallas import tpu as pltpu
MESH = pl.DeviceIdType.MESH
NC = 4
F32, BF = jnp.float32, jnp.bfloat16


def copy_to(src, dst, send, recv, dev):
    return pltpu.make_async_remote_copy(src_ref=src, dst_ref=dst, send_sem=send, recv_sem=recv, device_id=dev, device_id_type=MESH)


def greet(r, c, kinds=()):
    barrier = pltpu.get_barrier_semaphore()
    all_cols = any(kind != "dp" for kind in kinds)
    pl.semaphore_signal(barrier, inc=1, device_id={"rows": r ^ 1}, device_id_type=MESH)
    pl.semaphore_signal(barrier, inc=1, device_id={"rows": r ^ 2}, device_id_type=MESH)
    count = 2
    if all_cols:
        for s in range(1, NC):
            pl.semaphore_signal(barrier, inc=1, device_id={"cols": lax.rem(c + s, NC)}, device_id_type=MESH)
        count += NC - 1
    else:
        @pl.when(c > 0)
        def _():
            pl.semaphore_signal(barrier, inc=1, device_id={"cols": c - 1}, device_id_type=MESH)

        @pl.when(c < NC - 1)
        def _():
            pl.semaphore_signal(barrier, inc=1, device_id={"cols": c + 1}, device_id_type=MESH)
        count = count + jnp.where(c > 0, 1, 0) + jnp.where(c < NC - 1, 1, 0)
    if "dp" in kinds or "swap2" in kinds:
        groups = lax.axis_size("dp")
        for s in range(1, groups):
            pl.semaphore_signal(barrier, inc=1, device_id={"dp": lax.rem(lax.axis_index("dp") + s, groups)}, device_id_type=MESH)
        count = count + groups - 1
    pl.semaphore_wait(barrier, count)


def riders(kinds, ins, outs, send, recv, loc):
    r, c, g = lax.axis_index("rows"), lax.axis_index("cols"), lax.axis_index("dp")
    groups = lax.axis_size("dp")
    remote, local, late = [], [], []
    for e, kind in enumerate(kinds):
        src, dst = ins[e], outs[e]
        if kind == "dp":
            for s in range(1, groups):
                remote.append(copy_to(src, dst.at[s - 1], send.at[e, s - 1], recv.at[e, s - 1], {"dp": lax.rem(g + s, groups)}))
        elif kind == "swap":
            for s in range(1, NC):
                to = lax.rem(c + s, NC)
                remote.append(copy_to(src.at[to], dst.at[c], send.at[e, s - 1], recv.at[e, s - 1], {"cols": to}))
            local.append(pltpu.make_async_copy(src.at[c], dst.at[c], loc.at[e]))
        else:
            half = g if kind == "swap2" else r & 1
            other = {"dp": 1 - g} if kind == "swap2" else {"rows": r ^ 1}
            for s in range(1, NC):
                to, came = lax.rem(c + s, NC), lax.rem(c + NC - s, NC)
                first = copy_to(src.at[to, half] if kind == "swap2" else src.at[half], dst.at[c, half],
                                send.at[e, s - 1], recv.at[e, s - 1], {"cols": to})
                late.append((first, copy_to(dst.at[came, half], dst.at[came, half], send.at[e, NC + s - 1], recv.at[e, NC + s - 1], other)))
            if kind == "swap2":
                local.append(pltpu.make_async_copy(src.at[c], dst.at[c], loc.at[e]))
            else:
                local.append(pltpu.make_async_copy(src, dst.at[c], loc.at[e]))

    def start():
        for first, _ in late:
            first.start()
        for one in remote + local:
            one.start()

    def finish():
        for first, second in late:
            first.wait_recv()
            second.start()
        for one in remote + local:
            one.wait()
        for first, second in late:
            first.wait_send()
            second.wait()
    return start, finish


def rider_parts(kinds, arrays):
    groups = lax.axis_size("dp")
    shapes = []
    for kind, a in zip(kinds, arrays):
        lead = {"swap": (), "swap2": (), "bcast2": (NC,), "dp": (groups - 1,)}[kind]
        shapes.append(jax.ShapeDtypeStruct(lead + a.shape, a.dtype))
    n, most = len(kinds), max(2 * NC, groups)
    sems = [pltpu.SemaphoreType.DMA((n, most)), pltpu.SemaphoreType.DMA((n, most)), pltpu.SemaphoreType.DMA((n,))] if n else []
    return shapes, sems


SMALL = 96


def sum_groups(x_ref, others, held, dp_s, dp_r, n):
    g, groups = lax.axis_index("dp"), lax.axis_size("dp")
    copies = [copy_to(x_ref, others.at[s - 1], dp_s.at[s - 1], dp_r.at[s - 1], {"dp": lax.rem(g + s, groups)}) for s in range(1, groups)]
    for one in copies:
        one.start()
    total = x_ref[...]
    for s, one in enumerate(copies):
        one.wait()
        total = total + others[s]
    part = (lax.broadcasted_iota(jnp.int32, total.shape, 0) - SMALL) // n
    rest = total - total.astype(BF).astype(F32)
    rest2 = rest - rest.astype(BF).astype(F32)
    second, third = (part == 1) | (part == 4), (part == 2) | (part == 5)
    held[...] = jnp.where(second, rest, jnp.where(third, rest2, total)).astype(BF)
    return held


def ag_kernel(native, total, at, kinds, *refs):
    n = len(kinds)
    x_ref, ins, out_ref, outs = refs[0], refs[1:1 + n], refs[1 + n], refs[2 + n:2 + 2 * n]
    recv, zr_s, zl_s, y_s, k_s, loc, *sems = refs[2 + 2 * n:]
    r, c = lax.axis_index("rows"), lax.axis_index("cols")
    S, W = x_ref.shape
    greet(r, c, kinds)
    if total:
        others, held, dp_s, dp_r, *sems = sems
    ride, alight = riders(kinds, ins, outs, *sems) if n else (lambda: None, lambda: None)
    if total:
        x_ref = sum_groups(x_ref, others, held, dp_s, dp_r, total)

    def slab(rr, cc):
        if native:
            return out_ref.at[pl.ds(pl.multiple_of(rr * S, 16), S), pl.ds(pl.multiple_of(cc * W, 128), W)]
        return out_ref.at[pl.ds(pl.multiple_of((rr * NC + cc) * S, 16), S)]

    def right(cc, src):
        return copy_to(src, slab(r, cc), zr_s.at[cc], recv.at[r * NC + cc], {"cols": c + 1})

    def left(cc, src):
        return copy_to(src, slab(r, cc), zl_s.at[cc], recv.at[r * NC + cc], {"cols": c - 1})

    def ycopy(cc, src):
        return copy_to(src, slab(r, cc), y_s.at[cc], recv.at[r * NC + cc], {"rows": r ^ 2})

    def kcopy(rr, cc, src):
        return copy_to(src, slab(rr, cc), k_s.at[(rr >> 1) * NC + cc], recv.at[rr * NC + cc], {"rows": r ^ 1})

    def got(rr, cc):
        copy_to(slab(rr, cc), slab(rr, cc), k_s.at[0], recv.at[rr * NC + cc], {"rows": r ^ 1}).wait_recv()

    @pl.when(c < NC - 1)
    def _():
        right(c, x_ref).start()

    @pl.when(c > 0)
    def _():
        left(c, x_ref).start()
    ycopy(c, x_ref).start()
    kcopy(r, c, x_ref).start()
    own = pltpu.make_async_copy(x_ref, slab(r, c), loc)
    own.start()
    if at == 0:
        ride()

    def from_y(cc):
        got(r ^ 2, cc)
        kcopy(r ^ 2, cc, slab(r ^ 2, cc)).start()

    for d in range(1, NC):
        @pl.when(c >= d)
        def _():
            cc = c - d
            got(r, cc)

            @pl.when(c < NC - 1)
            def _():
                right(cc, slab(r, cc)).start()
            ycopy(cc, slab(r, cc)).start()
            kcopy(r, cc, slab(r, cc)).start()

        @pl.when(c + d < NC)
        def _():
            cc = c + d
            got(r, cc)

            @pl.when(c > 0)
            def _():
                left(cc, slab(r, cc)).start()
            ycopy(cc, slab(r, cc)).start()
            kcopy(r, cc, slab(r, cc)).start()
        if d == at:
            ride()
        if d == 1:
            from_y(c)
        else:
            @pl.when(c >= d - 1)
            def _():
                from_y(c - (d - 1))

            @pl.when(c + d - 1 < NC)
            def _():
                from_y(c + d - 1)
    d = NC

    @pl.when(c >= d - 1)
    def _():
        from_y(c - (d - 1))

    @pl.when(c + d - 1 < NC)
    def _():
        from_y(c + d - 1)
    for cc in range(NC):
        got(r ^ 1, cc)
        got(r ^ 3, cc)
    own.wait()
    for cc in range(NC):
        y_c = ycopy(cc, slab(r, cc))
        y_c.wait_send()
        kcopy(r, cc, slab(r, cc)).wait_send()
        kcopy(r ^ 2, cc, slab(r ^ 2, cc)).wait_send()

        @pl.when((cc <= c) & (c < NC - 1))
        def _():
            right(cc, slab(r, cc)).wait_send()

        @pl.when((cc >= c) & (c > 0))
        def _():
            left(cc, slab(r, cc)).wait_send()
    alight()


def gather16(x, cid, native, kinds, arrays, total=0, at=0):
    S, D = x.shape
    shapes, sems = rider_parts(kinds, arrays)
    if total:
        groups = lax.axis_size("dp")
        sems = [pltpu.VMEM((groups - 1, S, D), F32), pltpu.VMEM((S, D), BF), pltpu.SemaphoreType.DMA((groups - 1,)),
                pltpu.SemaphoreType.DMA((groups - 1,))] + sems
    any_space = pl.BlockSpec(memory_space=pl.ANY)
    return pl.pallas_call(
        functools.partial(ag_kernel, native, total, at, tuple(kinds)),
        out_shape=[jax.ShapeDtypeStruct((4 * S, NC * D) if native else (16 * S, D), BF)] + shapes,
        in_specs=[pl.BlockSpec(memory_space=pltpu.VMEM)] + [any_space] * len(kinds),
        out_specs=[pl.BlockSpec(memory_space=pltpu.VMEM)] + [any_space] * len(kinds),
        scratch_shapes=[pltpu.SemaphoreType.DMA((16,)), pltpu.SemaphoreType.DMA((NC,)), pltpu.SemaphoreType.DMA((NC,)),
                        pltpu.SemaphoreType.DMA((NC,)), pltpu.SemaphoreType.DMA((2 * NC,)), pltpu.SemaphoreType.DMA] + sems,
        compiler_params=pltpu.CompilerParams(collective_id=cid, has_side_effects=True, vmem_limit_bytes=48 << 20),
        cost_estimate=pl.CostEstimate(flops=0, bytes_accessed=64 << 20, transcendentals=0),
    )(x, *arrays)


def all_gather16(x, cid, kinds=(), arrays=()):
    return gather16(x, cid, False, kinds, arrays, 0, 3)


def gather_native(x, cid, kinds=(), arrays=()):
    return gather16(x, cid, True, kinds, arrays)


def rs_kernel(kinds, *refs):
    n = len(kinds)
    p_ref, ins, o_ref, outs = refs[0], refs[1:1 + n], refs[1 + n], refs[2 + n:2 + 2 * n]
    (k_buf, y_buf, l_buf, r_buf, y_out, zr_out, zl_out,
     k_s, k_r, y_s, y_r, zr_s, zr_r, zl_s, zl_r, *sems) = refs[2 + 2 * n:]
    r, c = lax.axis_index("rows"), lax.axis_index("cols")
    S, D = o_ref.shape
    yy, kk = r >> 1, r & 1
    greet(r, c, kinds)
    ride, alight = riders(kinds, ins, outs, *sems) if n else (lambda: None, lambda: None)

    def mine(rr, cc):
        return p_ref.at[pl.ds(pl.multiple_of((rr * NC + cc) * S, 16), S)]

    def kcopy(y2, cc):
        return copy_to(mine(y2 * 2 + (1 - kk), cc), k_buf.at[y2, cc], k_s.at[y2 * NC + cc], k_r.at[y2 * NC + cc], {"rows": r ^ 1})

    def ycopy(cc):
        return copy_to(y_out.at[cc], y_buf.at[cc], y_s.at[cc], y_r.at[cc], {"rows": r ^ 2})

    def rcopy(cc):
        return copy_to(zr_out.at[cc], r_buf.at[cc], zr_s.at[cc], zr_r.at[cc], {"cols": c + 1})

    def lcopy(cc):
        return copy_to(zl_out.at[cc], l_buf.at[cc], zl_s.at[cc], zl_r.at[cc], {"cols": c - 1})

    def order(f):
        for d in range(NC - 1, 0, -1):
            @pl.when(c + d < NC)
            def _():
                f(c + d)

            @pl.when(c >= d)
            def _():
                f(c - d)
        f(c)

    def start_k(cc):
        kcopy(1 - yy, cc).start()
    order(start_k)

    def start_k2(cc):
        kcopy(yy, cc).start()
    order(start_k2)
    ride()

    def do_y(cc):
        kcopy(1 - yy, cc).wait_recv()
        y_out[cc] = (mine((1 - yy) * 2 + kk, cc)[...].astype(F32) + k_buf[1 - yy, cc].astype(F32)).astype(BF)
        ycopy(cc).start()
    order(do_y)

    def partial(cc):
        kcopy(yy, cc).wait_recv()
        a = mine(r, cc)[...].astype(F32) + k_buf[yy, cc].astype(F32)
        ycopy(cc).wait_recv()
        return a + y_buf[cc].astype(F32)

    for d in range(NC - 1, 0, -1):
        @pl.when(c + d < NC)
        def _():
            cc = c + d
            a = partial(cc)
            zr_out[cc] = a.astype(BF)

            @pl.when(c > 0)
            def _():
                rcopy(cc).wait_recv()
                zr_out[cc] = (zr_out[cc].astype(F32) + r_buf[cc].astype(F32)).astype(BF)
            rcopy(cc).start()

        @pl.when(c >= d)
        def _():
            cc = c - d
            a = partial(cc)
            zl_out[cc] = a.astype(BF)

            @pl.when(c < NC - 1)
            def _():
                lcopy(cc).wait_recv()
                zl_out[cc] = (zl_out[cc].astype(F32) + l_buf[cc].astype(F32)).astype(BF)
            lcopy(cc).start()
    o_ref[...] = partial(c)

    @pl.when(c > 0)
    def _():
        rcopy(c).wait_recv()
        o_ref[...] += r_buf[c].astype(F32)

    @pl.when(c < NC - 1)
    def _():
        lcopy(c).wait_recv()
        o_ref[...] += l_buf[c].astype(F32)

    def fin(cc):
        kcopy(1 - yy, cc).wait_send()
        kcopy(yy, cc).wait_send()
        ycopy(cc).wait_send()
    order(fin)
    for d in range(NC - 1, 0, -1):
        @pl.when(c + d < NC)
        def _():
            rcopy(c + d).wait_send()

        @pl.when(c >= d)
        def _():
            lcopy(c - d).wait_send()
    alight()


def reduce_scatter16(p, cid, kinds=(), arrays=()):
    T, D = p.shape
    S = T // 16
    buf = lambda n: pltpu.VMEM((n, S, D), BF)
    sem = lambda n: pltpu.SemaphoreType.DMA((n,))
    shapes, sems = rider_parts(kinds, arrays)
    any_space = pl.BlockSpec(memory_space=pl.ANY)
    return pl.pallas_call(
        functools.partial(rs_kernel, tuple(kinds)),
        out_shape=[jax.ShapeDtypeStruct((S, D), F32)] + shapes,
        in_specs=[pl.BlockSpec(memory_space=pltpu.VMEM)] + [any_space] * len(kinds),
        out_specs=[pl.BlockSpec(memory_space=pltpu.VMEM)] + [any_space] * len(kinds),
        scratch_shapes=[pltpu.VMEM((2, NC, S, D), BF), buf(NC), buf(NC), buf(NC), buf(NC), buf(NC), buf(NC),
                        sem(8), sem(8), sem(4), sem(4), sem(4), sem(4), sem(4), sem(4)] + sems,
        compiler_params=pltpu.CompilerParams(collective_id=cid, has_side_effects=True, vmem_limit_bytes=56 << 20),
        cost_estimate=pl.CostEstimate(flops=0, bytes_accessed=64 << 20, transcendentals=0),
    )(p, *arrays)


HEAD_DIM = 64
STATE = 128
CONV = 4
SPAN = 256
HIGH = lax.Precision.HIGHEST
WIDE = 192
MIX = 2 * STATE + WIDE


def mm(a, b, ca=1, cb=0):
    return lax.dot_general(a.astype(BF), b.astype(BF), (((ca,), (cb,)), ((), ())), preferred_element_type=F32)


def exact(a, b, ca=1, cb=0):
    return lax.dot_general(a, b, (((ca,), (cb,)), ((), ())), preferred_element_type=F32, precision=HIGH)


def seg_at(place, l0, l1):
    return jnp.where(place < 0, -1, jnp.where(place >= l0, 1, 0) + jnp.where(place >= l0 + l1, 1, 0))


def sigmoid(x):
    return 1.0 / (1.0 + jnp.exp(-x))


def by_head(a, lane):
    return jnp.where(lane < HEAD_DIM, a[:, 0:1], jnp.where(lane < 2 * HEAD_DIM, a[:, 1:2], a[:, 2:3]))


def head_sums(a):
    i = lax.broadcasted_iota(jnp.int32, (WIDE, 128), 0)
    j = lax.broadcasted_iota(jnp.int32, (WIDE, 128), 1)
    return exact(a, jnp.where(i // HEAD_DIM == j, 1.0, 0.0).astype(F32))


class Block:
    def __init__(self, blk, lens, proj, before, cw, pv):
        self.l0, self.l1 = lens[0], lens[1]
        self.start = blk * SPAN
        v = proj[:, :MIX]
        self.place = self.start + lax.broadcasted_iota(jnp.int32, (SPAN, 1), 0)
        self.seg = seg_at(self.place, self.l0, self.l1)
        ext = jnp.concatenate([before[:, :MIX], v], axis=0)
        acc = cw[4:5] + cw[3:4] * v
        self.shifted = [v]
        for s in range(1, CONV):
            keep = jnp.where(seg_at(self.place - s, self.l0, self.l1) == self.seg, 1.0, 0.0)
            moved = ext[8 - s:8 - s + SPAN] * keep
            self.shifted.append(moved)
            acc = acc + cw[3 - s:4 - s] * moved
        self.acc = acc
        self.gate = sigmoid(acc)
        act = acc * self.gate
        self.b, self.c, self.x = act[:, :STATE], act[:, STATE:2 * STATE], act[:, 2 * STATE:]
        self.z = proj[:, MIX:MIX + WIDE]
        self.zs = sigmoid(self.z)
        self.raw = proj[:, MIX + WIDE:] + pv[2:3, :128]
        self.dt = jnp.maximum(self.raw, 0.0) + jnp.log1p(jnp.exp(-jnp.abs(self.raw)))
        self.rate = pv[3:4, :128] * self.dt
        i = lax.broadcasted_iota(jnp.int32, (SPAN, SPAN), 0)
        j = lax.broadcasted_iota(jnp.int32, (SPAN, SPAN), 1)
        self.low = jnp.where(j <= i, 1.0, 0.0).astype(F32)
        self.cum = exact(self.low, self.rate)
        self.cum_t = self.cum.T
        seg_row = seg_at(self.start + lax.broadcasted_iota(jnp.int32, (1, SPAN), 1), self.l0, self.l1)
        self.allowed = (j <= i) & (seg_row == self.seg)
        self.scores = mm(self.c, self.b, 1, 1)
        self.lane = lax.broadcasted_iota(jnp.int32, (SPAN, WIDE), 1)
        self.w = self.x * by_head(self.dt, self.lane)
        prior = seg_at(self.start - 1, self.l0, self.l1)
        last = seg_at(self.start + SPAN - 1, self.l0, self.l1)
        end = self.cum[SPAN - 1:SPAN]
        self.e = by_head(jnp.exp(self.cum), self.lane) * jnp.where(self.seg == prior, 1.0, 0.0)
        self.tail = by_head(jnp.exp(end - self.cum), self.lane) * jnp.where(self.seg == last, 1.0, 0.0)
        self.through = jnp.exp(end) * jnp.where(last == prior, 1.0, 0.0)
        row = lax.broadcasted_iota(jnp.int32, (WIDE, 1), 0)
        self.through_rows = jnp.where(row < HEAD_DIM, self.through[:, 0:1],
                                      jnp.where(row < 2 * HEAD_DIM, self.through[:, 1:2], self.through[:, 2:3]))

    def decay(self, h):
        return jnp.exp(jnp.where(self.allowed, self.cum[:, h:h + 1] - self.cum_t[h:h + 1, :], -1e30))

    def of_head(self, a, h):
        return jnp.where(self.lane // HEAD_DIM == h, a, 0.0)


def mixer_fwd_kernel(lens, proj, before, cw, pv, mixg, squares, y_out, states, state):
    blk = pl.program_id(0)

    @pl.when(blk == 0)
    def _():
        state[...] = jnp.zeros_like(state)
    k = Block(blk, lens, proj[...], before[...], cw[...], pv[...])
    s_in = state[...]
    states[0] = s_in
    y = mm(k.c, s_in, 1, 1) * k.e
    for h in range(3):
        y = y + mm(k.scores * k.decay(h), k.of_head(k.w, h))
    y = y + pv[1:2, :WIDE] * k.x
    state[...] = k.through_rows * s_in + mm(k.tail * k.w, k.b, 0, 0)
    y_out[...] = y
    gated = y * k.z * k.zs
    mixg[...] = (gated * pv[0:1, :WIDE]).astype(BF)
    squares[...] = jnp.broadcast_to(jnp.sum(gated * gated, axis=1, keepdims=True), squares.shape).astype(BF)


def mixer_bwd_kernel(lens, proj, before, cw, pv, y_ref, states, d_mix, extra, d_in, taps, rows, d_state, later):
    step = pl.program_id(0)
    blk = pl.num_programs(0) - 1 - step

    @pl.when(step == 0)
    def _():
        d_state[...] = jnp.zeros_like(d_state)
        later[...] = jnp.zeros_like(later)
        taps[...] = jnp.zeros_like(taps)
        rows[...] = jnp.zeros_like(rows)
    k = Block(blk, lens, proj[...], before[...], cw[...], pv[...])
    y, dm, s_in, ds = y_ref[...], d_mix[...], states[0], d_state[...]
    tilt = extra[:, 0:1].astype(F32) + extra[:, 64:65].astype(F32)
    silu_z = k.z * k.zs
    gated = y * silu_z
    d_gated = dm * pv[0:1, :WIDE] - gated * tilt
    d_z = d_gated * y * (k.zs * (1.0 + k.z * (1.0 - k.zs)))
    dy = d_gated * silu_z
    zeros = jnp.zeros((SPAN, 128), F32)
    lane = lax.broadcasted_iota(jnp.int32, (SPAN, 128), 1)
    top = lax.broadcasted_iota(jnp.int32, (128, SPAN), 0)
    d_cum, cols = zeros, jnp.zeros((128, SPAN), F32)
    d_scores = jnp.zeros((SPAN, SPAN), F32)
    dw = jnp.zeros((SPAN, WIDE), F32)
    for h in range(3):
        decay = k.decay(h)
        mixing = k.scores * decay
        dyh = k.of_head(dy, h).astype(BF)
        d_mixing = mm(dyh, k.w, 1, 1)
        d_scores = d_scores + d_mixing * decay
        moved = d_mixing * mixing
        d_cum = jnp.where(lane == h, jnp.sum(moved, axis=1, keepdims=True), d_cum)
        cols = jnp.where(top == h, jnp.sum(moved, axis=0, keepdims=True), cols)
        dw = dw + mm(mixing, dyh, 0, 0)
    e_dy, tail_w = k.e * dy, k.tail * k.w
    back = mm(k.b, ds, 1, 1)
    dw = dw + k.tail * back
    d_c = mm(d_scores, k.b) + mm(e_dy, s_in)
    d_b = mm(d_scores, k.c, 0, 0) + mm(tail_w, ds)
    through_state = mm(k.c, s_in, 1, 1) * k.e
    left = head_sums(tail_w * back)
    d_cum = d_cum - cols.T + head_sums(dy * through_state) - left
    own = jnp.sum(ds * s_in, axis=1, keepdims=True)
    of_row = lax.broadcasted_iota(jnp.int32, (WIDE, 128), 0) // HEAD_DIM
    own = jnp.sum(jnp.where(of_row == lax.broadcasted_iota(jnp.int32, (WIDE, 128), 1), own, 0.0), axis=0, keepdims=True)
    at_end = jnp.sum(left, axis=0, keepdims=True) + k.through * own
    is_last = lax.broadcasted_iota(jnp.int32, (SPAN, 128), 0) == SPAN - 1
    d_cum = d_cum + jnp.where(is_last, at_end, 0.0)
    d_rate = exact(k.low, d_cum, 0, 0)
    d_dt = head_sums(dw * k.x) + d_rate * pv[3:4, :128]
    d_raw = jnp.where(lane < 3, d_dt * sigmoid(k.raw), 0.0)
    d_x = dw * by_head(k.dt, k.lane) + pv[1:2, :WIDE] * dy
    d_pre = jnp.concatenate([d_b, d_c, d_x], axis=1) * (k.gate * (1.0 + k.acc * (1.0 - k.gate)))
    wide_rows = [jnp.sum(gated * dm, axis=0, keepdims=True), jnp.sum(dy * k.x, axis=0, keepdims=True)]
    thin_rows = [jnp.sum(d_raw, axis=0, keepdims=True), jnp.sum(d_rate * k.rate, axis=0, keepdims=True)]
    for i, one in enumerate(wide_rows):
        rows[i:i + 1, :WIDE] += one
    for i, one in enumerate(thin_rows):
        rows[2 + i:3 + i, :128] += one
    for s in range(CONV):
        taps[3 - s:4 - s] += jnp.sum(d_pre * k.shifted[s], axis=0, keepdims=True)
    taps[4:5] += jnp.sum(d_pre, axis=0, keepdims=True)
    ext = jnp.concatenate([d_pre, later[...]], axis=0)
    place = k.start + lax.broadcasted_iota(jnp.int32, (SPAN + 8, 1), 0)
    seg = seg_at(place, k.l0, k.l1)
    d_v = cw[3:4] * d_pre
    for s in range(1, CONV):
        keep = jnp.where(seg_at(place - s, k.l0, k.l1) == seg, 1.0, 0.0)
        d_v = d_v + cw[3 - s:4 - s] * (ext * keep)[s:s + SPAN]
    later[...] = d_pre[:8]
    d_in[...] = jnp.concatenate([d_v, d_z, d_raw], axis=1).astype(BF)
    d_state[...] = k.through_rows * ds + mm(e_dy, k.c, 0, 0)


def mixer_specs(n, order):
    block = lambda width: pl.BlockSpec((SPAN, width), lambda i: (order(i), 0))
    whole = lambda shape: pl.BlockSpec(shape, lambda i: (0, 0))
    before = pl.BlockSpec((8, MIX + WIDE + 128), lambda i: (jnp.maximum(order(i) * (SPAN // 8) - 1, 0), 0))
    return block, whole, [pl.BlockSpec(memory_space=pltpu.SMEM), block(MIX + WIDE + 128), before, whole((8, MIX)), whole((8, 256))]


def mixer_fwd(lens, proj, cw, pv):
    T = proj.shape[0]
    n = T // SPAN
    block, whole, first = mixer_specs(n, lambda i: i)
    return pl.pallas_call(
        mixer_fwd_kernel,
        grid=(n,),
        in_specs=first,
        out_specs=[block(WIDE), block(128), block(WIDE), pl.BlockSpec((1, WIDE, STATE), lambda i: (i, 0, 0))],
        out_shape=[jax.ShapeDtypeStruct((T, WIDE), BF), jax.ShapeDtypeStruct((T, 128), BF), jax.ShapeDtypeStruct((T, WIDE), F32),
                   jax.ShapeDtypeStruct((n, WIDE, STATE), F32)],
        scratch_shapes=[pltpu.VMEM((WIDE, STATE), F32)],
        compiler_params=pltpu.CompilerParams(vmem_limit_bytes=48 << 20, dimension_semantics=("arbitrary",)),
        cost_estimate=pl.CostEstimate(flops=4 << 30, bytes_accessed=16 << 20, transcendentals=4 << 20),
    )(lens, proj, proj, cw, pv)


def mixer_bwd(lens, proj, cw, pv, y, states, d_mix, g1_ext):
    T = proj.shape[0]
    n = T // SPAN
    order = lambda i: n - 1 - i
    block, whole, first = mixer_specs(n, order)
    at = g1_ext.shape[1] // 128 - 1
    return pl.pallas_call(
        mixer_bwd_kernel,
        grid=(n,),
        in_specs=first + [block(WIDE), pl.BlockSpec((1, WIDE, STATE), lambda i: (order(i), 0, 0)), block(WIDE),
                          pl.BlockSpec((SPAN, 128), lambda i: (order(i), at))],
        out_specs=[block(MIX + WIDE + 128), whole((8, MIX)), whole((8, 256))],
        out_shape=[jax.ShapeDtypeStruct((T, MIX + WIDE + 128), BF), jax.ShapeDtypeStruct((8, MIX), F32),
                   jax.ShapeDtypeStruct((8, 256), F32)],
        scratch_shapes=[pltpu.VMEM((WIDE, STATE), F32), pltpu.VMEM((8, MIX), F32)],
        compiler_params=pltpu.CompilerParams(vmem_limit_bytes=48 << 20, dimension_semantics=("arbitrary",)),
        cost_estimate=pl.CostEstimate(flops=12 << 30, bytes_accessed=24 << 20, transcendentals=8 << 20),
    )(lens, proj, proj, cw, pv, y, states, d_mix, g1_ext)


AHEAD_DIM = 64
SCALE = AHEAD_DIM ** (-0.5)
LOW = -1e30


def att_allowed(lens, i, j, n, flip):
    a, b = lax.broadcasted_iota(jnp.int32, (n, 1), 0), lax.broadcasted_iota(jnp.int32, (1, n), 1)
    qp, kp = (i * n + b, j * n + a) if flip else (i * n + a, j * n + b)
    return (kp <= qp) & (seg_at(kp, lens[0], lens[1]) == seg_at(qp, lens[0], lens[1]))


def att_fwd_kernel(lens, odd, qkv, attended, o_ref, lse):
    i = pl.program_id(0)
    n = o_ref.shape[0]
    lane = lax.broadcasted_iota(jnp.int32, (n, WIDE), 1)
    thin = lax.broadcasted_iota(jnp.int32, (n, 128), 1)
    mine = jnp.where((i == 0) | (i == 3), 0, 1) == odd[0]

    @pl.when(jnp.logical_not(mine))
    def _():
        attended[...] = jnp.zeros_like(attended)
        o_ref[...] = jnp.zeros_like(o_ref)
        lse[...] = jnp.zeros_like(lse)

    @pl.when(mine)
    def _():
        q = qkv[pl.ds(i * n, n), :WIDE] * jnp.asarray(SCALE, BF)
        heads = [jnp.where(lane // AHEAD_DIM == h, q, jnp.zeros_like(q)) for h in range(3)]

        def body(j, carry):
            tops, sums, acc = carry
            k, v = qkv[pl.ds(j * n, n), WIDE:2 * WIDE], qkv[pl.ds(j * n, n), 2 * WIDE:]
            allowed = att_allowed(lens, i, j, n, False)
            new_tops, new_sums = [], []
            for h in range(3):
                s = jnp.where(allowed, mm(heads[h], k, 1, 1), LOW)
                top = jnp.maximum(tops[h], jnp.max(s, axis=1, keepdims=True))
                p = jnp.exp(s - top)
                fade = jnp.exp(tops[h] - top)
                new_tops.append(top)
                new_sums.append(sums[h] * fade + jnp.sum(p, axis=1, keepdims=True))
                acc = jnp.where(lane // AHEAD_DIM == h, acc * fade + mm(p, v), acc)
            return tuple(new_tops), tuple(new_sums), acc

        zero = jnp.zeros((n, 1), F32)
        start = (tuple(zero + LOW for _ in range(3)), (zero,) * 3, jnp.zeros((n, WIDE), F32))
        tops, sums, acc = lax.fori_loop(0, i + 1, body, start)
        pick = lambda a: jnp.where(lane < AHEAD_DIM, a[0], jnp.where(lane < 2 * AHEAD_DIM, a[1], a[2]))
        out = acc / pick(sums)
        o_ref[...] = out
        attended[...] = out.astype(BF)
        logs = [t + jnp.log(s) for t, s in zip(tops, sums)]
        lse[...] = jnp.where(thin == 0, logs[0], jnp.where(thin == 1, logs[1], logs[2]))


def att_bwd_kernel(lens, odd, qkv, d_att, o_ref, lse, d_qkv, dk, dv):
    i = pl.program_id(0)
    n = lse.shape[0]
    lane = lax.broadcasted_iota(jnp.int32, (n, WIDE), 1)
    mine = jnp.where((i == 0) | (i == 3), 0, 1) == odd[0]

    @pl.when(i == 0)
    def _():
        dk[...] = jnp.zeros_like(dk)
        dv[...] = jnp.zeros_like(dv)

    @pl.when(jnp.logical_not(mine))
    def _():
        d_qkv[pl.ds(i * n, n), :WIDE] = jnp.zeros((n, WIDE), BF)

    @pl.when(mine)
    def _():
        q = qkv[pl.ds(i * n, n), :WIDE]
        do = d_att[...]
        delta = head_sums(o_ref[...] * do.astype(F32)).T
        logs = lse[...].T
        none = jnp.zeros_like(q)
        qs = [jnp.where(lane // AHEAD_DIM == h, q, none) for h in range(3)]
        dos = [jnp.where(lane // AHEAD_DIM == h, do, none) for h in range(3)]

        def body(j, dq):
            at = pl.ds(j * n, n)
            k, v = qkv[at, WIDE:2 * WIDE], qkv[at, 2 * WIDE:]
            allowed = att_allowed(lens, i, j, n, True)
            for h in range(3):
                s = mm(k, qs[h], 1, 1) * SCALE
                p = jnp.exp(jnp.where(allowed, s, LOW) - logs[h:h + 1])
                ds = (p * (mm(v, dos[h], 1, 1) - delta[h:h + 1]) * SCALE).astype(BF)
                dv[at, :] += mm(p, dos[h])
                dk[at, :] += mm(ds, qs[h])
                dq = jnp.where(lane // AHEAD_DIM == h, dq + mm(ds, k, 0, 0), dq)
            return dq

        dq = lax.fori_loop(0, i + 1, body, jnp.zeros((n, WIDE), F32))
        d_qkv[pl.ds(i * n, n), :WIDE] = dq.astype(BF)

    @pl.when(i == pl.num_programs(0) - 1)
    def _():
        d_qkv[:, WIDE:2 * WIDE] = dk[...].astype(BF)
        d_qkv[:, 2 * WIDE:] = dv[...].astype(BF)


def att_call(kernel, T, ins, blocked, out_specs, out_shape, scratch):
    n = T // 4
    smem = pl.BlockSpec(memory_space=pltpu.SMEM)
    specs = [smem, smem, pl.BlockSpec((T, 3 * WIDE), lambda i: (0, 0))]
    specs += [pl.BlockSpec((n, a.shape[1]), lambda i: (i, 0)) for a in blocked]
    return pl.pallas_call(
        kernel, grid=(4,), in_specs=specs, out_specs=out_specs, out_shape=out_shape, scratch_shapes=scratch,
        compiler_params=pltpu.CompilerParams(vmem_limit_bytes=56 << 20, dimension_semantics=("arbitrary",)),
        cost_estimate=pl.CostEstimate(flops=8 << 30, bytes_accessed=16 << 20, transcendentals=8 << 20),
    )(*ins, *blocked)


def att_fwd(lens, odd, qkv):
    T = qkv.shape[0]
    block = lambda w: pl.BlockSpec((T // 4, w), lambda i: (i, 0))
    return att_call(att_fwd_kernel, T, (lens, odd, qkv), (), [block(WIDE), block(WIDE), block(128)],
                    [jax.ShapeDtypeStruct((T, WIDE), BF), jax.ShapeDtypeStruct((T, WIDE), F32), jax.ShapeDtypeStruct((T, 128), F32)], [])


def att_bwd(lens, odd, qkv, d_att, o, lse):
    T = qkv.shape[0]
    return att_call(att_bwd_kernel, T, (lens, odd, qkv), (d_att, o, lse), pl.BlockSpec((T, 3 * WIDE), lambda i: (0, 0)),
                    jax.ShapeDtypeStruct((T, 3 * WIDE), BF), [pltpu.VMEM((T, WIDE), F32), pltpu.VMEM((T, WIDE), F32)])


P = jax.sharding.PartitionSpec
EPS = 1e-05


def dot(a, b):
    return jnp.dot(a, b, preferred_element_type=F32)


def dot_t(a, b):
    return lax.dot_general(a, b, (((1,), (1,)), ((), ())), preferred_element_type=F32)


def t_dot(a, b):
    return lax.dot_general(a, b, (((0,), (0,)), ((), ())), preferred_element_type=F32)


def cols_swap(pieces):
    c = lax.axis_index("cols")
    out = jnp.zeros_like(pieces)
    own = lax.dynamic_index_in_dim(pieces, c, 0, True)
    out = lax.dynamic_update_slice_in_dim(out, own, c, 0)
    for s in range(1, NC):
        away = lax.dynamic_index_in_dim(pieces, (c + s) % NC, 0, True)
        came = lax.ppermute(away, "cols", [(i, (i + s) % NC) for i in range(NC)])
        out = lax.dynamic_update_slice_in_dim(out, came, (c - s) % NC, 0)
    return out


def split_in(w):
    d, n = w.shape
    return w.reshape(d, NC, n // NC).transpose(1, 0, 2)


def split_pair(w):
    d, n = w.shape
    return jnp.repeat(w.reshape(d, 2, n // 2).transpose(1, 0, 2), NC // 2, axis=0)


def whole_out(got):
    return got.transpose(1, 0, 2).reshape(got.shape[1], -1)


def split_grad(g):
    n, d = g.shape
    return g.astype(BF).reshape(n, NC, d // NC).transpose(1, 0, 2)


def pair_sum(got):
    return got.astype(F32).reshape((2, NC // 2) + got.shape[1:]).sum(1).astype(BF)


def group_sum(own, others):
    return own.astype(F32) + others.astype(F32).sum(0)


def beside(a):
    k, d, n = a.shape
    return a.transpose(1, 0, 2).reshape(d, k * n)


def place_block(piece, start, full_len, axis):
    shape = piece.shape[:axis] + (full_len,) + piece.shape[axis + 1:]
    return lax.dynamic_update_slice_in_dim(jnp.zeros(shape, piece.dtype), piece, start, axis)


def rms_scale(x):
    return lax.rsqrt(jnp.mean(x * x, axis=1, keepdims=True) + EPS)


def norm_back(x, gain, scale, up):
    gain_grad = jnp.sum(x * scale * up, axis=0)
    tilted = up * gain[None, :]
    project = jnp.mean(x * tilted, axis=1, keepdims=True)
    return scale * tilted - x * (scale**3 * project), gain_grad


def per_device(hidden_in, lengths, norm1_gain, z_weight, x_weight, bcdt_weight, conv_x_weight, conv_x_bias,
               conv_bc_weight, conv_bc_bias, a_log, d_skip, dt_bias, gate_gain, mix_out_weight, norm2_gain,
               q_weight, k_weight, v_weight, att_out_weight, norm3_gain, up_weight, down_weight, grad_output):
    r, c = lax.axis_index("rows"), lax.axis_index("cols")
    rows = lax.axis_size("rows")
    tok_rows, feat = hidden_in.shape
    T, D = tok_rows * rows, feat * NC
    S = T // (rows * NC)
    slab = r * NC + c
    inner = z_weight.shape[1] * rows
    wide = z_weight.shape[1] // NC
    heads_row = a_log.shape[0]
    heads = heads_row // NC
    n_heads = heads_row * rows
    seq_lens = lengths[0]
    places = jnp.arange(T, dtype=jnp.int32)
    valid = (places < seq_lens[0] + seq_lens[1]).astype(F32)
    my_valid = lax.dynamic_slice_in_dim(valid, slab * S, S, 0)[:, None]
    pad = 128

    pair = "swap2" if lax.axis_size("dp") == 2 else "swap"

    def halved(a):
        return a.reshape(a.shape[0], 2, -1, a.shape[2]) if pair == "swap2" else a

    def joined(a):
        return a.reshape(a.shape[0], -1, a.shape[-1])

    zx_pieces = halved(jnp.concatenate([split_in(x_weight), split_in(z_weight)], axis=2))
    mix_pieces = halved(mix_out_weight.reshape(NC, -1, feat))
    bcdt_width = bcdt_weight.shape[1]
    bcdt_pad = -bcdt_width % 128
    bcdt_piece = jnp.pad(bcdt_weight, ((0, 0), (0, bcdt_pad))).reshape(2, feat // 2, -1)
    gain_piece = jnp.broadcast_to(jnp.pad(jnp.stack([norm1_gain, norm2_gain, norm3_gain]), ((0, 5), (0, 0)))[None], (2, 8, feat))
    hidden_all, w_zx, mix_got, w_bcdt, gains = gather_native(
        hidden_in, 0, (pair, pair, "bcast2", "bcast2"), (zx_pieces, mix_pieces, bcdt_piece, gain_piece))
    w_mix = whole_out(joined(mix_got))
    gains = gains[:, 0, :3].transpose(1, 0, 2).reshape(3, D)
    w_bcdt = w_bcdt.reshape(D, -1)
    w_dt = jnp.pad(lax.dynamic_slice_in_dim(w_bcdt, 2 * STATE + slab * heads, heads, 1), ((0, 0), (0, 128 - heads)))
    w_in = jnp.concatenate([w_bcdt[:, :2 * STATE], w_zx.reshape(D, 2 * wide), w_dt], axis=1)
    qkv_pieces = halved(jnp.concatenate([split_pair(q_weight), split_pair(k_weight), split_pair(v_weight)], axis=2))
    o_pieces = halved(jnp.repeat(att_out_weight.reshape(2, -1, feat), NC // 2, axis=0))
    grad_output, hidden_all = lax.optimization_barrier((grad_output, hidden_all))
    grad_all = lax.all_gather(grad_output, ("rows", "cols"), axis=0)
    grad_all = grad_all.reshape(rows, NC, tok_rows, feat).transpose(0, 2, 1, 3).reshape(T, D)

    hid_all = hidden_all.astype(F32)
    u1 = (hid_all * rms_scale(hid_all) * gains[0][None, :]).astype(BF)
    proj = dot(u1, w_in)
    mine = lambda a, n: lax.dynamic_slice_in_dim(a, c * n, n, a.ndim - 1)
    cw = jnp.concatenate([conv_bc_weight, mine(conv_x_weight, wide)], axis=1)
    cw = jnp.concatenate([cw, jnp.concatenate([conv_bc_bias, mine(conv_x_bias, wide)])[None], jnp.zeros((3, MIX), F32)])
    wide_row = lambda a: jnp.pad(a, (0, 256 - a.shape[0]))[None]
    pv = jnp.concatenate([wide_row(mine(gate_gain, wide)), wide_row(jnp.repeat(mine(d_skip, heads), HEAD_DIM)),
                          wide_row(mine(dt_bias, heads)), wide_row(-jnp.exp(mine(a_log, heads))), jnp.zeros((4, 256), F32)])
    mixg, squares, y, states = mixer_fwd(seq_lens, proj, cw, pv)
    part = jnp.concatenate([dot(mixg, w_mix).astype(BF), squares], axis=1)
    summed, qkv_got, o_got = reduce_scatter16(part, 2, (pair, pair), (qkv_pieces, o_pieces))
    w_qkv, w_o = qkv_got.reshape(D, -1), whole_out(joined(o_got))
    gate_scale = lax.rsqrt(summed[:, D:D + 1] / inner + EPS)
    mix_out = summed[:, :D] * gate_scale
    h0 = lax.dynamic_slice_in_dim(hidden_all, slab * S, S, 0).astype(F32)
    h1 = h0 + mix_out
    s2 = rms_scale(h1)
    u2, up_got = all_gather16((h1 * s2 * gains[1][None, :]).astype(BF), 3, (pair,), (halved(split_in(up_weight)),))
    w_up = up_got.reshape(D, -1)

    qkv = dot(u2, w_qkv).astype(BF)
    att = w_o.shape[0]
    odd = (c % 2)[None]
    attended, att_exact, lse = att_fwd(seq_lens, odd, qkv)
    att_part, down_got = reduce_scatter16(dot(attended, w_o).astype(BF), 4, (pair,), (halved(down_weight.reshape(NC, -1, feat)),))
    w_down = whole_out(joined(down_got))
    h2 = h1 + att_part
    s3 = rms_scale(h2)
    u3, = all_gather16((h2 * s3 * gains[2][None, :]).astype(BF), 1)

    act, = (dot(u3, w_up),)
    gelu, gelu_back = jax.vjp(functools.partial(jax.nn.gelu, approximate=True), act)
    hid = gelu.astype(BF)
    h3 = h2 + lax.psum_scatter(dot(hid, w_down).astype(BF), ("rows", "cols"), scatter_dimension=0, tiled=True).astype(F32)
    out_slab = (h3 * my_valid).astype(BF)
    output = cols_swap(out_slab.reshape(S, NC, feat).transpose(1, 0, 2)).reshape(NC * S, feat)

    g3 = (grad_all.astype(F32) * valid[:, None]).astype(BF)
    g3_mine = lax.dynamic_slice_in_dim(g3, slab * S, S, 0).astype(F32)
    d_act = gelu_back(dot_t(g3, w_down))[0].astype(BF)
    down_pieces = split_grad(t_dot(hid, g3))
    up_pieces = t_dot(u3, d_act).astype(BF).reshape(NC, feat, -1)
    d_u3, down_back = reduce_scatter16(dot_t(d_act, w_up).astype(BF), 6, ("swap",), (down_pieces,))
    d_n3, gain3_grad = norm_back(h2, gains[2], s3, d_u3)
    dh2 = g3_mine + d_n3
    g2, up_back, down_other = all_gather16(dh2.astype(BF), 7, ("swap", "dp"), (up_pieces, down_back))
    down_grad = group_sum(down_back, down_other).reshape(-1, feat)
    d_att = dot_t(g2, w_o).astype(BF)
    o_pieces = split_grad(t_dot(attended, g2))
    d_qkv = att_bwd(seq_lens, odd, qkv, d_att, att_exact, lse)
    qkv_pieces = t_dot(u2, d_qkv).astype(BF).reshape(NC, feat, -1)
    d_u2, o_back, up_other = reduce_scatter16(dot_t(d_qkv, w_qkv).astype(BF), 8, ("swap", "dp"), (o_pieces, up_back))
    up_grad = beside(group_sum(up_back, up_other))
    o_back = pair_sum(o_back)
    d_n2, gain2_grad = norm_back(h1, gains[1], s2, d_u2)
    dh1 = dh2 + d_n2
    tilt = gate_scale * gate_scale * jnp.sum(dh1 * mix_out, axis=1, keepdims=True) / inner
    tilt_hi = tilt.astype(BF)
    tilt_lo = (tilt - tilt_hi.astype(F32)).astype(BF)
    tail = jnp.concatenate([jnp.broadcast_to(tilt_hi, (S, pad // 2)), jnp.broadcast_to(tilt_lo, (S, pad // 2))], axis=1)
    g1_ext, qkv_back, o_other = all_gather16(jnp.concatenate([(dh1 * gate_scale).astype(BF), tail], axis=1), 9, ("swap", "dp"), (qkv_pieces, o_back))
    o_grad = group_sum(o_back, o_other).reshape(-1, feat)
    qkv_back = pair_sum(qkv_back)
    g1 = g1_ext[:, :D]
    d_mix = dot_t(g1, w_mix)
    mix_pieces = split_grad(t_dot(mixg, g1))
    d_in, tap_grads, row_grads = mixer_bwd(seq_lens, proj, cw, pv, y, states, d_mix, g1_ext)
    cbw_grad, cxw_grad = tap_grads[:CONV, :2 * STATE], tap_grads[:CONV, 2 * STATE:]
    cbb_grad, cxb_grad = tap_grads[CONV, :2 * STATE], tap_grads[CONV, 2 * STATE:]
    gate_gain_grad, dt_bias_grad, a_log_grad = row_grads[0, :wide], row_grads[2, :heads], row_grads[3, :heads]
    d_skip_grad = row_grads[1, :wide].reshape(heads, HEAD_DIM).sum(1)
    in_grad = t_dot(u1, d_in)
    zx_pieces = in_grad[:, 2 * STATE:2 * STATE + 2 * wide].astype(BF).reshape(NC, feat, -1)
    slabs = rows * NC
    dt_grads = place_block(in_grad[:, 2 * STATE + 2 * wide:2 * STATE + 2 * wide + heads].astype(BF), slab * heads, bcdt_width + bcdt_pad - 2 * STATE, 1)
    bcdt_part = jnp.concatenate([in_grad[:, :2 * STATE].astype(BF), dt_grads], axis=1).reshape(slabs, SMALL, -1)
    misc = jnp.concatenate([cbw_grad.reshape(-1), cbb_grad] + [
        place_block(a, slab * heads, n_heads, 0) for a in (a_log_grad, d_skip_grad, dt_bias_grad)])
    n_misc = misc.shape[0]
    small = jnp.concatenate([gain2_grad[None], gain3_grad[None], place_block(cxw_grad, slab * wide, inner, 1).reshape(-1, D),
                             place_block(cxb_grad, slab * wide, inner, 0).reshape(-1, D),
                             place_block(gate_gain_grad, slab * wide, inner, 0).reshape(-1, D), jnp.pad(misc, (0, D - n_misc))[None]])
    thin = bcdt_width + bcdt_pad
    four = D // thin
    small = jnp.pad(small, ((0, slabs - small.shape[0]), (0, 0))).reshape(slabs, four, thin)
    small_hi = small.astype(BF)
    small_lo = (small - small_hi.astype(F32)).astype(BF)
    side = jnp.concatenate([bcdt_part, small_hi, small_lo, jnp.zeros((slabs, S - SMALL - 2 * four, thin), BF)], axis=1)
    payload = jnp.concatenate([dot_t(d_in, w_in).astype(BF), side.reshape(T, thin)], axis=1)
    d_u1, zx_back, mix_back, qkv_other = reduce_scatter16(
        payload, 10, ("swap", "swap", "dp"), (zx_pieces, mix_pieces, qkv_back))
    rest, d_u1 = d_u1[:, D:], d_u1[:, :D]
    qkv_sum = group_sum(qkv_back, qkv_other)
    q_grad, k_grad, v_grad = (beside(qkv_sum[:, :, i * att:(i + 1) * att]) for i in range(3))
    d_n1, gain1_grad = norm_back(h0, gains[0], rms_scale(h0), d_u1)
    in_slab = dh1 + d_n1
    own = rest[SMALL:SMALL + four] + rest[SMALL + four:SMALL + 2 * four]
    gain1_rows = gain1_grad.reshape(four, thin)
    mine_small = jnp.concatenate([rest[:SMALL], own, own, own, gain1_rows, gain1_rows, gain1_rows,
                                  jnp.zeros((S - SMALL - 6 * four, thin), F32)])
    rest_all, in_got, zx_other, mix_other = gather16(
        mine_small, 11, False, ("swap", "dp", "dp"), (in_slab.reshape(S, NC, feat).transpose(1, 0, 2), zx_back, mix_back), four)
    rest_all = rest_all.reshape(slabs, S, thin)
    bcdt_grad = rest_all[:, :SMALL].reshape(D, thin)[:, :bcdt_width].astype(F32)
    tail_rows = rest_all[:, SMALL:SMALL + 6 * four].astype(F32).reshape(slabs, 6, D)
    small = tail_rows[:, 0] + tail_rows[:, 1] + tail_rows[:, 2]
    gain1_grad = (tail_rows[:, 3] + tail_rows[:, 4] + tail_rows[:, 5]).sum(0)
    per_inner = inner // D
    edges = [2 + CONV * per_inner, 2 + (CONV + 1) * per_inner, 2 + (CONV + 2) * per_inner]
    cxw_sum = small[2:edges[0]].reshape(CONV, inner)
    cxb_sum, gate_gain_sum = small[edges[0]:edges[1]].reshape(-1), small[edges[1]:edges[2]].reshape(-1)
    misc = small[edges[2]]
    cbw_sum, cbb_sum = misc[:CONV * 2 * STATE].reshape(CONV, 2 * STATE), misc[CONV * 2 * STATE:(CONV + 1) * 2 * STATE]
    a_log_sum, d_skip_sum, dt_bias_sum = jnp.split(misc[n_misc - 3 * n_heads:n_misc], 3)
    input_grad = in_got.reshape(NC * S, feat)
    zx_sum = group_sum(zx_back, zx_other)
    x_grad, z_grad = beside(zx_sum[:, :, :wide]), beside(zx_sum[:, :, wide:])
    mix_grad = group_sum(mix_back, mix_other).reshape(-1, feat)

    return (output, input_grad, gain1_grad, z_grad, x_grad, bcdt_grad, cxw_sum, cxb_sum, cbw_sum, cbb_sum, a_log_sum, d_skip_sum,
            dt_bias_sum, gate_gain_sum, mix_grad, small[0], q_grad, k_grad, v_grad, o_grad, small[1], up_grad, down_grad)


def solution(mesh):
    assert mesh.shape["rows"] == 4 and mesh.shape["cols"] == NC
    token = P(("dp", "rows"), "cols")
    w_in, w_out = P("cols", "rows"), P("rows", "cols")
    row, col, whole = P("rows"), P("cols"), P()
    placed = (token, P("dp", None), col, w_in, w_in, P("cols", None), P(None, "rows"), row, whole, whole, row, row, row, row,
              w_out, col, w_in, w_in, w_in, w_out, col, w_in, w_out, token)
    given = (token, token, whole, w_in, w_in, whole, whole, whole, whole, whole, whole, whole, whole, whole, w_out, whole,
             w_in, w_in, w_in, w_out, whole, w_in, w_out)
    return jax.shard_map(per_device, mesh=mesh, in_specs=placed, out_specs=given, check_vma=False)
```

```python
import functools
import jax, jax.numpy as jnp
from jax import lax
from jax.experimental import pallas as pl
from jax.experimental.pallas import tpu as pltpu
MESH = pl.DeviceIdType.MESH
NC = 4
F32, BF = jnp.float32, jnp.bfloat16


def copy_to(src, dst, send, recv, dev):
    return pltpu.make_async_remote_copy(src_ref=src, dst_ref=dst, send_sem=send, recv_sem=recv, device_id=dev, device_id_type=MESH)


def greet(r, c, kinds=()):
    barrier = pltpu.get_barrier_semaphore()
    all_cols = any(kind != "dp" for kind in kinds)
    pl.semaphore_signal(barrier, inc=1, device_id={"rows": r ^ 1}, device_id_type=MESH)
    pl.semaphore_signal(barrier, inc=1, device_id={"rows": r ^ 2}, device_id_type=MESH)
    count = 2
    if all_cols:
        for s in range(1, NC):
            pl.semaphore_signal(barrier, inc=1, device_id={"cols": lax.rem(c + s, NC)}, device_id_type=MESH)
        count += NC - 1
    else:
        @pl.when(c > 0)
        def _():
            pl.semaphore_signal(barrier, inc=1, device_id={"cols": c - 1}, device_id_type=MESH)

        @pl.when(c < NC - 1)
        def _():
            pl.semaphore_signal(barrier, inc=1, device_id={"cols": c + 1}, device_id_type=MESH)
        count = count + jnp.where(c > 0, 1, 0) + jnp.where(c < NC - 1, 1, 0)
    if any(kind in ("dp", "swap2", "reduce") for kind in kinds):
        groups = lax.axis_size("dp")
        for s in range(1, groups):
            pl.semaphore_signal(barrier, inc=1, device_id={"dp": lax.rem(lax.axis_index("dp") + s, groups)}, device_id_type=MESH)
        count = count + groups - 1
    pl.semaphore_wait(barrier, count)


class Riders:
    def __init__(self, kinds, ins, outs, send, recv, loc, *held):
        r, c, g = lax.axis_index("rows"), lax.axis_index("cols"), lax.axis_index("dp")
        groups = lax.axis_size("dp")
        self.remote, self.local, self.late, self.sums = [], [], [], []
        held = iter(held)
        for e, kind in enumerate(kinds):
            src, dst = ins[e], outs[e]
            if kind == "dp":
                for s in range(1, groups):
                    self.remote.append(copy_to(src, dst.at[s - 1], send.at[e, s - 1], recv.at[e, s - 1], {"dp": lax.rem(g + s, groups)}))
                continue
            if kind == "swap":
                for s in range(1, NC):
                    to = lax.rem(c + s, NC)
                    self.remote.append(copy_to(src.at[to], dst.at[c], send.at[e, s - 1], recv.at[e, s - 1], {"cols": to}))
                self.local.append(pltpu.make_async_copy(src.at[c], dst.at[c], loc.at[e]))
                continue
            half = r & 1 if kind == "bcast2" else g
            other = {"rows": r ^ 1} if kind == "bcast2" else {"dp": 1 - g}
            pairs = []
            if kind == "reduce":
                own, got = next(held), next(held)
                first = copy_to(src.at[:, 1 - g], got, send.at[e, 2 * NC - 1], recv.at[e, 2 * NC - 1], other)
                self.sums.append((first, pltpu.make_async_copy(src.at[:, g], own, loc.at[e]), own, got, pairs))
                piece = lambda to: own.at[to]
                keep = pltpu.make_async_copy(own.at[c], dst.at[c, g], loc.at[e])
                pairs.append((None, keep, copy_to(own.at[c], dst.at[c, g], send.at[e, NC - 1], recv.at[e, NC - 1], other)))
            elif kind == "swap2":
                piece = lambda to: src.at[to, half]
                self.local.append(pltpu.make_async_copy(src.at[c], dst.at[c], loc.at[e]))
            else:
                piece = lambda to: src.at[half]
                self.local.append(pltpu.make_async_copy(src, dst.at[c], loc.at[e]))
            for s in range(1, NC):
                to, came = lax.rem(c + s, NC), lax.rem(c + NC - s, NC)
                first = copy_to(piece(to), dst.at[c, half], send.at[e, s - 1], recv.at[e, s - 1], {"cols": to})
                pairs.append((first, None, copy_to(dst.at[came, half], dst.at[came, half], send.at[e, NC + s - 1], recv.at[e, NC + s - 1], other)))
            if kind != "reduce":
                self.late.extend(pairs)

    def start(self):
        for first, keep, own, got, pairs in self.sums:
            first.start()
            keep.start()
        for first, _, _ in self.late:
            first.start()
        for one in self.remote + self.local:
            one.start()

    def add(self):
        for first, keep, own, got, pairs in self.sums:
            keep.wait()
            first.wait()
            own[...] = (own[...].astype(F32) + got[...].astype(F32)).astype(BF)
            for one, local, second in pairs:
                if one is None:
                    local.start()
                    second.start()
                else:
                    one.start()

    def relay(self):
        for first, _, second in self.late + [p for one in self.sums for p in one[4] if p[0] is not None]:
            first.wait_recv()
            second.start()

    def finish(self):
        for one in self.remote + self.local:
            one.wait()
        for first, local, second in self.late + [p for one in self.sums for p in one[4]]:
            if first is None:
                local.wait()
            else:
                first.wait_send()
            second.wait()


def rider_parts(kinds, arrays):
    groups = lax.axis_size("dp")
    shapes = []
    for kind, a in zip(kinds, arrays):
        lead = {"swap": (), "swap2": (), "reduce": (), "bcast2": (NC,), "dp": (groups - 1,)}[kind]
        shapes.append(jax.ShapeDtypeStruct(lead + a.shape, a.dtype))
    n, most = len(kinds), max(2 * NC, groups)
    sems = [pltpu.SemaphoreType.DMA((n, most)), pltpu.SemaphoreType.DMA((n, most)), pltpu.SemaphoreType.DMA((n,))] if n else []
    for kind, a in zip(kinds, arrays):
        if kind == "reduce":
            sems += [pltpu.VMEM(a.shape[:1] + a.shape[2:], a.dtype)] * 2
    return shapes, sems


SMALL = 96


def sum_groups(x_ref, others, held, dp_s, dp_r, n):
    g, groups = lax.axis_index("dp"), lax.axis_size("dp")
    copies = [copy_to(x_ref, others.at[s - 1], dp_s.at[s - 1], dp_r.at[s - 1], {"dp": lax.rem(g + s, groups)}) for s in range(1, groups)]
    for one in copies:
        one.start()
    total = x_ref[...]
    for s, one in enumerate(copies):
        one.wait()
        total = total + others[s]
    part = (lax.broadcasted_iota(jnp.int32, total.shape, 0) - SMALL) // n
    rest = total - total.astype(BF).astype(F32)
    rest2 = rest - rest.astype(BF).astype(F32)
    second, third = (part == 1) | (part == 4), (part == 2) | (part == 5)
    held[...] = jnp.where(second, rest, jnp.where(third, rest2, total)).astype(BF)
    return held


def ag_kernel(native, at, kinds, *refs):
    n = len(kinds)
    x_ref, ins, out_ref, outs = refs[0], refs[1:1 + n], refs[1 + n], refs[2 + n:2 + 2 * n]
    recv, zr_s, zl_s, y_s, k_s, loc, *sems = refs[2 + 2 * n:]
    r, c = lax.axis_index("rows"), lax.axis_index("cols")
    S, W = x_ref.shape
    greet(r, c, kinds)
    riding = Riders(kinds, ins, outs, *sems) if n else Riders((), (), (), None, None, None)

    def slab(rr, cc):
        if native:
            return out_ref.at[pl.ds(pl.multiple_of(rr * S, 16), S), pl.ds(pl.multiple_of(cc * W, 128), W)]
        return out_ref.at[pl.ds(pl.multiple_of((rr * NC + cc) * S, 16), S)]

    def right(cc, src):
        return copy_to(src, slab(r, cc), zr_s.at[cc], recv.at[r * NC + cc], {"cols": c + 1})

    def left(cc, src):
        return copy_to(src, slab(r, cc), zl_s.at[cc], recv.at[r * NC + cc], {"cols": c - 1})

    def ycopy(cc, src):
        return copy_to(src, slab(r, cc), y_s.at[cc], recv.at[r * NC + cc], {"rows": r ^ 2})

    def kcopy(rr, cc, src):
        return copy_to(src, slab(rr, cc), k_s.at[(rr >> 1) * NC + cc], recv.at[rr * NC + cc], {"rows": r ^ 1})

    def got(rr, cc):
        copy_to(slab(rr, cc), slab(rr, cc), k_s.at[0], recv.at[rr * NC + cc], {"rows": r ^ 1}).wait_recv()

    @pl.when(c < NC - 1)
    def _():
        right(c, x_ref).start()

    @pl.when(c > 0)
    def _():
        left(c, x_ref).start()
    ycopy(c, x_ref).start()
    kcopy(r, c, x_ref).start()
    own = pltpu.make_async_copy(x_ref, slab(r, c), loc)
    own.start()
    if at == 0:
        riding.start()

    def from_y(cc):
        got(r ^ 2, cc)
        kcopy(r ^ 2, cc, slab(r ^ 2, cc)).start()

    for d in range(1, NC):
        @pl.when(c >= d)
        def _():
            cc = c - d
            got(r, cc)

            @pl.when(c < NC - 1)
            def _():
                right(cc, slab(r, cc)).start()
            ycopy(cc, slab(r, cc)).start()
            kcopy(r, cc, slab(r, cc)).start()

        @pl.when(c + d < NC)
        def _():
            cc = c + d
            got(r, cc)

            @pl.when(c > 0)
            def _():
                left(cc, slab(r, cc)).start()
            ycopy(cc, slab(r, cc)).start()
            kcopy(r, cc, slab(r, cc)).start()
        if d == at:
            riding.start()
        if d == 1:
            from_y(c)
        else:
            @pl.when(c >= d - 1)
            def _():
                from_y(c - (d - 1))

            @pl.when(c + d - 1 < NC)
            def _():
                from_y(c + d - 1)
    d = NC

    @pl.when(c >= d - 1)
    def _():
        from_y(c - (d - 1))

    @pl.when(c + d - 1 < NC)
    def _():
        from_y(c + d - 1)
    for cc in range(NC):
        got(r ^ 1, cc)
        got(r ^ 3, cc)
    own.wait()
    for cc in range(NC):
        y_c = ycopy(cc, slab(r, cc))
        y_c.wait_send()
        kcopy(r, cc, slab(r, cc)).wait_send()
        kcopy(r ^ 2, cc, slab(r ^ 2, cc)).wait_send()

        @pl.when((cc <= c) & (c < NC - 1))
        def _():
            right(cc, slab(r, cc)).wait_send()

        @pl.when((cc >= c) & (c > 0))
        def _():
            left(cc, slab(r, cc)).wait_send()
    riding.relay()
    riding.finish()


def gather16(x, cid, native, kinds, arrays, at=0):
    S, D = x.shape
    shapes, sems = rider_parts(kinds, arrays)
    any_space = pl.BlockSpec(memory_space=pl.ANY)
    return pl.pallas_call(
        functools.partial(ag_kernel, native, at, tuple(kinds)),
        out_shape=[jax.ShapeDtypeStruct((4 * S, NC * D) if native else (16 * S, D), BF)] + shapes,
        in_specs=[pl.BlockSpec(memory_space=pltpu.VMEM)] + [any_space] * len(kinds),
        out_specs=[pl.BlockSpec(memory_space=pltpu.VMEM)] + [any_space] * len(kinds),
        scratch_shapes=[pltpu.SemaphoreType.DMA((16,)), pltpu.SemaphoreType.DMA((NC,)), pltpu.SemaphoreType.DMA((NC,)),
                        pltpu.SemaphoreType.DMA((NC,)), pltpu.SemaphoreType.DMA((2 * NC,)), pltpu.SemaphoreType.DMA] + sems,
        compiler_params=pltpu.CompilerParams(collective_id=cid, has_side_effects=True, vmem_limit_bytes=48 << 20),
        cost_estimate=pl.CostEstimate(flops=0, bytes_accessed=64 << 20, transcendentals=0),
    )(x, *arrays)


def gather_native(x, cid, kinds=(), arrays=()):
    return gather16(x, cid, True, kinds, arrays)


HEAD_DIM = 64
STATE = 128
CONV = 4
SPAN = 256
HIGH = lax.Precision.HIGHEST
WIDE = 192
MIX = 2 * STATE + WIDE


def mm(a, b, ca=1, cb=0):
    return lax.dot_general(a.astype(BF), b.astype(BF), (((ca,), (cb,)), ((), ())), preferred_element_type=F32)


def exact(a, b, ca=1, cb=0):
    return lax.dot_general(a, b, (((ca,), (cb,)), ((), ())), preferred_element_type=F32, precision=HIGH)


def seg_at(place, l0, l1):
    return jnp.where(place < 0, -1, jnp.where(place >= l0, 1, 0) + jnp.where(place >= l0 + l1, 1, 0))


def sigmoid(x):
    return 1.0 / (1.0 + jnp.exp(-x))


def by_head(a, lane):
    return jnp.where(lane < HEAD_DIM, a[:, 0:1], jnp.where(lane < 2 * HEAD_DIM, a[:, 1:2], a[:, 2:3]))


def head_sums(a):
    i = lax.broadcasted_iota(jnp.int32, (WIDE, 128), 0)
    j = lax.broadcasted_iota(jnp.int32, (WIDE, 128), 1)
    return exact(a, jnp.where(i // HEAD_DIM == j, 1.0, 0.0).astype(F32))


class Block:
    def __init__(self, blk, lens, proj, before, cw, pv):
        self.l0, self.l1 = lens[0], lens[1]
        self.start = blk * SPAN
        v = proj[:, :MIX]
        self.place = self.start + lax.broadcasted_iota(jnp.int32, (SPAN, 1), 0)
        self.seg = seg_at(self.place, self.l0, self.l1)
        ext = jnp.concatenate([before[:, :MIX], v], axis=0)
        acc = cw[4:5] + cw[3:4] * v
        self.shifted = [v]
        for s in range(1, CONV):
            keep = jnp.where(seg_at(self.place - s, self.l0, self.l1) == self.seg, 1.0, 0.0)
            moved = ext[8 - s:8 - s + SPAN] * keep
            self.shifted.append(moved)
            acc = acc + cw[3 - s:4 - s] * moved
        self.acc = acc
        self.gate = sigmoid(acc)
        act = acc * self.gate
        self.b, self.c, self.x = act[:, :STATE], act[:, STATE:2 * STATE], act[:, 2 * STATE:]
        self.z = proj[:, MIX:MIX + WIDE]
        self.zs = sigmoid(self.z)
        self.raw = proj[:, MIX + WIDE:] + pv[2:3, :128]
        self.dt = jnp.maximum(self.raw, 0.0) + jnp.log1p(jnp.exp(-jnp.abs(self.raw)))
        self.rate = pv[3:4, :128] * self.dt
        i = lax.broadcasted_iota(jnp.int32, (SPAN, SPAN), 0)
        j = lax.broadcasted_iota(jnp.int32, (SPAN, SPAN), 1)
        self.low = jnp.where(j <= i, 1.0, 0.0).astype(F32)
        self.cum = exact(self.low, self.rate)
        self.cum_t = self.cum.T
        seg_row = seg_at(self.start + lax.broadcasted_iota(jnp.int32, (1, SPAN), 1), self.l0, self.l1)
        self.allowed = (j <= i) & (seg_row == self.seg)
        self.scores = mm(self.c, self.b, 1, 1)
        self.lane = lax.broadcasted_iota(jnp.int32, (SPAN, WIDE), 1)
        self.w = self.x * by_head(self.dt, self.lane)
        prior = seg_at(self.start - 1, self.l0, self.l1)
        last = seg_at(self.start + SPAN - 1, self.l0, self.l1)
        end = self.cum[SPAN - 1:SPAN]
        self.e = by_head(jnp.exp(self.cum), self.lane) * jnp.where(self.seg == prior, 1.0, 0.0)
        self.tail = by_head(jnp.exp(end - self.cum), self.lane) * jnp.where(self.seg == last, 1.0, 0.0)
        self.through = jnp.exp(end) * jnp.where(last == prior, 1.0, 0.0)
        row = lax.broadcasted_iota(jnp.int32, (WIDE, 1), 0)
        self.through_rows = jnp.where(row < HEAD_DIM, self.through[:, 0:1],
                                      jnp.where(row < 2 * HEAD_DIM, self.through[:, 1:2], self.through[:, 2:3]))

    def decay(self, h):
        return jnp.exp(jnp.where(self.allowed, self.cum[:, h:h + 1] - self.cum_t[h:h + 1, :], -1e30))

    def of_head(self, a, h):
        return jnp.where(self.lane // HEAD_DIM == h, a, 0.0)


def mixer_fwd_kernel(lens, proj, before, cw, pv, mixg, squares, y_out, states, state):
    blk = pl.program_id(0)

    @pl.when(blk == 0)
    def _():
        state[...] = jnp.zeros_like(state)
    k = Block(blk, lens, proj[...], before[...], cw[...], pv[...])
    s_in = state[...]
    states[0] = s_in
    y = mm(k.c, s_in, 1, 1) * k.e
    for h in range(3):
        y = y + mm(k.scores * k.decay(h), k.of_head(k.w, h))
    y = y + pv[1:2, :WIDE] * k.x
    state[...] = k.through_rows * s_in + mm(k.tail * k.w, k.b, 0, 0)
    y_out[...] = y
    gated = y * k.z * k.zs
    mixg[...] = (gated * pv[0:1, :WIDE]).astype(BF)
    squares[...] = jnp.broadcast_to(jnp.sum(gated * gated, axis=1, keepdims=True), squares.shape).astype(BF)


def mixer_bwd_kernel(lens, proj, before, cw, pv, y_ref, states, d_mix, extra, d_in, taps, rows, d_state, later):
    step = pl.program_id(0)
    blk = pl.num_programs(0) - 1 - step

    @pl.when(step == 0)
    def _():
        d_state[...] = jnp.zeros_like(d_state)
        later[...] = jnp.zeros_like(later)
        taps[...] = jnp.zeros_like(taps)
        rows[...] = jnp.zeros_like(rows)
    k = Block(blk, lens, proj[...], before[...], cw[...], pv[...])
    y, dm, s_in, ds = y_ref[...], d_mix[...], states[0], d_state[...]
    tilt = extra[:, 0:1].astype(F32) + extra[:, 64:65].astype(F32)
    silu_z = k.z * k.zs
    gated = y * silu_z
    d_gated = dm * pv[0:1, :WIDE] - gated * tilt
    d_z = d_gated * y * (k.zs * (1.0 + k.z * (1.0 - k.zs)))
    dy = d_gated * silu_z
    zeros = jnp.zeros((SPAN, 128), F32)
    lane = lax.broadcasted_iota(jnp.int32, (SPAN, 128), 1)
    top = lax.broadcasted_iota(jnp.int32, (128, SPAN), 0)
    d_cum, cols = zeros, jnp.zeros((128, SPAN), F32)
    d_scores = jnp.zeros((SPAN, SPAN), F32)
    dw = jnp.zeros((SPAN, WIDE), F32)
    for h in range(3):
        decay = k.decay(h)
        mixing = k.scores * decay
        dyh = k.of_head(dy, h).astype(BF)
        d_mixing = mm(dyh, k.w, 1, 1)
        d_scores = d_scores + d_mixing * decay
        moved = d_mixing * mixing
        d_cum = jnp.where(lane == h, jnp.sum(moved, axis=1, keepdims=True), d_cum)
        cols = jnp.where(top == h, jnp.sum(moved, axis=0, keepdims=True), cols)
        dw = dw + mm(mixing, dyh, 0, 0)
    e_dy, tail_w = k.e * dy, k.tail * k.w
    back = mm(k.b, ds, 1, 1)
    dw = dw + k.tail * back
    d_c = mm(d_scores, k.b) + mm(e_dy, s_in)
    d_b = mm(d_scores, k.c, 0, 0) + mm(tail_w, ds)
    through_state = mm(k.c, s_in, 1, 1) * k.e
    left = head_sums(tail_w * back)
    d_cum = d_cum - cols.T + head_sums(dy * through_state) - left
    own = jnp.sum(ds * s_in, axis=1, keepdims=True)
    of_row = lax.broadcasted_iota(jnp.int32, (WIDE, 128), 0) // HEAD_DIM
    own = jnp.sum(jnp.where(of_row == lax.broadcasted_iota(jnp.int32, (WIDE, 128), 1), own, 0.0), axis=0, keepdims=True)
    at_end = jnp.sum(left, axis=0, keepdims=True) + k.through * own
    is_last = lax.broadcasted_iota(jnp.int32, (SPAN, 128), 0) == SPAN - 1
    d_cum = d_cum + jnp.where(is_last, at_end, 0.0)
    d_rate = exact(k.low, d_cum, 0, 0)
    d_dt = head_sums(dw * k.x) + d_rate * pv[3:4, :128]
    d_raw = jnp.where(lane < 3, d_dt * sigmoid(k.raw), 0.0)
    d_x = dw * by_head(k.dt, k.lane) + pv[1:2, :WIDE] * dy
    d_pre = jnp.concatenate([d_b, d_c, d_x], axis=1) * (k.gate * (1.0 + k.acc * (1.0 - k.gate)))
    wide_rows = [jnp.sum(gated * dm, axis=0, keepdims=True), jnp.sum(dy * k.x, axis=0, keepdims=True)]
    thin_rows = [jnp.sum(d_raw, axis=0, keepdims=True), jnp.sum(d_rate * k.rate, axis=0, keepdims=True)]
    for i, one in enumerate(wide_rows):
        rows[i:i + 1, :WIDE] += one
    for i, one in enumerate(thin_rows):
        rows[2 + i:3 + i, :128] += one
    for s in range(CONV):
        taps[3 - s:4 - s] += jnp.sum(d_pre * k.shifted[s], axis=0, keepdims=True)
    taps[4:5] += jnp.sum(d_pre, axis=0, keepdims=True)
    ext = jnp.concatenate([d_pre, later[...]], axis=0)
    place = k.start + lax.broadcasted_iota(jnp.int32, (SPAN + 8, 1), 0)
    seg = seg_at(place, k.l0, k.l1)
    d_v = cw[3:4] * d_pre
    for s in range(1, CONV):
        keep = jnp.where(seg_at(place - s, k.l0, k.l1) == seg, 1.0, 0.0)
        d_v = d_v + cw[3 - s:4 - s] * (ext * keep)[s:s + SPAN]
    later[...] = d_pre[:8]
    d_in[...] = jnp.concatenate([d_v, d_z, d_raw], axis=1).astype(BF)
    d_state[...] = k.through_rows * ds + mm(e_dy, k.c, 0, 0)


def mixer_specs(n, order):
    block = lambda width: pl.BlockSpec((SPAN, width), lambda i: (order(i), 0))
    whole = lambda shape: pl.BlockSpec(shape, lambda i: (0, 0))
    before = pl.BlockSpec((8, MIX + WIDE + 128), lambda i: (jnp.maximum(order(i) * (SPAN // 8) - 1, 0), 0))
    return block, whole, [pl.BlockSpec(memory_space=pltpu.SMEM), block(MIX + WIDE + 128), before, whole((8, MIX)), whole((8, 256))]


def mixer_fwd(lens, proj, cw, pv):
    T = proj.shape[0]
    n = T // SPAN
    block, whole, first = mixer_specs(n, lambda i: i)
    return pl.pallas_call(
        mixer_fwd_kernel,
        grid=(n,),
        in_specs=first,
        out_specs=[block(WIDE), block(128), block(WIDE), pl.BlockSpec((1, WIDE, STATE), lambda i: (i, 0, 0))],
        out_shape=[jax.ShapeDtypeStruct((T, WIDE), BF), jax.ShapeDtypeStruct((T, 128), BF), jax.ShapeDtypeStruct((T, WIDE), F32),
                   jax.ShapeDtypeStruct((n, WIDE, STATE), F32)],
        scratch_shapes=[pltpu.VMEM((WIDE, STATE), F32)],
        compiler_params=pltpu.CompilerParams(vmem_limit_bytes=48 << 20, dimension_semantics=("arbitrary",)),
        cost_estimate=pl.CostEstimate(flops=4 << 30, bytes_accessed=16 << 20, transcendentals=4 << 20),
    )(lens, proj, proj, cw, pv)


def mixer_bwd(lens, proj, cw, pv, y, states, d_mix, g1_ext):
    T = proj.shape[0]
    n = T // SPAN
    order = lambda i: n - 1 - i
    block, whole, first = mixer_specs(n, order)
    at = g1_ext.shape[1] // 128 - 1
    return pl.pallas_call(
        mixer_bwd_kernel,
        grid=(n,),
        in_specs=first + [block(WIDE), pl.BlockSpec((1, WIDE, STATE), lambda i: (order(i), 0, 0)), block(WIDE),
                          pl.BlockSpec((SPAN, 128), lambda i: (order(i), at))],
        out_specs=[block(MIX + WIDE + 128), whole((8, MIX)), whole((8, 256))],
        out_shape=[jax.ShapeDtypeStruct((T, MIX + WIDE + 128), BF), jax.ShapeDtypeStruct((8, MIX), F32),
                   jax.ShapeDtypeStruct((8, 256), F32)],
        scratch_shapes=[pltpu.VMEM((WIDE, STATE), F32), pltpu.VMEM((8, MIX), F32)],
        compiler_params=pltpu.CompilerParams(vmem_limit_bytes=48 << 20, dimension_semantics=("arbitrary",)),
        cost_estimate=pl.CostEstimate(flops=12 << 30, bytes_accessed=24 << 20, transcendentals=8 << 20),
    )(lens, proj, proj, cw, pv, y, states, d_mix, g1_ext)


AHEAD_DIM = 64
SCALE = AHEAD_DIM ** (-0.5)
LOW = -1e30


def att_allowed(lens, i, j, n, flip):
    a, b = lax.broadcasted_iota(jnp.int32, (n, 1), 0), lax.broadcasted_iota(jnp.int32, (1, n), 1)
    qp, kp = (i * n + b, j * n + a) if flip else (i * n + a, j * n + b)
    return (kp <= qp) & (seg_at(kp, lens[0], lens[1]) == seg_at(qp, lens[0], lens[1]))


def att_fwd_kernel(lens, odd, qkv, attended, o_ref, lse):
    i = pl.program_id(0)
    n = o_ref.shape[0]
    lane = lax.broadcasted_iota(jnp.int32, (n, WIDE), 1)
    thin = lax.broadcasted_iota(jnp.int32, (n, 128), 1)
    mine = jnp.where((i == 0) | (i == 3), 0, 1) == odd[0]

    @pl.when(jnp.logical_not(mine))
    def _():
        attended[...] = jnp.zeros_like(attended)
        o_ref[...] = jnp.zeros_like(o_ref)
        lse[...] = jnp.zeros_like(lse)

    @pl.when(mine)
    def _():
        q = qkv[pl.ds(i * n, n), :WIDE] * jnp.asarray(SCALE, BF)
        heads = [jnp.where(lane // AHEAD_DIM == h, q, jnp.zeros_like(q)) for h in range(3)]

        def body(j, carry):
            tops, sums, acc = carry
            k, v = qkv[pl.ds(j * n, n), WIDE:2 * WIDE], qkv[pl.ds(j * n, n), 2 * WIDE:]
            allowed = att_allowed(lens, i, j, n, False)
            new_tops, new_sums = [], []
            for h in range(3):
                s = jnp.where(allowed, mm(heads[h], k, 1, 1), LOW)
                top = jnp.maximum(tops[h], jnp.max(s, axis=1, keepdims=True))
                p = jnp.exp(s - top)
                fade = jnp.exp(tops[h] - top)
                new_tops.append(top)
                new_sums.append(sums[h] * fade + jnp.sum(p, axis=1, keepdims=True))
                acc = jnp.where(lane // AHEAD_DIM == h, acc * fade + mm(p, v), acc)
            return tuple(new_tops), tuple(new_sums), acc

        zero = jnp.zeros((n, 1), F32)
        start = (tuple(zero + LOW for _ in range(3)), (zero,) * 3, jnp.zeros((n, WIDE), F32))
        tops, sums, acc = lax.fori_loop(0, i + 1, body, start)
        pick = lambda a: jnp.where(lane < AHEAD_DIM, a[0], jnp.where(lane < 2 * AHEAD_DIM, a[1], a[2]))
        out = acc / pick(sums)
        o_ref[...] = out
        attended[...] = out.astype(BF)
        logs = [t + jnp.log(s) for t, s in zip(tops, sums)]
        lse[...] = jnp.where(thin == 0, logs[0], jnp.where(thin == 1, logs[1], logs[2]))


def att_bwd_kernel(lens, odd, qkv, d_att, o_ref, lse, d_qkv, dk, dv):
    i = pl.program_id(0)
    n = lse.shape[0]
    lane = lax.broadcasted_iota(jnp.int32, (n, WIDE), 1)
    mine = jnp.where((i == 0) | (i == 3), 0, 1) == odd[0]

    @pl.when(i == 0)
    def _():
        dk[...] = jnp.zeros_like(dk)
        dv[...] = jnp.zeros_like(dv)

    @pl.when(jnp.logical_not(mine))
    def _():
        d_qkv[pl.ds(i * n, n), :WIDE] = jnp.zeros((n, WIDE), BF)

    @pl.when(mine)
    def _():
        q = qkv[pl.ds(i * n, n), :WIDE]
        do = d_att[...]
        delta = head_sums(o_ref[...] * do.astype(F32)).T
        logs = lse[...].T
        none = jnp.zeros_like(q)
        qs = [jnp.where(lane // AHEAD_DIM == h, q, none) for h in range(3)]
        dos = [jnp.where(lane // AHEAD_DIM == h, do, none) for h in range(3)]

        def body(j, dq):
            at = pl.ds(j * n, n)
            k, v = qkv[at, WIDE:2 * WIDE], qkv[at, 2 * WIDE:]
            allowed = att_allowed(lens, i, j, n, True)
            for h in range(3):
                s = mm(k, qs[h], 1, 1) * SCALE
                p = jnp.exp(jnp.where(allowed, s, LOW) - logs[h:h + 1])
                ds = (p * (mm(v, dos[h], 1, 1) - delta[h:h + 1]) * SCALE).astype(BF)
                dv[at, :] += mm(p, dos[h])
                dk[at, :] += mm(ds, qs[h])
                dq = jnp.where(lane // AHEAD_DIM == h, dq + mm(ds, k, 0, 0), dq)
            return dq

        dq = lax.fori_loop(0, i + 1, body, jnp.zeros((n, WIDE), F32))
        d_qkv[pl.ds(i * n, n), :WIDE] = dq.astype(BF)

    @pl.when(i == pl.num_programs(0) - 1)
    def _():
        d_qkv[:, WIDE:2 * WIDE] = dk[...].astype(BF)
        d_qkv[:, 2 * WIDE:] = dv[...].astype(BF)


def att_call(kernel, T, ins, blocked, out_specs, out_shape, scratch):
    n = T // 4
    smem = pl.BlockSpec(memory_space=pltpu.SMEM)
    specs = [smem, smem, pl.BlockSpec((T, 3 * WIDE), lambda i: (0, 0))]
    specs += [pl.BlockSpec((n, a.shape[1]), lambda i: (i, 0)) for a in blocked]
    return pl.pallas_call(
        kernel, grid=(4,), in_specs=specs, out_specs=out_specs, out_shape=out_shape, scratch_shapes=scratch,
        compiler_params=pltpu.CompilerParams(vmem_limit_bytes=56 << 20, dimension_semantics=("arbitrary",)),
        cost_estimate=pl.CostEstimate(flops=8 << 30, bytes_accessed=16 << 20, transcendentals=8 << 20),
    )(*ins, *blocked)


def att_fwd(lens, odd, qkv):
    T = qkv.shape[0]
    block = lambda w: pl.BlockSpec((T // 4, w), lambda i: (i, 0))
    return att_call(att_fwd_kernel, T, (lens, odd, qkv), (), [block(WIDE), block(WIDE), block(128)],
                    [jax.ShapeDtypeStruct((T, WIDE), BF), jax.ShapeDtypeStruct((T, WIDE), F32), jax.ShapeDtypeStruct((T, 128), F32)], [])


def att_bwd(lens, odd, qkv, d_att, o, lse):
    T = qkv.shape[0]
    return att_call(att_bwd_kernel, T, (lens, odd, qkv), (d_att, o, lse), pl.BlockSpec((T, 3 * WIDE), lambda i: (0, 0)),
                    jax.ShapeDtypeStruct((T, 3 * WIDE), BF), [pltpu.VMEM((T, WIDE), F32), pltpu.VMEM((T, WIDE), F32)])


VMEM, ANY = pltpu.VMEM, pl.ANY


HALVES = 2


class Sum:
    def __init__(self, r, c, partial, bufs):
        self.r, self.c, self.partial = r, c, partial
        self.yy, self.kk = r >> 1, r & 1
        (self.part, self.p_out, self.k_buf, self.y_out, self.y_buf, self.zr_out, self.zl_out, self.r_buf, self.l_buf,
         self.k_s, self.k_r, self.y_s, self.y_r, self.zr_s, self.zr_r, self.zl_s, self.zl_r) = bufs
        self.cut = self.part.shape[1] // HALVES

    @staticmethod
    def scratch(S, W):
        buf, sem = (lambda *n: VMEM(n + (S, W), BF)), (lambda n: pltpu.SemaphoreType.DMA((n,)))
        return [VMEM((NC, S, W), F32), buf(2, NC), buf(2, NC)] + [buf(NC)] * 6 + [sem(2 * NC), sem(2 * NC)] + [sem(HALVES * NC)] * 6

    def k_copy(self, y, cc):
        i = y * NC + cc
        return copy_to(self.p_out.at[y, cc], self.k_buf.at[y, cc], self.k_s.at[i], self.k_r.at[i], {"rows": self.r ^ 1})

    def piece(self, src, dst, send, recv, cc, h, to):
        at, i = pl.ds(h * self.cut, self.cut), cc * HALVES + h
        return copy_to(src.at[cc, at], dst.at[cc, at], send.at[i], recv.at[i], to)

    def y_copy(self, cc, h):
        return self.piece(self.y_out, self.y_buf, self.y_s, self.y_r, cc, h, {"rows": self.r ^ 2})

    def r_copy(self, cc, h):
        return self.piece(self.zr_out, self.r_buf, self.zr_s, self.zr_r, cc, h, {"cols": self.c + 1})

    def l_copy(self, cc, h):
        return self.piece(self.zl_out, self.l_buf, self.zl_s, self.zl_r, cc, h, {"cols": self.c - 1})

    def nth(self, j):
        return jnp.where(self.c < NC // 2, NC - 1 - j, j)

    def each(self, f):
        def body(j, carry):
            f(self.nth(j))
            return carry
        lax.fori_loop(0, NC, body, 0)

    def to_core(self):
        def half(i, carry):
            y = jnp.where(i == 0, 1 - self.yy, self.yy)

            def one(cc):
                self.p_out[y, cc] = self.partial(y * 2 + (1 - self.kk), cc).astype(BF)
                self.k_copy(y, cc).start()
            self.each(one)
            return carry
        lax.fori_loop(0, 2, half, 0)

    def to_y(self):
        def one(cc):
            mine = self.partial((1 - self.yy) * 2 + self.kk, cc)
            self.k_copy(1 - self.yy, cc).wait_recv()
            self.y_out[cc] = (mine + self.k_buf[1 - self.yy, cc].astype(F32)).astype(BF)
            for h in range(HALVES):
                self.y_copy(cc, h).start()
        self.each(one)

    def own(self):
        def one(cc):
            mine = self.partial(self.r, cc)
            self.k_copy(self.yy, cc).wait_recv()
            self.part[cc] = mine + self.k_buf[self.yy, cc].astype(F32)
        self.each(one)

    def step(self, j):
        c, cc = self.c, self.nth(j)
        for h in range(HALVES):
            at = pl.ds(h * self.cut, self.cut)
            self.y_copy(cc, h).wait_recv()
            self.part[cc, at] += self.y_buf[cc, at].astype(F32)

            @pl.when(cc > c)
            def _():
                @pl.when(c > 0)
                def _():
                    self.r_copy(cc, h).wait_recv()
                    self.part[cc, at] += self.r_buf[cc, at].astype(F32)
                self.zr_out[cc, at] = self.part[cc, at].astype(BF)
                self.r_copy(cc, h).start()

            @pl.when(cc < c)
            def _():
                @pl.when(c < NC - 1)
                def _():
                    self.l_copy(cc, h).wait_recv()
                    self.part[cc, at] += self.l_buf[cc, at].astype(F32)
                self.zl_out[cc, at] = self.part[cc, at].astype(BF)
                self.l_copy(cc, h).start()

    def last(self, total):
        c = self.c
        total[...] = self.part[c]

        @pl.when(c > 0)
        def _():
            for h in range(HALVES):
                self.r_copy(c, h).wait_recv()
            total[...] += self.r_buf[c].astype(F32)

        @pl.when(c < NC - 1)
        def _():
            for h in range(HALVES):
                self.l_copy(c, h).wait_recv()
            total[...] += self.l_buf[c].astype(F32)

    def finish(self):
        def one(cc):
            self.k_copy(0, cc).wait_send()
            self.k_copy(1, cc).wait_send()
            for h in range(HALVES):
                self.y_copy(cc, h).wait_send()

                @pl.when(cc > self.c)
                def _():
                    self.r_copy(cc, h).wait_send()

                @pl.when(cc < self.c)
                def _():
                    self.l_copy(cc, h).wait_send()
        self.each(one)


class Gather:
    def __init__(self, r, c, out, S, sems, use=None):
        self.r, self.c, self.out, self.S, self.use = r, c, out, S, use
        self.recv, self.zr_s, self.zl_s, self.y_s, self.k_s = sems

    @staticmethod
    def scratch():
        return [pltpu.SemaphoreType.DMA((HALVES * n,)) for n in (4 * NC, NC, NC, NC, 2 * NC)]

    def slab(self, rr, cc):
        return self.out.at[pl.ds(pl.multiple_of((rr * NC + cc) * self.S, 16), self.S)]

    def move(self, rr, cc, h, sem, to):
        cut = self.S // HALVES
        ref = self.out.at[pl.ds(pl.multiple_of((rr * NC + cc) * self.S + h * cut, 16), cut)]
        return copy_to(ref, ref, sem, self.recv.at[(rr * NC + cc) * HALVES + h], to)

    def right(self, cc, h):
        return self.move(self.r, cc, h, self.zr_s.at[cc * HALVES + h], {"cols": self.c + 1})

    def left(self, cc, h):
        return self.move(self.r, cc, h, self.zl_s.at[cc * HALVES + h], {"cols": self.c - 1})

    def y_copy(self, cc, h):
        return self.move(self.r, cc, h, self.y_s.at[cc * HALVES + h], {"rows": self.r ^ 2})

    def k_copy(self, rr, cc, h):
        return self.move(rr, cc, h, self.k_s.at[((rr >> 1) * NC + cc) * HALVES + h], {"rows": self.r ^ 1})

    def got(self, rr, cc, h):
        self.k_copy(rr, cc, h).wait_recv()

    def pass_on(self, cc, h):
        c = self.c

        @pl.when((cc <= c) & (c < NC - 1))
        def _():
            self.right(cc, h).start()

        @pl.when((cc >= c) & (c > 0))
        def _():
            self.left(cc, h).start()
        self.y_copy(cc, h).start()
        self.k_copy(self.r, cc, h).start()

    def begin(self):
        for h in range(HALVES):
            self.pass_on(self.c, h)

    def sides(self, off, f):
        for h in range(HALVES):
            for s in (-1, 1):
                cc = self.c + s * off
                fits = (cc >= 0) & (cc < NC) & (off < NC)
                if s == 1:
                    fits = fits & (off > 0)

                @pl.when(fits)
                def _():
                    f(cc, h)

    def forward(self, d):
        def along(cc, h):
            self.got(self.r, cc, h)
            self.pass_on(cc, h)

        def across(cc, h):
            self.got(self.r ^ 2, cc, h)
            self.k_copy(self.r ^ 2, cc, h).start()
        self.sides(d, along)
        self.sides(d - 1, across)

    def uses(self, d):
        def one(i, carry):
            kind, s = i >> 1, (i & 1) * 2 - 1
            off = d - jnp.where(kind == 0, 0, jnp.where(kind == 3, 2, 1))
            rr = self.r ^ jnp.where(kind == 0, 0, jnp.where(kind == 1, 2, jnp.where(kind == 2, 1, 3)))
            cc = self.c + s * off
            fits = (off >= 0) & (off < NC) & (cc >= 0) & (cc < NC) & ((s < 0) | (off > 0))

            @pl.when(fits)
            def _():
                @pl.when(kind >= 2)
                def _():
                    for h in range(HALVES):
                        self.got(rr, cc, h)
                if self.use is not None:
                    self.use(rr, cc)
            return carry
        lax.fori_loop(0, 8, one, 0)

    def stage(self, d):
        self.forward(d)
        self.uses(d)

    def finish(self):
        def body(cc, carry):
            for h in range(HALVES):
                self.y_copy(cc, h).wait_send()
                self.k_copy(self.r, cc, h).wait_send()
                self.k_copy(self.r ^ 2, cc, h).wait_send()

                @pl.when((cc <= self.c) & (self.c < NC - 1))
                def _():
                    self.right(cc, h).wait_send()

                @pl.when((cc >= self.c) & (self.c > 0))
                def _():
                    self.left(cc, h).wait_send()
            return carry
        lax.fori_loop(0, NC, body, 0)


def link_call(kernel, cid, ins, in_spaces, outs, out_spaces, scratch, flops):
    return pl.pallas_call(
        kernel,
        out_shape=[jax.ShapeDtypeStruct(s, d) for s, d in outs],
        in_specs=[pl.BlockSpec(memory_space=s) for s in in_spaces],
        out_specs=[pl.BlockSpec(memory_space=s) for s in out_spaces],
        scratch_shapes=scratch,
        compiler_params=pltpu.CompilerParams(collective_id=cid, has_side_effects=True, vmem_limit_bytes=60 << 20),
        cost_estimate=pl.CostEstimate(flops=flops, bytes_accessed=96 << 20, transcendentals=0),
    )(*ins)


def link_kernel(spec, *refs):
    it = iter(refs)
    take = lambda n: [next(it) for _ in range(n)]
    maybe = lambda key, n=1: take(n) if spec[key] else [None] * n
    a, w1 = take(2)
    side, = maybe("side")
    mid_in = take(spec["n_mid"])
    w2, = take(1) if spec["w2"] in ("in", "in_t") else [None]
    a2, v2 = maybe("more_sum", 2)
    slab2, = maybe("more_gather")
    early_in = take(len(spec["early"]))
    late_in = take(sum(src is None for _, src in spec["late"]))
    u_all = next(it)
    mid_out = take(spec["n_mid_out"])
    post_out = take(spec["n_post"])
    sum2, = maybe("more_sum")
    all2, = maybe("more_gather")
    early_out, late_out = take(len(spec["early"])), take(len(spec["late"]))
    total, = take(1)
    sum_bufs, gather_sems = take(17), take(5)
    sum2_bufs = take(18) if spec["more_sum"] else []
    gather2_sems = take(6) if spec["more_gather"] else []
    small = take(6) if spec["small"] else None
    early_sems, late_sems = take(spec["n_early_sems"]), take(spec["n_late_sems"])
    r, c = lax.axis_index("rows"), lax.axis_index("cols")
    S, W = total.shape
    D = w1.shape[0] if spec["w1_t"] else w1.shape[1]
    late_kinds = tuple(kind for kind, _ in spec["late"])
    greet(r, c, spec["early"] + late_kinds + (("dp",) if spec["small"] else ()))
    none = [None] * 3
    early = Riders(spec["early"], early_in, early_out, *(early_sems or none))
    late_in = iter(late_in)
    sources = [next(late_in) if src is None else mid_out[src] for _, src in spec["late"]]
    late = Riders(late_kinds, sources, late_out, *(late_sems or none))
    rows_of = lambda rr, cc: pl.ds(pl.multiple_of((rr * NC + cc) * S, 16), S)

    def partial(rr, cc):
        p = mm(a[rows_of(rr, cc), :], w1[...], 1, 1 if spec["w1_t"] else 0)
        return p if side is None else jnp.concatenate([p, side[rows_of(rr, cc), :].astype(F32)], axis=1)

    def use(rr, cc):
        w = early_out[0][...].reshape(D, -1) if spec["w2"] == "rider" else w2[...]
        u = u_all[rows_of(rr, cc), :D] if u_all.shape[1] > D else u_all[rows_of(rr, cc), :]
        spec["post"](mm(u, w, 1, 1 if spec["w2"] == "in_t" else 0), rows_of(rr, cc), post_out)

    summing = Sum(r, c, partial, sum_bufs)
    gather = Gather(r, c, u_all, S, gather_sems, use if spec["w2"] else None)
    summing2 = gather2 = None
    if spec["more_gather"]:
        gather2 = Gather(r, c, all2, S, gather2_sems[:5])
        own2 = pltpu.make_async_copy(slab2, gather2.slab(r, c), gather2_sems[5])
        own2.start()
    summing.to_core()
    early.start()
    summing.to_y()
    if gather2:
        own2.wait()
        gather2.begin()
    if spec["more_sum"]:
        summing2 = Sum(r, c, lambda rr, cc: mm(a2[rows_of(rr, cc), :], v2[...]), sum2_bufs[:17])
        summing2.to_core()
        summing2.to_y()
        summing2.own()
    summing.own()
    summing.step(0)
    summing.step(1)
    early.add()
    summing.step(2)
    if gather2:
        gather2.stage(1)
    summing.step(3)
    summing.last(total)
    if spec["small"]:
        mine, others, held, dp_s, dp_r, loc = small
        spec["mid"](total, mid_in, mid_out, mine)
        late.start()
        sum_groups(mine, others, held, dp_s, dp_r, 4)
        place = pltpu.make_async_copy(held, gather.slab(r, c), loc)
        place.start()
        place.wait()
        gather.begin()
    else:
        u_all[rows_of(r, c), :] = spec["mid"](total, mid_in, mid_out)
        gather.begin()
        late.start()
    if spec["w2"] == "rider":
        early.relay()
        gather.forward(1)
        early.finish()
    if spec["w2"]:
        use(r, c)
    for d in range(1, NC + 2):
        if summing2 and d <= NC:
            summing2.step(d - 1)
        if gather2 and d < NC + 1:
            gather2.stage(d + 1)
        if d > 1 or spec["w2"] != "rider":
            gather.forward(d)
        gather.uses(d)
        if d == 2 and spec["w2"] != "rider":
            early.relay()
    gather.finish()
    summing.finish()
    if gather2:
        gather2.finish()
    if summing2:
        summing2.last(sum2_bufs[17])
        sum2[...] = sum2_bufs[17][...]
        summing2.finish()
    late.add()
    late.relay()
    if spec["w2"] != "rider":
        early.finish()
    late.finish()


def link(cid, a, w1, mid, mid_in, mid_out, *, w1_t=False, side=None, w2=None, w2_kind=None, post=None, post_out=(), early=(), early_in=(),
         late=(), late_in=(), extra=0, small=0, more_sum=None, more_gather=None):
    T = a.shape[0]
    D = w1.shape[0] if w1_t else w1.shape[1]
    S = T // (4 * NC)
    W = D + (0 if side is None else side.shape[1])
    width = small or D + extra
    early_shapes, early_sems = rider_parts(early, early_in)
    late_it = iter(late_in)
    late_arrays = [next(late_it) if src is None else jax.ShapeDtypeStruct(*mid_out[src]) for _, src in late]
    late_shapes, late_sems = rider_parts(tuple(k for k, _ in late), late_arrays)
    spec = dict(w1_t=w1_t, side=side is not None, mid=mid, n_mid=len(mid_in), n_mid_out=len(mid_out), w2=w2_kind, post=post,
                n_post=len(post_out), early=tuple(early), late=tuple(late), small=small, more_sum=more_sum is not None,
                more_gather=more_gather is not None, n_early_sems=len(early_sems), n_late_sems=len(late_sems))
    ins = [a, w1] + ([side] if side is not None else []) + list(mid_in) + ([w2] if w2 is not None else [])
    ins += list(more_sum or ()) + ([more_gather] if more_gather is not None else [])
    in_spaces = [VMEM] * len(ins) + [ANY] * (len(early_in) + len(late_in))
    ins += list(early_in) + list(late_in)
    outs = [((T, width), BF)] + list(mid_out) + list(post_out)
    if more_sum is not None:
        outs.append(((S, D), F32))
    if more_gather is not None:
        outs.append(((T, D), BF))
    out_spaces = [VMEM] * len(outs) + [ANY] * len(early_shapes + late_shapes)
    if w2_kind == "rider":
        out_spaces[len(outs)] = VMEM
    outs += [(s.shape, s.dtype) for s in early_shapes + late_shapes]
    scratch = [VMEM((S, W), F32)] + Sum.scratch(S, W) + Gather.scratch()
    if more_sum is not None:
        scratch += Sum.scratch(S, D) + [VMEM((S, D), F32)]
    if more_gather is not None:
        scratch += Gather.scratch() + [pltpu.SemaphoreType.DMA]
    if small:
        groups = lax.axis_size("dp")
        scratch += [VMEM((S, small), F32), VMEM((groups - 1, S, small), F32), VMEM((S, small), BF), pltpu.SemaphoreType.DMA((groups - 1,)),
                    pltpu.SemaphoreType.DMA((groups - 1,)), pltpu.SemaphoreType.DMA]
    scratch += early_sems + late_sems
    return link_call(functools.partial(link_kernel, spec), cid, ins, in_spaces, outs, out_spaces, scratch, 8 << 30)


EPS = 1e-05


def norm_scale(x):
    return lax.rsqrt(jnp.mean(x * x, axis=1, keepdims=True) + EPS)


def norm_grad(x, gain, up, gain_grad):
    s = norm_scale(x)
    gain_grad[0:1] = jnp.sum(x * s * up, axis=0, keepdims=True)
    tilted = up * gain
    return s * tilted - x * (s * s * s * jnp.mean(x * tilted, axis=1, keepdims=True))


def mid_mixer(inner, total, ins, outs):
    h0, gain = ins
    h1, mix_out, gate_scale = outs
    D = h0.shape[1]
    s = lax.rsqrt(total[:, D:D + 1] / inner + EPS)
    out = total[:, :D] * s
    mix_out[...] = out
    gate_scale[...] = jnp.broadcast_to(s, gate_scale.shape)
    h = h0[...].astype(F32) + out
    h1[...] = h
    return (h * norm_scale(h) * gain[...]).astype(BF)


def mid_attention(total, ins, outs):
    h1, gain = ins
    h = h1[...] + total[...]
    outs[0][...] = h
    return (h * norm_scale(h) * gain[...]).astype(BF)


def mid_ff_back(total, ins, outs):
    h2, gain, grad = ins
    dh2, gain_grad = outs
    d = grad[...].astype(F32) + norm_grad(h2[...], gain[...], total[...], gain_grad)
    dh2[...] = d
    return d.astype(BF)


def mid_att_back(inner, total, ins, outs):
    h1, gain, dh2, mix_out, gate_scale = ins
    dh1, gain_grad = outs
    d = dh2[...] + norm_grad(h1[...], gain[...], total[...], gain_grad)
    dh1[...] = d
    s = gate_scale[:, 0:1]
    tilt = s * s * jnp.sum(d * mix_out[...], axis=1, keepdims=True) / inner
    high = tilt.astype(BF).astype(F32)
    lane = lax.broadcasted_iota(jnp.int32, (d.shape[0], 128), 1)
    return jnp.concatenate([d * s, jnp.where(lane < 64, high, tilt - high)], axis=1).astype(BF)


def mid_mixer_back(total, ins, outs, small):
    h0, gain, dh1 = ins
    in_slab, gain_grad = outs
    D = h0.shape[1]
    thin = small.shape[1]
    four = D // thin
    d = dh1[...] + norm_grad(h0[...].astype(F32), gain[...], total[:, :D], gain_grad)
    feat = D // NC
    for i in range(NC):
        in_slab[i] = d[:, i * feat:(i + 1) * feat]
    rest = total[:, D:]
    small[...] = jnp.zeros_like(small)
    small[:SMALL] = rest[:SMALL]
    own = rest[SMALL:SMALL + four] + rest[SMALL + four:SMALL + 2 * four]
    row = gain_grad[0:1]
    for i in range(3):
        small[SMALL + i * four:SMALL + (i + 1) * four] = own
        for j in range(four):
            at = SMALL + (3 + i) * four + j
            small[at:at + 1] = row[:, j * thin:(j + 1) * thin]


def post_plain(p, at, outs):
    outs[0][at, :] = p.astype(outs[0].dtype)


def post_gelu(p, at, outs):
    outs[0][at, :] = p
    outs[1][at, :] = (0.5 * p * (1.0 + jnp.tanh(0.7978845608028654 * (p + 0.044715 * (p * p * p))))).astype(BF)


P = jax.sharding.PartitionSpec


def dot(a, b):
    return jnp.dot(a, b, preferred_element_type=F32)


def dot_t(a, b):
    return lax.dot_general(a, b, (((1,), (1,)), ((), ())), preferred_element_type=F32)


def t_dot(a, b):
    return lax.dot_general(a, b, (((0,), (0,)), ((), ())), preferred_element_type=F32)


def split_in(w):
    d, n = w.shape
    return w.reshape(d, NC, n // NC).transpose(1, 0, 2)


def split_pair(w):
    d, n = w.shape
    return jnp.repeat(w.reshape(d, 2, n // 2).transpose(1, 0, 2), NC // 2, axis=0)


def whole_out(got):
    return got.transpose(1, 0, 2).reshape(got.shape[1], -1)


def split_grad(g):
    n, d = g.shape
    return g.astype(BF).reshape(n, NC, d // NC).transpose(1, 0, 2)


def pair_sum(got):
    return got.astype(F32).reshape((2, NC // 2) + got.shape[1:]).sum(1)


def beside(a):
    k, d, n = a.shape
    return a.transpose(1, 0, 2).reshape(d, k * n)


def place_block(piece, start, full_len, axis):
    shape = piece.shape[:axis] + (full_len,) + piece.shape[axis + 1:]
    return lax.dynamic_update_slice_in_dim(jnp.zeros(shape, piece.dtype), piece, start, axis)


def rms_scale(x):
    return lax.rsqrt(jnp.mean(x * x, axis=1, keepdims=True) + EPS)


def per_device(hidden_in, lengths, norm1_gain, z_weight, x_weight, bcdt_weight, conv_x_weight, conv_x_bias,
               conv_bc_weight, conv_bc_bias, a_log, d_skip, dt_bias, gate_gain, mix_out_weight, norm2_gain,
               q_weight, k_weight, v_weight, att_out_weight, norm3_gain, up_weight, down_weight, grad_output):
    r, c = lax.axis_index("rows"), lax.axis_index("cols")
    rows = lax.axis_size("rows")
    tok_rows, feat = hidden_in.shape
    T, D = tok_rows * rows, feat * NC
    S = T // (rows * NC)
    slab = r * NC + c
    inner = z_weight.shape[1] * rows
    wide = z_weight.shape[1] // NC
    heads_row = a_log.shape[0]
    heads = heads_row // NC
    n_heads = heads_row * rows
    seq_lens = lengths[0]
    places = jnp.arange(T, dtype=jnp.int32)
    one_f32, row8 = ((S, D), F32), ((8, D), F32)
    valid = (places < seq_lens[0] + seq_lens[1]).astype(F32)
    my_valid = lax.dynamic_slice_in_dim(valid, slab * S, S, 0)[:, None]
    pad = 128

    pair = "swap2" if lax.axis_size("dp") == 2 else "swap"

    def halved(a):
        return a.reshape(a.shape[0], 2, -1, a.shape[2]) if pair == "swap2" else a

    def joined(a):
        return a.reshape(a.shape[0], -1, a.shape[-1])

    zx_pieces = halved(jnp.concatenate([split_in(x_weight), split_in(z_weight)], axis=2))
    mix_pieces = halved(mix_out_weight.reshape(NC, -1, feat))
    bcdt_width = bcdt_weight.shape[1]
    bcdt_pad = -bcdt_width % 128
    bcdt_piece = jnp.pad(bcdt_weight, ((0, 0), (0, bcdt_pad))).reshape(2, feat // 2, -1)
    gain_piece = jnp.broadcast_to(jnp.pad(jnp.stack([norm1_gain, norm2_gain, norm3_gain]), ((0, 5), (0, 0)))[None], (2, 8, feat))
    hidden_all, w_zx, mix_got, w_bcdt, gains = gather_native(
        hidden_in, 0, (pair, pair, "bcast2", "bcast2"), (zx_pieces, mix_pieces, bcdt_piece, gain_piece))
    w_mix = whole_out(joined(mix_got))
    gains = gains[:, 0, :3].transpose(1, 0, 2).reshape(3, D)
    w_bcdt = w_bcdt.reshape(D, -1)
    w_dt = jnp.pad(lax.dynamic_slice_in_dim(w_bcdt, 2 * STATE + slab * heads, heads, 1), ((0, 0), (0, 128 - heads)))
    w_in = jnp.concatenate([w_bcdt[:, :2 * STATE], w_zx.reshape(D, 2 * wide), w_dt], axis=1)
    qkv_pieces = halved(jnp.concatenate([split_pair(q_weight), split_pair(k_weight), split_pair(v_weight)], axis=2))
    o_pieces = halved(jnp.repeat(att_out_weight.reshape(2, -1, feat), NC // 2, axis=0))

    hid_all = hidden_all.astype(F32)
    u1 = (hid_all * rms_scale(hid_all) * gains[0][None, :]).astype(BF)
    proj = dot(u1, w_in)
    mine = lambda a, n: lax.dynamic_slice_in_dim(a, c * n, n, a.ndim - 1)
    cw = jnp.concatenate([conv_bc_weight, mine(conv_x_weight, wide)], axis=1)
    cw = jnp.concatenate([cw, jnp.concatenate([conv_bc_bias, mine(conv_x_bias, wide)])[None], jnp.zeros((3, MIX), F32)])
    wide_row = lambda a: jnp.pad(a, (0, 256 - a.shape[0]))[None]
    pv = jnp.concatenate([wide_row(mine(gate_gain, wide)), wide_row(jnp.repeat(mine(d_skip, heads), HEAD_DIM)),
                          wide_row(mine(dt_bias, heads)), wide_row(-jnp.exp(mine(a_log, heads))), jnp.zeros((4, 256), F32)])
    mixg, squares, y, states = mixer_fwd(seq_lens, proj, cw, pv)
    h0 = lax.dynamic_slice_in_dim(hidden_all, slab * S, S, 0)
    att3 = qkv_pieces.shape[-1]
    u2, h1, mix_out, gate_scale, qkv, qkv_got, o_got, grad_got = link(
        1, mixg, w_mix, functools.partial(mid_mixer, inner), (h0, gains[1:2]), (one_f32, one_f32, ((S, 128), F32)), side=squares,
        w2_kind="rider", post=post_plain, post_out=(((T, att3), BF),), early=(pair, pair), early_in=(qkv_pieces, o_pieces),
        late=(("swap", None),), late_in=(grad_output.reshape(NC, S, feat),))
    w_qkv, w_o = qkv_got.reshape(D, -1), whole_out(joined(o_got))
    g3_mine = (grad_got.transpose(1, 0, 2).reshape(S, D).astype(F32) * my_valid).astype(BF)
    att = att3 // 3

    odd = (c % 2)[None]
    attended, att_exact, lse = att_fwd(seq_lens, odd, qkv)
    hidden_units = up_weight.shape[1] // NC
    u3, h2, act, hid, g3, up_got, down_got = link(
        2, attended, w_o, mid_attention, (h1, gains[2:3]), (one_f32,), w2_kind="rider", post=post_gelu,
        post_out=(((T, hidden_units), F32), ((T, hidden_units), BF)), early=(pair,), early_in=(halved(split_in(up_weight)),),
        late=((pair, None),), late_in=(halved(down_weight.reshape(NC, -1, feat)),), more_gather=g3_mine)
    w_up, w_down = up_got.reshape(D, -1), whole_out(joined(down_got))
    gelu_back = jax.vjp(functools.partial(jax.nn.gelu, approximate=True), act)[1]

    reduce = "reduce" if pair == "swap2" else "swap"

    def settle(got):
        return joined(got) if reduce == "reduce" else lax.psum(got, "dp")

    d_act = gelu_back(dot_t(g3, w_down))[0].astype(BF)
    down_pieces = halved(split_grad(t_dot(hid, g3)))
    up_pieces = halved(t_dot(u3, d_act).astype(BF).reshape(NC, feat, -1))
    g2, dh2, gain3_rows, d_att, ff_out, down_back, up_back = link(
        3, d_act, w_up, mid_ff_back, (h2, gains[2:3], g3_mine), (one_f32, row8), w1_t=True, w2=w_o, w2_kind="in_t", post=post_plain,
        post_out=(((T, att), BF),), early=(reduce, reduce), early_in=(down_pieces, up_pieces), more_sum=(hid, w_down))
    out_slab = ((h2 + ff_out) * my_valid).astype(BF)
    o_pieces = halved(split_grad(t_dot(attended, g2)))
    d_qkv = att_bwd(seq_lens, odd, qkv, d_att, att_exact, lse)
    qkv_pieces = halved(t_dot(u2, d_qkv).astype(BF).reshape(NC, feat, -1))
    g1_ext, dh1, gain2_rows, d_mix, o_back, qkv_back, out_got = link(
        4, d_qkv, w_qkv, functools.partial(mid_att_back, inner), (h1, gains[1:2], dh2, mix_out, gate_scale), (one_f32, row8), w1_t=True,
        w2=w_mix, w2_kind="in_t", post=post_plain, post_out=(((T, wide), F32),), extra=128,
        early=(reduce, reduce), early_in=(o_pieces, qkv_pieces), late=(("swap", None),), late_in=(out_slab.reshape(S, NC, feat).transpose(1, 0, 2),))
    g1 = g1_ext[:, :D]
    output = out_got.reshape(NC * S, feat)
    down_grad = settle(down_back).astype(F32).reshape(-1, feat)
    up_grad = beside(settle(up_back)).astype(F32)
    o_grad = pair_sum(settle(o_back)).reshape(-1, feat)
    qkv_sum = pair_sum(settle(qkv_back))
    q_grad, k_grad, v_grad = (beside(qkv_sum[:, :, i * att:(i + 1) * att]) for i in range(3))
    mix_pieces = halved(split_grad(t_dot(mixg, g1)))
    d_in, tap_grads, row_grads = mixer_bwd(seq_lens, proj, cw, pv, y, states, d_mix, g1_ext)
    cbw_grad, cxw_grad = tap_grads[:CONV, :2 * STATE], tap_grads[:CONV, 2 * STATE:]
    cbb_grad, cxb_grad = tap_grads[CONV, :2 * STATE], tap_grads[CONV, 2 * STATE:]
    gate_gain_grad, dt_bias_grad, a_log_grad = row_grads[0, :wide], row_grads[2, :heads], row_grads[3, :heads]
    d_skip_grad = row_grads[1, :wide].reshape(heads, HEAD_DIM).sum(1)
    in_grad = t_dot(u1, d_in)
    zx_pieces = halved(in_grad[:, 2 * STATE:2 * STATE + 2 * wide].astype(BF).reshape(NC, feat, -1))
    slabs = rows * NC
    dt_grads = place_block(in_grad[:, 2 * STATE + 2 * wide:2 * STATE + 2 * wide + heads].astype(BF), slab * heads, bcdt_width + bcdt_pad - 2 * STATE, 1)
    bcdt_part = jnp.concatenate([in_grad[:, :2 * STATE].astype(BF), dt_grads], axis=1).reshape(slabs, SMALL, -1)
    misc = jnp.concatenate([cbw_grad.reshape(-1), cbb_grad] + [
        place_block(a, slab * heads, n_heads, 0) for a in (a_log_grad, d_skip_grad, dt_bias_grad)])
    n_misc = misc.shape[0]
    small = jnp.concatenate([gain2_rows[:1], gain3_rows[:1], place_block(cxw_grad, slab * wide, inner, 1).reshape(-1, D),
                             place_block(cxb_grad, slab * wide, inner, 0).reshape(-1, D),
                             place_block(gate_gain_grad, slab * wide, inner, 0).reshape(-1, D), jnp.pad(misc, (0, D - n_misc))[None]])
    thin = bcdt_width + bcdt_pad
    four = D // thin
    small = jnp.pad(small, ((0, slabs - small.shape[0]), (0, 0))).reshape(slabs, four, thin)
    small_hi = small.astype(BF)
    small_lo = (small - small_hi.astype(F32)).astype(BF)
    side = jnp.concatenate([bcdt_part, small_hi, small_lo, jnp.zeros((slabs, S - SMALL - 2 * four, thin), BF)], axis=1)
    rest_all, _, _, zx_back, mix_back, in_got = link(
        5, d_in, w_in, mid_mixer_back, (h0, gains[0:1], dh1), (((NC, S, feat), F32), row8), w1_t=True, side=side.reshape(T, thin), small=thin,
        early=(reduce, reduce), early_in=(zx_pieces, mix_pieces), late=(("swap", 0),))
    rest_all = rest_all.reshape(slabs, S, thin)
    bcdt_grad = rest_all[:, :SMALL].reshape(D, thin)[:, :bcdt_width].astype(F32)
    tail_rows = rest_all[:, SMALL:SMALL + 6 * four].astype(F32).reshape(slabs, 6, D)
    small = tail_rows[:, 0] + tail_rows[:, 1] + tail_rows[:, 2]
    gain1_grad = (tail_rows[:, 3] + tail_rows[:, 4] + tail_rows[:, 5]).sum(0)
    per_inner = inner // D
    edges = [2 + CONV * per_inner, 2 + (CONV + 1) * per_inner, 2 + (CONV + 2) * per_inner]
    cxw_sum = small[2:edges[0]].reshape(CONV, inner)
    cxb_sum, gate_gain_sum = small[edges[0]:edges[1]].reshape(-1), small[edges[1]:edges[2]].reshape(-1)
    misc = small[edges[2]]
    cbw_sum, cbb_sum = misc[:CONV * 2 * STATE].reshape(CONV, 2 * STATE), misc[CONV * 2 * STATE:(CONV + 1) * 2 * STATE]
    a_log_sum, d_skip_sum, dt_bias_sum = jnp.split(misc[n_misc - 3 * n_heads:n_misc], 3)
    input_grad = in_got.reshape(NC * S, feat)
    zx_sum = settle(zx_back).astype(F32)
    x_grad, z_grad = beside(zx_sum[:, :, :wide]), beside(zx_sum[:, :, wide:])
    mix_grad = settle(mix_back).astype(F32).reshape(-1, feat)
    return (output, input_grad, gain1_grad, z_grad, x_grad, bcdt_grad, cxw_sum, cxb_sum, cbw_sum, cbb_sum, a_log_sum, d_skip_sum,
            dt_bias_sum, gate_gain_sum, mix_grad, small[0], q_grad, k_grad, v_grad, o_grad, small[1], up_grad, down_grad)


def solution(mesh):
    assert mesh.shape["rows"] == 4 and mesh.shape["cols"] == NC
    token = P(("dp", "rows"), "cols")
    w_in, w_out = P("cols", "rows"), P("rows", "cols")
    row, col, whole = P("rows"), P("cols"), P()
    placed = (token, P("dp", None), col, w_in, w_in, P("cols", None), P(None, "rows"), row, whole, whole, row, row, row, row,
              w_out, col, w_in, w_in, w_in, w_out, col, w_in, w_out, token)
    given = (token, token, whole, w_in, w_in, whole, whole, whole, whole, whole, whole, whole, whole, whole, w_out, whole,
             w_in, w_in, w_in, w_out, whole, w_in, w_out)
    return jax.shard_map(per_device, mesh=mesh, in_specs=placed, out_specs=given, check_vma=False)
```

```python
import functools
import jax, jax.numpy as jnp
from jax import lax
from jax.experimental import pallas as pl
from jax.experimental.pallas import tpu as pltpu
MESH = pl.DeviceIdType.MESH
NC = 4
F32, BF = jnp.float32, jnp.bfloat16


def copy_to(src, dst, send, recv, dev):
    return pltpu.make_async_remote_copy(src_ref=src, dst_ref=dst, send_sem=send, recv_sem=recv, device_id=dev, device_id_type=MESH)


def greet(r, c, kinds=(), partners=True):
    barrier = pltpu.get_barrier_semaphore()
    all_cols = any(kind not in ("dp", "half", "spread") for kind in kinds)
    count = 0
    if partners:
        pl.semaphore_signal(barrier, inc=1, device_id={"rows": r ^ 1}, device_id_type=MESH)
        pl.semaphore_signal(barrier, inc=1, device_id={"rows": r ^ 2}, device_id_type=MESH)
        count = 2
    if all_cols:
        for s in range(1, NC):
            pl.semaphore_signal(barrier, inc=1, device_id={"cols": lax.rem(c + s, NC)}, device_id_type=MESH)
        count += NC - 1
    elif partners:
        @pl.when(c > 0)
        def _():
            pl.semaphore_signal(barrier, inc=1, device_id={"cols": c - 1}, device_id_type=MESH)

        @pl.when(c < NC - 1)
        def _():
            pl.semaphore_signal(barrier, inc=1, device_id={"cols": c + 1}, device_id_type=MESH)
        count = count + jnp.where(c > 0, 1, 0) + jnp.where(c < NC - 1, 1, 0)
    if any(kind in ("dp", "swap2", "half", "spread", "reduce") for kind in kinds):
        groups = lax.axis_size("dp")
        for s in range(1, groups):
            pl.semaphore_signal(barrier, inc=1, device_id={"dp": lax.rem(lax.axis_index("dp") + s, groups)}, device_id_type=MESH)
        count = count + groups - 1
    pl.semaphore_wait(barrier, count)


class Riders:
    def __init__(self, kinds, ins, outs, send, recv, loc, *held):
        r, c, g = lax.axis_index("rows"), lax.axis_index("cols"), lax.axis_index("dp")
        groups = lax.axis_size("dp")
        self.remote, self.local, self.late, self.sums = [], [], [], []
        held = iter(held)
        for e, kind in enumerate(kinds):
            src, dst = ins[e], outs[e]
            if kind == "half":
                self.remote.append(copy_to(src.at[:, 1 - g], dst, send.at[e, 0], recv.at[e, 0], {"dp": 1 - g}))
                continue
            if kind == "spread":
                place = dst.at[:, g] if groups == 2 else dst
                self.local.append(pltpu.make_async_copy(src, place, loc.at[e]))
                if groups == 2:
                    self.remote.append(copy_to(src, place, send.at[e, 0], recv.at[e, 0], {"dp": 1 - g}))
                continue
            if kind == "swaph":
                few = src.shape[0] != NC
                piece = lambda to, few=few, src=src: src.at[to >> 1 if few else to, g]
                for s in range(1, NC):
                    to = lax.rem(c + s, NC)
                    self.remote.append(copy_to(piece(to), dst.at[c], send.at[e, s - 1], recv.at[e, s - 1], {"cols": to}))
                self.local.append(pltpu.make_async_copy(piece(c), dst.at[c], loc.at[e]))
                continue
            if kind == "dp":
                for s in range(1, groups):
                    self.remote.append(copy_to(src, dst.at[s - 1], send.at[e, s - 1], recv.at[e, s - 1], {"dp": lax.rem(g + s, groups)}))
                continue
            if kind == "swap":
                for s in range(1, NC):
                    to = lax.rem(c + s, NC)
                    self.remote.append(copy_to(src.at[to], dst.at[c], send.at[e, s - 1], recv.at[e, s - 1], {"cols": to}))
                self.local.append(pltpu.make_async_copy(src.at[c], dst.at[c], loc.at[e]))
                continue
            half = r & 1 if kind == "bcast2" else g
            other = {"rows": r ^ 1} if kind == "bcast2" else {"dp": 1 - g}
            pairs = []
            if kind == "reduce":
                own, got = next(held), next(held)
                first = copy_to(src.at[:, 1 - g], got, send.at[e, 2 * NC - 1], recv.at[e, 2 * NC - 1], other)
                self.sums.append((first, pltpu.make_async_copy(src.at[:, g], own, loc.at[e]), own, got, pairs))
                piece = lambda to, own=own: own.at[to]
                keep = pltpu.make_async_copy(own.at[c], dst.at[c, g], loc.at[e])
                pairs.append((None, keep, copy_to(own.at[c], dst.at[c, g], send.at[e, NC - 1], recv.at[e, NC - 1], other)))
            elif kind == "swap2":
                few = src.shape[0] != NC
                piece = lambda to, few=few, src=src, half=half: src.at[to >> 1 if few else to, half]
                self.local.append(pltpu.make_async_copy(src.at[c >> 1 if few else c], dst.at[c], loc.at[e]))
            else:
                piece = lambda to, src=src, half=half: src.at[half]
                self.local.append(pltpu.make_async_copy(src, dst.at[c], loc.at[e]))
            for s in range(1, NC):
                to, came = lax.rem(c + s, NC), lax.rem(c + NC - s, NC)
                first = copy_to(piece(to), dst.at[c, half], send.at[e, s - 1], recv.at[e, s - 1], {"cols": to})
                pairs.append((first, None, copy_to(dst.at[came, half], dst.at[came, half], send.at[e, NC + s - 1], recv.at[e, NC + s - 1], other)))
            if kind != "reduce":
                self.late.extend(pairs)

    def start(self):
        for first, keep, own, got, pairs in self.sums:
            first.start()
            keep.start()
        for first, _, _ in self.late:
            first.start()
        for one in self.remote + self.local:
            one.start()

    def add(self):
        for first, keep, own, got, pairs in self.sums:
            keep.wait()
            first.wait()
            own[...] = (own[...].astype(F32) + got[...].astype(F32)).astype(BF)
            for one, local, second in pairs:
                if one is None:
                    local.start()
                    second.start()
                else:
                    one.start()

    def relay(self):
        for first, _, second in self.late + [p for one in self.sums for p in one[4] if p[0] is not None]:
            first.wait_recv()
            second.start()

    def finish(self):
        for one in self.remote + self.local:
            one.wait()
        for first, local, second in self.late + [p for one in self.sums for p in one[4]]:
            if first is None:
                local.wait()
            else:
                first.wait_send()
            second.wait()


def rider_parts(kinds, arrays):
    groups = lax.axis_size("dp")
    shapes = []
    for kind, a in zip(kinds, arrays):
        if kind == "swap2":
            a = jax.ShapeDtypeStruct((NC,) + a.shape[1:], a.dtype)
        if kind in ("half", "swaph"):
            a = jax.ShapeDtypeStruct((NC,) + a.shape[2:], a.dtype)
        if kind == "spread":
            a = jax.ShapeDtypeStruct((NC,) + (2,) * (groups == 2) + a.shape[1:], a.dtype)
        lead = {"swap": (), "swap2": (), "half": (), "swaph": (), "spread": (), "reduce": (), "bcast2": (NC,), "dp": (groups - 1,)}[kind]
        shapes.append(jax.ShapeDtypeStruct(lead + a.shape, a.dtype))
    n, most = len(kinds), max(2 * NC, groups)
    sems = [pltpu.SemaphoreType.DMA((n, most)), pltpu.SemaphoreType.DMA((n, most)), pltpu.SemaphoreType.DMA((n,))] if n else []
    for kind, a in zip(kinds, arrays):
        if kind == "reduce":
            sems += [pltpu.VMEM(a.shape[:1] + a.shape[2:], a.dtype)] * 2
    return shapes, sems


SMALL = 96


def sum_groups(x_ref, others, held, dp_s, dp_r, n):
    g, groups = lax.axis_index("dp"), lax.axis_size("dp")
    copies = [copy_to(x_ref, others.at[s - 1], dp_s.at[s - 1], dp_r.at[s - 1], {"dp": lax.rem(g + s, groups)}) for s in range(1, groups)]
    for one in copies:
        one.start()

    def settle():
        total = x_ref[...]
        for s, one in enumerate(copies):
            one.wait()
            total = total + others[s]
        part = (lax.broadcasted_iota(jnp.int32, total.shape, 0) - SMALL) // n
        rest = total - total.astype(BF).astype(F32)
        rest2 = rest - rest.astype(BF).astype(F32)
        second, third = (part == 1) | (part == 4), (part == 2) | (part == 5)
        held[...] = jnp.where(second, rest, jnp.where(third, rest2, total)).astype(BF)
    return settle


def ridden(kernel, n_in, n_out, kinds):
    n = len(kinds)

    def run(*refs):
        ins, rest = refs[:n_in], refs[n_in + n:]
        outs, tail = rest[:n_out], rest[n_out + n:]
        riding = Riders(kinds, refs[n_in:n_in + n], rest[n_out:n_out + n], *tail[-3:])
        step = pl.program_id(0)

        @pl.when(step == 0)
        def _():
            greet(lax.axis_index("rows"), lax.axis_index("cols"), kinds, False)
            riding.start()
        kernel(*ins, *outs, *tail[:-3])

        @pl.when(step == pl.num_programs(0) - 1)
        def _():
            riding.finish()
    return run


def ridden_call(kernel, cid, grid, ins, in_specs, outs, out_specs, scratch, flops, kinds, arrays):
    shapes, sems = rider_parts(kinds, arrays)
    any_space = [pl.BlockSpec(memory_space=pl.ANY)] * len(kinds)
    return pl.pallas_call(
        ridden(kernel, len(ins), len(outs), tuple(kinds)),
        grid=(grid,),
        in_specs=list(in_specs) + any_space,
        out_specs=list(out_specs) + any_space,
        out_shape=[jax.ShapeDtypeStruct(*o) for o in outs] + shapes,
        scratch_shapes=list(scratch) + sems,
        compiler_params=pltpu.CompilerParams(collective_id=cid, has_side_effects=True, vmem_limit_bytes=56 << 20,
                                             dimension_semantics=("arbitrary",)),
        cost_estimate=pl.CostEstimate(flops=flops, bytes_accessed=24 << 20, transcendentals=4 << 20),
    )(*ins, *arrays)


HEAD_DIM = 64
STATE = 128
CONV = 4
SPAN = 256
HIGH = lax.Precision.HIGHEST
WIDE = 192
MIX = 2 * STATE + WIDE


def mm(a, b, ca=1, cb=0):
    return lax.dot_general(a.astype(BF), b.astype(BF), (((ca,), (cb,)), ((), ())), preferred_element_type=F32)


def exact(a, b, ca=1, cb=0):
    return lax.dot_general(a, b, (((ca,), (cb,)), ((), ())), preferred_element_type=F32, precision=HIGH)


def seg_at(place, l0, l1):
    return jnp.where(place < 0, -1, jnp.where(place >= l0, 1, 0) + jnp.where(place >= l0 + l1, 1, 0))


def sigmoid(x):
    return 1.0 / (1.0 + jnp.exp(-x))


def by_head(a, lane):
    return jnp.where(lane < HEAD_DIM, a[:, 0:1], jnp.where(lane < 2 * HEAD_DIM, a[:, 1:2], a[:, 2:3]))


def head_sums(a):
    i = lax.broadcasted_iota(jnp.int32, (WIDE, 128), 0)
    j = lax.broadcasted_iota(jnp.int32, (WIDE, 128), 1)
    return exact(a, jnp.where(i // HEAD_DIM == j, 1.0, 0.0).astype(F32))


class Block:
    def __init__(self, blk, lens, proj, before, cw, pv):
        self.l0, self.l1 = lens[0], lens[1]
        self.start = blk * SPAN
        v = proj[:, :MIX]
        self.place = self.start + lax.broadcasted_iota(jnp.int32, (SPAN, 1), 0)
        self.seg = seg_at(self.place, self.l0, self.l1)
        ext = jnp.concatenate([before[:, :MIX], v], axis=0)
        acc = cw[4:5] + cw[3:4] * v
        self.shifted = [v]
        for s in range(1, CONV):
            keep = jnp.where(seg_at(self.place - s, self.l0, self.l1) == self.seg, 1.0, 0.0)
            moved = ext[8 - s:8 - s + SPAN] * keep
            self.shifted.append(moved)
            acc = acc + cw[3 - s:4 - s] * moved
        self.acc = acc
        self.gate = sigmoid(acc)
        act = acc * self.gate
        self.b, self.c, self.x = act[:, :STATE], act[:, STATE:2 * STATE], act[:, 2 * STATE:]
        self.z = proj[:, MIX:MIX + WIDE]
        self.zs = sigmoid(self.z)
        self.raw = proj[:, MIX + WIDE:] + pv[2:3, :128]
        self.dt = jnp.maximum(self.raw, 0.0) + jnp.log1p(jnp.exp(-jnp.abs(self.raw)))
        self.rate = pv[3:4, :128] * self.dt
        i = lax.broadcasted_iota(jnp.int32, (SPAN, SPAN), 0)
        j = lax.broadcasted_iota(jnp.int32, (SPAN, SPAN), 1)
        self.low = jnp.where(j <= i, 1.0, 0.0).astype(F32)
        self.cum = exact(self.low, self.rate)
        self.cum_t = self.cum.T
        seg_row = seg_at(self.start + lax.broadcasted_iota(jnp.int32, (1, SPAN), 1), self.l0, self.l1)
        self.allowed = (j <= i) & (seg_row == self.seg)
        self.scores = mm(self.c, self.b, 1, 1)
        self.lane = lax.broadcasted_iota(jnp.int32, (SPAN, WIDE), 1)
        self.w = self.x * by_head(self.dt, self.lane)
        prior = seg_at(self.start - 1, self.l0, self.l1)
        last = seg_at(self.start + SPAN - 1, self.l0, self.l1)
        end = self.cum[SPAN - 1:SPAN]
        self.e = by_head(jnp.exp(self.cum), self.lane) * jnp.where(self.seg == prior, 1.0, 0.0)
        self.tail = by_head(jnp.exp(end - self.cum), self.lane) * jnp.where(self.seg == last, 1.0, 0.0)
        self.through = jnp.exp(end) * jnp.where(last == prior, 1.0, 0.0)
        row = lax.broadcasted_iota(jnp.int32, (WIDE, 1), 0)
        self.through_rows = jnp.where(row < HEAD_DIM, self.through[:, 0:1],
                                      jnp.where(row < 2 * HEAD_DIM, self.through[:, 1:2], self.through[:, 2:3]))

    def decay(self, h):
        return jnp.exp(jnp.where(self.allowed, self.cum[:, h:h + 1] - self.cum_t[h:h + 1, :], -1e30))

    def of_head(self, a, h):
        return jnp.where(self.lane // HEAD_DIM == h, a, 0.0)


def mixer_fwd_kernel(lens, hidden, gain, w_bc, w_xz, w_dt, cw, pv, u_out, proj_out, mixg, squares, y_out, states, state, before):
    blk = pl.program_id(0)

    @pl.when(blk == 0)
    def _():
        state[...] = jnp.zeros_like(state)
        before[...] = jnp.zeros_like(before)
    parts = [hidden[0, i].astype(F32) for i in range(NC)]
    feat = parts[0].shape[1]
    squares_in = sum(jnp.sum(p * p, axis=1, keepdims=True) for p in parts)
    scale = lax.rsqrt(squares_in / (NC * feat) + 1e-05)
    for i, p in enumerate(parts):
        at = slice(i * feat, (i + 1) * feat)
        u_out[:, at] = (p * scale * gain[:, at]).astype(BF)
    u = u_out[...]
    proj = jnp.concatenate([mm(u, w_bc[:, :2 * STATE]), mm(u, w_xz[...]), mm(u, w_dt[...])], axis=1)
    proj_out[...] = proj
    k = Block(blk, lens, proj, before[...], cw[...], pv[...])
    before[...] = proj[SPAN - 8:]
    s_in = state[...]
    states[0] = s_in
    y = mm(k.c, s_in, 1, 1) * k.e
    for h in range(3):
        y = y + mm(k.scores * k.decay(h), k.of_head(k.w, h))
    y = y + pv[1:2, :WIDE] * k.x
    state[...] = k.through_rows * s_in + mm(k.tail * k.w, k.b, 0, 0)
    y_out[...] = y
    gated = y * k.z * k.zs
    mixg[...] = (gated * pv[0:1, :WIDE]).astype(BF)
    squares[...] = jnp.broadcast_to(jnp.sum(gated * gated, axis=1, keepdims=True), squares.shape).astype(BF)


def mixer_bwd_kernel(lens, proj, before, cw, pv, y_ref, states, d_mix, extra, d_in, taps, rows, d_state, later):
    step = pl.program_id(0)
    blk = pl.num_programs(0) - 1 - step

    @pl.when(step == 0)
    def _():
        d_state[...] = jnp.zeros_like(d_state)
        later[...] = jnp.zeros_like(later)
        taps[...] = jnp.zeros_like(taps)
        rows[...] = jnp.zeros_like(rows)
    k = Block(blk, lens, proj[...], before[...], cw[...], pv[...])
    y, dm, s_in, ds = y_ref[...], d_mix[...], states[0], d_state[...]
    tilt = extra[:, 0:1].astype(F32) + extra[:, 64:65].astype(F32)
    silu_z = k.z * k.zs
    gated = y * silu_z
    d_gated = dm * pv[0:1, :WIDE] - gated * tilt
    d_z = d_gated * y * (k.zs * (1.0 + k.z * (1.0 - k.zs)))
    dy = d_gated * silu_z
    zeros = jnp.zeros((SPAN, 128), F32)
    lane = lax.broadcasted_iota(jnp.int32, (SPAN, 128), 1)
    top = lax.broadcasted_iota(jnp.int32, (128, SPAN), 0)
    d_cum, cols = zeros, jnp.zeros((128, SPAN), F32)
    d_scores = jnp.zeros((SPAN, SPAN), F32)
    dw = jnp.zeros((SPAN, WIDE), F32)
    for h in range(3):
        decay = k.decay(h)
        mixing = k.scores * decay
        dyh = k.of_head(dy, h).astype(BF)
        d_mixing = mm(dyh, k.w, 1, 1)
        d_scores = d_scores + d_mixing * decay
        moved = d_mixing * mixing
        d_cum = jnp.where(lane == h, jnp.sum(moved, axis=1, keepdims=True), d_cum)
        cols = jnp.where(top == h, jnp.sum(moved, axis=0, keepdims=True), cols)
        dw = dw + mm(mixing, dyh, 0, 0)
    e_dy, tail_w = k.e * dy, k.tail * k.w
    back = mm(k.b, ds, 1, 1)
    dw = dw + k.tail * back
    d_c = mm(d_scores, k.b) + mm(e_dy, s_in)
    d_b = mm(d_scores, k.c, 0, 0) + mm(tail_w, ds)
    through_state = mm(k.c, s_in, 1, 1) * k.e
    left = head_sums(tail_w * back)
    d_cum = d_cum - cols.T + head_sums(dy * through_state) - left
    own = jnp.sum(ds * s_in, axis=1, keepdims=True)
    of_row = lax.broadcasted_iota(jnp.int32, (WIDE, 128), 0) // HEAD_DIM
    own = jnp.sum(jnp.where(of_row == lax.broadcasted_iota(jnp.int32, (WIDE, 128), 1), own, 0.0), axis=0, keepdims=True)
    at_end = jnp.sum(left, axis=0, keepdims=True) + k.through * own
    is_last = lax.broadcasted_iota(jnp.int32, (SPAN, 128), 0) == SPAN - 1
    d_cum = d_cum + jnp.where(is_last, at_end, 0.0)
    d_rate = exact(k.low, d_cum, 0, 0)
    d_dt = head_sums(dw * k.x) + d_rate * pv[3:4, :128]
    d_raw = jnp.where(lane < 3, d_dt * sigmoid(k.raw), 0.0)
    d_x = dw * by_head(k.dt, k.lane) + pv[1:2, :WIDE] * dy
    d_pre = jnp.concatenate([d_b, d_c, d_x], axis=1) * (k.gate * (1.0 + k.acc * (1.0 - k.gate)))
    wide_rows = [jnp.sum(gated * dm, axis=0, keepdims=True), jnp.sum(dy * k.x, axis=0, keepdims=True)]
    thin_rows = [jnp.sum(d_raw, axis=0, keepdims=True), jnp.sum(d_rate * k.rate, axis=0, keepdims=True)]
    for i, one in enumerate(wide_rows):
        rows[i:i + 1, :WIDE] += one
    for i, one in enumerate(thin_rows):
        rows[2 + i:3 + i, :128] += one
    for s in range(CONV):
        taps[3 - s:4 - s] += jnp.sum(d_pre * k.shifted[s], axis=0, keepdims=True)
    taps[4:5] += jnp.sum(d_pre, axis=0, keepdims=True)
    ext = jnp.concatenate([d_pre, later[...]], axis=0)
    place = k.start + lax.broadcasted_iota(jnp.int32, (SPAN + 8, 1), 0)
    seg = seg_at(place, k.l0, k.l1)
    d_v = cw[3:4] * d_pre
    for s in range(1, CONV):
        keep = jnp.where(seg_at(place - s, k.l0, k.l1) == seg, 1.0, 0.0)
        d_v = d_v + cw[3 - s:4 - s] * (ext * keep)[s:s + SPAN]
    later[...] = d_pre[:8]
    d_in[...] = jnp.concatenate([d_v, d_z, d_raw], axis=1).astype(BF)
    d_state[...] = k.through_rows * ds + mm(e_dy, k.c, 0, 0)


def mixer_specs(n, order):
    block = lambda width: pl.BlockSpec((SPAN, width), lambda i: (order(i), 0))
    whole = lambda shape: pl.BlockSpec(shape, lambda i: (0, 0))
    before = pl.BlockSpec((8, MIX + WIDE + 128), lambda i: (jnp.maximum(order(i) * (SPAN // 8) - 1, 0), 0))
    return block, whole, [pl.BlockSpec(memory_space=pltpu.SMEM), block(MIX + WIDE + 128), before, whole((8, MIX)), whole((8, 256))]


def mixer_fwd(cid, lens, hidden, gain, w_bc, w_xz, w_dt, cw, pv, kinds, arrays):
    _, _, tok, feat = hidden.shape
    T, D = hidden.shape[0] * tok, NC * feat
    n, per = T // SPAN, tok // SPAN
    block, whole, _ = mixer_specs(n, lambda i: i)
    cols = MIX + WIDE + 128
    return ridden_call(
        mixer_fwd_kernel, cid, n, (lens, hidden, gain, w_bc, w_xz, w_dt, cw, pv),
        [pl.BlockSpec(memory_space=pltpu.SMEM), pl.BlockSpec((1, NC, SPAN, feat), lambda i: (i // per, 0, i % per, 0)),
         whole((1, D)), whole(w_bc.shape), whole(w_xz.shape), whole(w_dt.shape), whole((8, MIX)), whole((8, 256))],
        [((T, D), BF), ((T, cols), F32), ((T, WIDE), BF), ((T, 128), BF), ((T, WIDE), F32), ((n, WIDE, STATE), F32)],
        [block(D), block(cols), block(WIDE), block(128), block(WIDE), pl.BlockSpec((1, WIDE, STATE), lambda i: (i, 0, 0))],
        [pltpu.VMEM((WIDE, STATE), F32), pltpu.VMEM((8, cols), F32)], 8 << 30, kinds, arrays)


def mixer_bwd(cid, lens, proj, cw, pv, y, states, d_mix, g1_ext, kinds, arrays):
    T = proj.shape[0]
    n = T // SPAN
    order = lambda i: n - 1 - i
    block, whole, first = mixer_specs(n, order)
    at = g1_ext.shape[1] // 128 - 1
    return ridden_call(
        mixer_bwd_kernel, cid, n, (lens, proj, proj, cw, pv, y, states, d_mix, g1_ext),
        first + [block(WIDE), pl.BlockSpec((1, WIDE, STATE), lambda i: (order(i), 0, 0)), block(WIDE),
                 pl.BlockSpec((SPAN, 128), lambda i: (order(i), at))],
        [((T, MIX + WIDE + 128), BF), ((8, MIX), F32), ((8, 256), F32)],
        [block(MIX + WIDE + 128), whole((8, MIX)), whole((8, 256))],
        [pltpu.VMEM((WIDE, STATE), F32), pltpu.VMEM((8, MIX), F32)], 12 << 30, kinds, arrays)


AHEAD_DIM = 64
SCALE = AHEAD_DIM ** (-0.5)
LOW = -1e30


def att_allowed(lens, i, j, n, flip):
    a, b = lax.broadcasted_iota(jnp.int32, (n, 1), 0), lax.broadcasted_iota(jnp.int32, (1, n), 1)
    qp, kp = (i * n + b, j * n + a) if flip else (i * n + a, j * n + b)
    return (kp <= qp) & (seg_at(kp, lens[0], lens[1]) == seg_at(qp, lens[0], lens[1]))


def att_fwd_kernel(lens, qkv, attended, o_ref, lse):
    i = pl.program_id(0)
    n = o_ref.shape[0]
    lane = lax.broadcasted_iota(jnp.int32, (n, WIDE), 1)
    thin = lax.broadcasted_iota(jnp.int32, (n, 128), 1)
    mine = jnp.where((i == 0) | (i == 3), 0, 1) == lax.rem(lax.axis_index("cols"), 2)

    @pl.when(jnp.logical_not(mine))
    def _():
        attended[...] = jnp.zeros_like(attended)
        o_ref[...] = jnp.zeros_like(o_ref)
        lse[...] = jnp.zeros_like(lse)

    @pl.when(mine)
    def _():
        q = qkv[pl.ds(i * n, n), :WIDE] * jnp.asarray(SCALE, BF)
        heads = [jnp.where(lane // AHEAD_DIM == h, q, jnp.zeros_like(q)) for h in range(3)]

        def body(j, carry):
            tops, sums, acc = carry
            k, v = qkv[pl.ds(j * n, n), WIDE:2 * WIDE], qkv[pl.ds(j * n, n), 2 * WIDE:]
            allowed = att_allowed(lens, i, j, n, False)
            new_tops, new_sums = [], []
            for h in range(3):
                s = jnp.where(allowed, mm(heads[h], k, 1, 1), LOW)
                top = jnp.maximum(tops[h], jnp.max(s, axis=1, keepdims=True))
                p = jnp.exp(s - top)
                fade = jnp.exp(tops[h] - top)
                new_tops.append(top)
                new_sums.append(sums[h] * fade + jnp.sum(p, axis=1, keepdims=True))
                acc = jnp.where(lane // AHEAD_DIM == h, acc * fade + mm(p, v), acc)
            return tuple(new_tops), tuple(new_sums), acc

        zero = jnp.zeros((n, 1), F32)
        start = (tuple(zero + LOW for _ in range(3)), (zero,) * 3, jnp.zeros((n, WIDE), F32))
        tops, sums, acc = lax.fori_loop(0, i + 1, body, start)
        pick = lambda a: jnp.where(lane < AHEAD_DIM, a[0], jnp.where(lane < 2 * AHEAD_DIM, a[1], a[2]))
        out = acc / pick(sums)
        o_ref[...] = out
        attended[...] = out.astype(BF)
        logs = [t + jnp.log(s) for t, s in zip(tops, sums)]
        lse[...] = jnp.where(thin == 0, logs[0], jnp.where(thin == 1, logs[1], logs[2]))


def att_bwd_kernel(lens, qkv, d_att, o_ref, lse, d_qkv, dk, dv):
    i = pl.program_id(0)
    n = lse.shape[0]
    lane = lax.broadcasted_iota(jnp.int32, (n, WIDE), 1)
    mine = jnp.where((i == 0) | (i == 3), 0, 1) == lax.rem(lax.axis_index("cols"), 2)

    @pl.when(i == 0)
    def _():
        dk[...] = jnp.zeros_like(dk)
        dv[...] = jnp.zeros_like(dv)

    @pl.when(jnp.logical_not(mine))
    def _():
        d_qkv[pl.ds(i * n, n), :WIDE] = jnp.zeros((n, WIDE), BF)

    @pl.when(mine)
    def _():
        q = qkv[pl.ds(i * n, n), :WIDE]
        do = d_att[...]
        delta = head_sums(o_ref[...] * do.astype(F32)).T
        logs = lse[...].T
        none = jnp.zeros_like(q)
        qs = [jnp.where(lane // AHEAD_DIM == h, q, none) for h in range(3)]
        dos = [jnp.where(lane // AHEAD_DIM == h, do, none) for h in range(3)]

        def body(j, dq):
            at = pl.ds(j * n, n)
            k, v = qkv[at, WIDE:2 * WIDE], qkv[at, 2 * WIDE:]
            allowed = att_allowed(lens, i, j, n, True)
            for h in range(3):
                s = mm(k, qs[h], 1, 1) * SCALE
                p = jnp.exp(jnp.where(allowed, s, LOW) - logs[h:h + 1])
                ds = (p * (mm(v, dos[h], 1, 1) - delta[h:h + 1]) * SCALE).astype(BF)
                dv[at, :] += mm(p, dos[h])
                dk[at, :] += mm(ds, qs[h])
                dq = jnp.where(lane // AHEAD_DIM == h, dq + mm(ds, k, 0, 0), dq)
            return dq

        dq = lax.fori_loop(0, i + 1, body, jnp.zeros((n, WIDE), F32))
        d_qkv[pl.ds(i * n, n), :WIDE] = dq.astype(BF)

    @pl.when(i == pl.num_programs(0) - 1)
    def _():
        d_qkv[:, WIDE:2 * WIDE] = dk[...].astype(BF)
        d_qkv[:, 2 * WIDE:] = dv[...].astype(BF)


def att_call(kernel, cid, lens, qkv, blocked, outs, out_specs, scratch, kinds, arrays):
    T = qkv.shape[0]
    specs = [pl.BlockSpec(memory_space=pltpu.SMEM), pl.BlockSpec((T, 3 * WIDE), lambda i: (0, 0))]
    specs += [pl.BlockSpec((T // 4, a.shape[1]), lambda i: (i, 0)) for a in blocked]
    return ridden_call(kernel, cid, 4, (lens, qkv) + blocked, specs, outs, out_specs, scratch, 8 << 30, kinds, arrays)


def att_fwd(cid, lens, qkv, kinds, arrays):
    T = qkv.shape[0]
    block = lambda w: pl.BlockSpec((T // 4, w), lambda i: (i, 0))
    return att_call(att_fwd_kernel, cid, lens, qkv, (), [((T, WIDE), BF), ((T, WIDE), F32), ((T, 128), F32)],
                    [block(WIDE), block(WIDE), block(128)], [], kinds, arrays)


def att_bwd(cid, lens, qkv, d_att, o, lse, kinds, arrays):
    T = qkv.shape[0]
    return att_call(att_bwd_kernel, cid, lens, qkv, (d_att, o, lse), [((T, 3 * WIDE), BF)],
                    [pl.BlockSpec((T, 3 * WIDE), lambda i: (0, 0))], [pltpu.VMEM((T, WIDE), F32), pltpu.VMEM((T, WIDE), F32)], kinds, arrays)


VMEM, ANY = pltpu.VMEM, pl.ANY


HALVES = 2


class Sum:
    def __init__(self, r, c, partial, bufs):
        self.r, self.c, self.partial = r, c, partial
        self.yy, self.kk = r >> 1, r & 1
        (self.part, self.p_out, self.k_buf, self.y_out, self.y_buf, self.z_out, self.r_buf, self.l_buf,
         self.k_s, self.k_r, self.y_s, self.y_r, self.zr_s, self.zr_r, self.zl_s, self.zl_r) = bufs
        self.cut = self.part.shape[1] // HALVES

    @staticmethod
    def scratch(S, W):
        buf, sem = (lambda *n: VMEM(n + (S, W), BF)), (lambda n: pltpu.SemaphoreType.DMA((n,)))
        return [VMEM((NC, S, W), F32), buf(2, NC), buf(2, NC)] + [buf(NC)] * 5 + [sem(2 * NC), sem(2 * NC)] + [sem(HALVES * NC)] * 6

    def k_copy(self, y, cc):
        i = y * NC + cc
        return copy_to(self.p_out.at[y, cc], self.k_buf.at[y, cc], self.k_s.at[i], self.k_r.at[i], {"rows": self.r ^ 1})

    def piece(self, src, dst, send, recv, cc, h, to):
        at, i = pl.ds(h * self.cut, self.cut), cc * HALVES + h
        return copy_to(src.at[cc, at], dst.at[cc, at], send.at[i], recv.at[i], to)

    def y_copy(self, cc, h):
        return self.piece(self.y_out, self.y_buf, self.y_s, self.y_r, cc, h, {"rows": self.r ^ 2})

    def r_copy(self, cc, h):
        return self.piece(self.z_out, self.r_buf, self.zr_s, self.zr_r, cc, h, {"cols": self.c + 1})

    def l_copy(self, cc, h):
        return self.piece(self.z_out, self.l_buf, self.zl_s, self.zl_r, cc, h, {"cols": self.c - 1})

    def nth(self, j):
        return jnp.where(self.c < NC // 2, NC - 1 - j, j)

    def each(self, f):
        def body(j, carry):
            f(self.nth(j))
            return carry
        lax.fori_loop(0, NC, body, 0)

    def to_core(self):
        def half(i, carry):
            y = jnp.where(i == 0, 1 - self.yy, self.yy)

            def one(cc):
                self.p_out[y, cc] = self.partial(y * 2 + (1 - self.kk), cc).astype(BF)
                self.k_copy(y, cc).start()
            self.each(one)
            return carry
        lax.fori_loop(0, 2, half, 0)

    def to_y(self):
        def one(cc):
            mine = self.partial((1 - self.yy) * 2 + self.kk, cc)
            self.k_copy(1 - self.yy, cc).wait_recv()
            self.y_out[cc] = (mine + self.k_buf[1 - self.yy, cc].astype(F32)).astype(BF)
            self.y_copy(cc, 0).start()
        self.each(one)
        for h in range(1, HALVES):
            self.each(lambda cc: self.y_copy(cc, h).start())

    def own(self):
        def one(cc):
            mine = self.partial(self.r, cc)
            self.k_copy(self.yy, cc).wait_recv()
            self.part[cc] = mine + self.k_buf[self.yy, cc].astype(F32)
        self.each(one)

    def step(self, j, h):
        c, cc = self.c, self.nth(j)
        at = pl.ds(h * self.cut, self.cut)
        self.y_copy(cc, h).wait_recv()
        self.part[cc, at] += self.y_buf[cc, at].astype(F32)

        @pl.when(cc > c)
        def _():
            @pl.when(c > 0)
            def _():
                self.r_copy(cc, h).wait_recv()
                self.part[cc, at] += self.r_buf[cc, at].astype(F32)
            self.z_out[cc, at] = self.part[cc, at].astype(BF)
            self.r_copy(cc, h).start()

        @pl.when(cc < c)
        def _():
            @pl.when(c < NC - 1)
            def _():
                self.l_copy(cc, h).wait_recv()
                self.part[cc, at] += self.l_buf[cc, at].astype(F32)
            self.z_out[cc, at] = self.part[cc, at].astype(BF)
            self.l_copy(cc, h).start()

    def last(self, total, h):
        c, at = self.c, pl.ds(h * self.cut, self.cut)
        total[at] = self.part[c, at]

        @pl.when(c > 0)
        def _():
            self.r_copy(c, h).wait_recv()
            total[at] += self.r_buf[c, at].astype(F32)

        @pl.when(c < NC - 1)
        def _():
            self.l_copy(c, h).wait_recv()
            total[at] += self.l_buf[c, at].astype(F32)

    def finish(self):
        def one(cc):
            self.k_copy(0, cc).wait_send()
            self.k_copy(1, cc).wait_send()
            for h in range(HALVES):
                self.y_copy(cc, h).wait_send()

                @pl.when(cc > self.c)
                def _():
                    self.r_copy(cc, h).wait_send()

                @pl.when(cc < self.c)
                def _():
                    self.l_copy(cc, h).wait_send()
        self.each(one)


class Gather:
    def __init__(self, r, c, out, S, sems, use=None):
        self.r, self.c, self.out, self.S, self.use = r, c, out, S, use
        self.recv, self.zr_s, self.zl_s, self.y_s, self.k_s = sems

    @staticmethod
    def scratch():
        return [pltpu.SemaphoreType.DMA((HALVES * n,)) for n in (4 * NC, NC, NC, NC, 2 * NC)]

    def slab(self, rr, cc):
        return self.out.at[pl.ds(pl.multiple_of((rr * NC + cc) * self.S, 16), self.S)]

    def move(self, rr, cc, h, sem, to):
        cut = self.S // HALVES
        ref = self.out.at[pl.ds(pl.multiple_of((rr * NC + cc) * self.S + h * cut, 16), cut)]
        return copy_to(ref, ref, sem, self.recv.at[(rr * NC + cc) * HALVES + h], to)

    def right(self, cc, h):
        return self.move(self.r, cc, h, self.zr_s.at[cc * HALVES + h], {"cols": self.c + 1})

    def left(self, cc, h):
        return self.move(self.r, cc, h, self.zl_s.at[cc * HALVES + h], {"cols": self.c - 1})

    def y_copy(self, cc, h):
        return self.move(self.r, cc, h, self.y_s.at[cc * HALVES + h], {"rows": self.r ^ 2})

    def k_copy(self, rr, cc, h):
        return self.move(rr, cc, h, self.k_s.at[((rr >> 1) * NC + cc) * HALVES + h], {"rows": self.r ^ 1})

    def got(self, rr, cc, h):
        self.k_copy(rr, cc, h).wait_recv()

    def pass_on(self, cc, h):
        c = self.c

        @pl.when((cc <= c) & (c < NC - 1))
        def _():
            self.right(cc, h).start()

        @pl.when((cc >= c) & (c > 0))
        def _():
            self.left(cc, h).start()
        self.y_copy(cc, h).start()
        self.k_copy(self.r, cc, h).start()

    def begin(self):
        for h in range(HALVES):
            self.pass_on(self.c, h)

    def sides(self, off, f):
        for s in (-1, 1):
            cc = self.c + s * off
            fits = (cc >= 0) & (cc < NC) & (off < NC)
            if s == 1:
                fits = fits & (off > 0)

            @pl.when(fits)
            def _():
                f(cc)

    def forward(self, d, halves=range(HALVES)):
        for h in halves:
            def along(cc):
                self.got(self.r, cc, h)
                self.pass_on(cc, h)

            def across(cc):
                self.got(self.r ^ 2, cc, h)
                self.k_copy(self.r ^ 2, cc, h).start()
            self.sides(d, along)
            self.sides(d - 1, across)

    def uses(self, d):
        def one(i, carry):
            kind, s = i >> 1, (i & 1) * 2 - 1
            off = d - jnp.where(kind == 0, 0, jnp.where(kind == 3, 2, 1))
            rr = self.r ^ jnp.where(kind == 0, 0, jnp.where(kind == 1, 2, jnp.where(kind == 2, 1, 3)))
            cc = self.c + s * off
            fits = (off >= 0) & (off < NC) & (cc >= 0) & (cc < NC) & ((s < 0) | (off > 0))

            @pl.when(fits)
            def _():
                @pl.when(kind >= 2)
                def _():
                    for h in range(HALVES):
                        self.got(rr, cc, h)
                if self.use is not None:
                    self.use(rr, cc)
            return carry
        lax.fori_loop(0, 8, one, 0)

    def finish(self):
        def body(cc, carry):
            for h in range(HALVES):
                self.y_copy(cc, h).wait_send()
                self.k_copy(self.r, cc, h).wait_send()
                self.k_copy(self.r ^ 2, cc, h).wait_send()

                @pl.when((cc <= self.c) & (self.c < NC - 1))
                def _():
                    self.right(cc, h).wait_send()

                @pl.when((cc >= self.c) & (self.c > 0))
                def _():
                    self.left(cc, h).wait_send()
            return carry
        lax.fori_loop(0, NC, body, 0)


def link_call(kernel, cid, ins, in_spaces, outs, out_spaces, scratch, flops):
    return pl.pallas_call(
        kernel,
        out_shape=[jax.ShapeDtypeStruct(s, d) for s, d in outs],
        in_specs=[pl.BlockSpec(memory_space=s) for s in in_spaces],
        out_specs=[pl.BlockSpec(memory_space=s) for s in out_spaces],
        scratch_shapes=scratch,
        compiler_params=pltpu.CompilerParams(collective_id=cid, has_side_effects=True, vmem_limit_bytes=62 << 20),
        cost_estimate=pl.CostEstimate(flops=flops, bytes_accessed=96 << 20, transcendentals=0),
    )(*ins)


def entry_kernel(kinds, *refs):
    n = len(kinds)
    it = iter(refs)
    take = lambda k: [next(it) for _ in range(k)]
    hidden, grad = take(2)
    ins = take(n)
    hid_all, g_all, h0 = take(3)
    outs = take(n)
    got, = take(1)
    hid_sems, g_sems, swap_sems, sems = take(5), take(5), take(3), take(3)
    r, c = lax.axis_index("rows"), lax.axis_index("cols")
    greet(r, c, kinds)
    big, S = hidden.shape[0], got.shape[1]
    feat = hidden.shape[1]
    first = Gather(r, c, hid_all, big, hid_sems)
    second = Gather(r, c, g_all, S, g_sems)
    swap = Riders(("swap",), (grad,), (got,), *swap_sems)
    riding = Riders(kinds, ins, outs, *sems)
    hid_all[pl.ds(pl.multiple_of((r * NC + c) * big, 16), big), :] = hidden[...]
    first.begin()
    riding.start()
    swap.start()
    for d in range(1, NC):
        first.forward(d)
        first.uses(d)
        if d == 1:
            swap.finish()
            for i in range(NC):
                g_all[pl.ds(pl.multiple_of((r * NC + c) * S, 16), S), i * feat:(i + 1) * feat] = got[i]
            second.begin()
        if d == 2:
            riding.relay()
            second.forward(1)
            second.uses(1)
    for i in range(NC):
        h0[:, i * feat:(i + 1) * feat] = hid_all[pl.ds(pl.multiple_of((r * NC + i) * big + c * S, 16), S), :]
    for d in range(NC, NC + 2):
        first.forward(d)
        first.uses(d)
        second.forward(d - 2)
        second.uses(d - 2)
    for d in range(NC, NC + 2):
        second.forward(d)
        second.uses(d)
    first.finish()
    second.finish()
    riding.finish()


def entry(cid, hidden, grad, kinds, arrays):
    big, feat = hidden.shape
    S, D = big // NC, feat * NC
    shapes, sems = rider_parts(kinds, arrays)
    _, swap_sems = rider_parts(("swap",), (grad,))
    outs = [((4 * NC * big, feat), BF), ((4 * NC * S, D), BF), ((S, D), BF)] + [(s.shape, s.dtype) for s in shapes]
    scratch = [VMEM(grad.shape, BF)] + Gather.scratch() + Gather.scratch() + swap_sems + sems
    return link_call(functools.partial(entry_kernel, tuple(kinds)), cid, [hidden, grad] + list(arrays), [VMEM] + [ANY] * (1 + len(kinds)),
                     outs, [VMEM] * 3 + [ANY] * len(kinds), scratch, 1 << 20)


def link_kernel(spec, *refs):
    it = iter(refs)
    take = lambda n: [next(it) for _ in range(n)]
    maybe = lambda key, n=1: take(n) if spec[key] else [None] * n
    a, w1 = take(2)
    side, = maybe("side")
    mid_in = take(spec["n_mid"])
    w2, = take(1) if spec["w2"] in ("in", "in_t") else [None]
    a2, v2 = maybe("more_sum", 2)
    after_in = take(spec["n_after"])
    early_in = take(len(spec["early"]))
    late_in = take(sum(src is None for _, src in spec["late"]))
    u_all = next(it)
    mid_out = take(spec["n_mid_out"])
    post_out = take(spec["n_post"])
    after_out = take(spec["n_after_out"])
    early_out, late_out = take(len(spec["early"])), take(len(spec["late"]))
    final_out = take(len(after_out))
    total, = take(1)
    sum_bufs, gather_sems = take(16), take(5)
    sum2_bufs = take(17) if spec["more_sum"] else []
    small = take(6) if spec["small"] else None
    early_sems, late_sems, final_sems = take(spec["n_early_sems"]), take(spec["n_late_sems"]), take(3 * (len(after_out) > 0))
    r, c = lax.axis_index("rows"), lax.axis_index("cols")
    S, W = total.shape
    D = w1.shape[0] if spec["w1_t"] else w1.shape[1]
    late_kinds = tuple(kind for kind, _ in spec["late"])
    greet(r, c, spec["early"] + late_kinds + (("dp",) if spec["small"] else ()))
    none = [None] * 3
    early = Riders(spec["early"], early_in, early_out, *(early_sems or none))
    late_in = iter(late_in)
    sources = [next(late_in) if src is None else mid_out[src] for _, src in spec["late"]]
    late = Riders(late_kinds, sources, late_out, *(late_sems or none))
    final = Riders(("swap",) * len(after_out), after_out, final_out, *(final_sems or none))
    rows_of = lambda rr, cc: pl.ds(pl.multiple_of((rr * NC + cc) * S, 16), S)

    def partial(rr, cc):
        p = mm(a[rows_of(rr, cc), :], w1[...], 1, 1 if spec["w1_t"] else 0)
        return p if side is None else jnp.concatenate([p, side[rows_of(rr, cc), :].astype(F32)], axis=1)

    def use(rr, cc):
        w = early_out[0][...].reshape(D, -1) if spec["w2"] == "rider" else w2[...]
        u = u_all[rows_of(rr, cc), :D] if u_all.shape[1] > D else u_all[rows_of(rr, cc), :]
        spec["post"](mm(u, w, 1, 1 if spec["w2"] == "in_t" else 0), rows_of(rr, cc), post_out)

    summing = Sum(r, c, partial, sum_bufs)
    gather = Gather(r, c, u_all, S, gather_sems, use if spec["w2"] else None)
    summing2 = None
    summing.to_core()
    early.start()
    summing.to_y()
    if spec["more_sum"]:
        summing2 = Sum(r, c, lambda rr, cc: mm(a2[rows_of(rr, cc), :], v2[...]), sum2_bufs[:16])
    summing.own()
    for j in range(NC):
        summing.step(j, 0)
        if spec["small"] and j == 1:
            early.add()
        if summing2 and j == 1:
            summing2.to_core()
    summing.last(total, 0)
    if summing2:
        summing2.to_y()
        summing2.own()
    if spec["small"]:
        for j in range(NC):
            summing.step(j, 1)
        summing.last(total, 1)
        mine, others, held, dp_s, dp_r, loc = small
        spec["mid"](total, mid_in, mid_out, mine)
        settle = sum_groups(mine, others, held, dp_s, dp_r, 4)
        late.start()
        settle()
        place = pltpu.make_async_copy(held, gather.slab(r, c), loc)
        place.start()
        place.wait()
        gather.begin()
        early.relay()
    else:
        def advance(h):
            at = pl.ds(h * (S // HALVES), S // HALVES)
            off = pl.multiple_of((r * NC + c) * S + h * (S // HALVES), 16)
            u_all[pl.ds(off, S // HALVES), :] = spec["mid"](total, mid_in, mid_out, at, h)
            gather.pass_on(c, h)
        advance(0)
        early.add()
        summing.step(0, 1)
        summing.step(1, 1)
        gather.forward(1, (0,))
        summing.step(2, 1)
        summing.step(3, 1)
        summing.last(total, 1)
        advance(1)
        late.start()
    if spec["w2"] == "rider":
        early.relay()
        early.finish()
    if spec["w2"]:
        use(r, c)
    for d in range(1, NC + 2):
        if summing2 and d <= NC:
            summing2.step(d - 1, 0)
            summing2.step(d - 1, 1)
        if spec["small"]:
            gather.forward(d)
        else:
            gather.forward(d, (1,))
            gather.forward(d + 1, (0,))
        gather.uses(d)
        if d == 2 and spec["w2"] != "rider" and not spec["small"]:
            early.relay()
    gather.finish()
    summing.finish()
    if summing2:
        for h in range(HALVES):
            summing2.last(sum2_bufs[16], h)
        spec["after"](sum2_bufs[16], after_in, after_out)
        final.start()
        summing2.finish()
        final.finish()
    late.add()
    late.relay()
    if spec["w2"] != "rider":
        early.finish()
    late.finish()


def link(cid, a, w1, mid, mid_in, mid_out, *, w1_t=False, side=None, w2=None, w2_kind=None, post=None, post_out=(), early=(), early_in=(),
         late=(), late_in=(), extra=0, small=0, more_sum=None, after=None, after_in=(), after_out=()):
    T = a.shape[0]
    D = w1.shape[0] if w1_t else w1.shape[1]
    S = T // (4 * NC)
    W = D + (0 if side is None else side.shape[1])
    width = small or D + extra
    early_shapes, early_sems = rider_parts(early, early_in)
    late_it = iter(late_in)
    late_arrays = [next(late_it) if src is None else jax.ShapeDtypeStruct(*mid_out[src]) for _, src in late]
    late_shapes, late_sems = rider_parts(tuple(k for k, _ in late), late_arrays)
    final_shapes, final_sems = rider_parts(("swap",) * len(after_out), [jax.ShapeDtypeStruct(*o) for o in after_out])
    spec = dict(w1_t=w1_t, side=side is not None, mid=mid, n_mid=len(mid_in), n_mid_out=len(mid_out), w2=w2_kind, post=post,
                n_post=len(post_out), early=tuple(early), late=tuple(late), small=small, more_sum=more_sum is not None,
                after=after, n_after=len(after_in), n_after_out=len(after_out), n_early_sems=len(early_sems), n_late_sems=len(late_sems))
    ins = [a, w1] + ([side] if side is not None else []) + list(mid_in) + ([w2] if w2 is not None else [])
    ins += list(more_sum or ()) + list(after_in)
    riding = list(early_in) + list(late_in)
    in_spaces = [VMEM] * len(ins) + [ANY] * len(riding)
    ins += riding
    outs = [((T, width), BF)] + list(mid_out) + list(post_out)
    outs += list(after_out)
    out_spaces = [VMEM] * len(outs) + [ANY] * len(early_shapes + late_shapes + final_shapes)
    if w2_kind == "rider":
        out_spaces[len(outs)] = VMEM
    outs += [(s.shape, s.dtype) for s in early_shapes + late_shapes + final_shapes]
    scratch = [VMEM((S, W), F32)] + Sum.scratch(S, W) + Gather.scratch()
    if more_sum is not None:
        scratch += Sum.scratch(S, D) + [VMEM((S, D), F32)]
    if small:
        groups = lax.axis_size("dp")
        scratch += [VMEM((S, small), F32), VMEM((groups - 1, S, small), F32), VMEM((S, small), BF), pltpu.SemaphoreType.DMA((groups - 1,)),
                    pltpu.SemaphoreType.DMA((groups - 1,)), pltpu.SemaphoreType.DMA]
    scratch += early_sems + late_sems + final_sems
    return link_call(functools.partial(link_kernel, spec), cid, ins, in_spaces, outs, out_spaces, scratch, 8 << 30)


EPS = 1e-05


def norm_scale(x):
    return lax.rsqrt(jnp.mean(x * x, axis=1, keepdims=True) + EPS)


def norm_grad(x, gain, up, gain_grad, h):
    s = norm_scale(x)
    own = jnp.sum(x * s * up, axis=0, keepdims=True)
    gain_grad[0:1] = own if h == 0 else gain_grad[0:1] + own
    tilted = up * gain
    return s * tilted - x * (s * s * s * jnp.mean(x * tilted, axis=1, keepdims=True))


def mid_mixer(inner, total, ins, outs, at, h):
    h0, gain = ins
    h1, mix_out, gate_scale = outs
    D = h0.shape[1]
    s = lax.rsqrt(total[at, D:D + 1] / inner + EPS)
    out = total[at, :D] * s
    mix_out[at] = out
    gate_scale[at] = jnp.broadcast_to(s, (out.shape[0], gate_scale.shape[1]))
    x = h0[at].astype(F32) + out
    h1[at] = x
    return (x * norm_scale(x) * gain[...]).astype(BF)


def mid_attention(total, ins, outs, at, h):
    h1, gain = ins
    x = h1[at] + total[at]
    outs[0][at] = x
    return (x * norm_scale(x) * gain[...]).astype(BF)


def mid_ff_back(total, ins, outs, at, h):
    h2, gain, grad = ins
    dh2, gain_grad = outs
    d = grad[at].astype(F32) + norm_grad(h2[at], gain[...], total[at], gain_grad, h)
    dh2[at] = d
    return d.astype(BF)


def mid_att_back(inner, total, ins, outs, at, h):
    h1, gain, dh2, mix_out, gate_scale = ins
    dh1, gain_grad = outs
    d = dh2[at] + norm_grad(h1[at], gain[...], total[at], gain_grad, h)
    dh1[at] = d
    s = gate_scale[at, 0:1]
    tilt = s * s * jnp.sum(d * mix_out[at], axis=1, keepdims=True) / inner
    high = tilt.astype(BF).astype(F32)
    lane = lax.broadcasted_iota(jnp.int32, (d.shape[0], 128), 1)
    return jnp.concatenate([d * s, jnp.where(lane < 64, high, tilt - high)], axis=1).astype(BF)


def mid_mixer_back(total, ins, outs, small):
    h0, gain, dh1 = ins
    in_slab, gain_grad = outs
    D = h0.shape[1]
    thin = small.shape[1]
    four = D // thin
    d = dh1[...] + norm_grad(h0[...].astype(F32), gain[...], total[:, :D], gain_grad, 0)
    feat = D // NC
    for i in range(NC):
        in_slab[i] = d[:, i * feat:(i + 1) * feat].astype(BF)
    rest = total[:, D:]
    small[...] = jnp.zeros_like(small)
    small[:SMALL] = rest[:SMALL]
    own = rest[SMALL:SMALL + four] + rest[SMALL + four:SMALL + 2 * four]
    row = gain_grad[0:1]
    for i in range(3):
        small[SMALL + i * four:SMALL + (i + 1) * four] = own
        for j in range(four):
            at = SMALL + (3 + i) * four + j
            small[at:at + 1] = row[:, j * thin:(j + 1) * thin]


def after_output(total, ins, outs):
    h2, valid = ins
    x = (h2[...] + total[...]) * valid[:, 0:1]
    feat = x.shape[1] // NC
    for i in range(NC):
        outs[0][i] = x[:, i * feat:(i + 1) * feat].astype(BF)


def post_plain(p, at, outs):
    outs[0][at, :] = p.astype(outs[0].dtype)


def post_gelu(p, at, outs):
    outs[0][at, :] = p
    outs[1][at, :] = (0.5 * p * (1.0 + jnp.tanh(0.7978845608028654 * (p + 0.044715 * (p * p * p))))).astype(BF)


def finish_kernel(zx, mix, qkv, o, ff, rest, x_g, z_g, q_g, k_g, v_g, mix_g, o_g, up_g, down_g, bcdt_g, small, gain):
    i = pl.program_id(0)
    rows, part = zx.shape[2], ff.shape[2] // 2
    for h in range(2):
        at = slice(h * rows, (h + 1) * rows)
        piece = zx[0, h].astype(F32)
        x_new, z_new = piece[:, :WIDE], piece[:, WIDE:]
        three = qkv[0, h].astype(F32)
        for j in range(NC):
            @pl.when(i == j)
            def _():
                x_g[at, j * WIDE:(j + 1) * WIDE] = x_new
                z_g[at, j * WIDE:(j + 1) * WIDE] = z_new
                to = slice((j // 2) * WIDE, (j // 2 + 1) * WIDE)
                for n, out in enumerate((q_g, k_g, v_g)):
                    new = three[:, n * WIDE:(n + 1) * WIDE]
                    out[at, to] = new if j % 2 == 0 else out[at, to] + new
        half = mix.shape[2]
        mix_g[h * half:(h + 1) * half] = mix[0, h].astype(F32)
        o_at = slice(h * half, (h + 1) * half)

        @pl.when(i % 2 == 0)
        def _():
            o_g[o_at] = o[0, h].astype(F32)

        @pl.when(i % 2 == 1)
        def _():
            o_g[o_at] += o[0, h].astype(F32)
        down_g[h * part:(h + 1) * part] = ff[0, h, :part].astype(F32)
        up_g[h * part:(h + 1) * part] = ff[0, h, part:].astype(F32)
    wide = bcdt_g.shape[1]

    @pl.when(i == 0)
    def _():
        gain[...] = jnp.zeros_like(gain)
    for j in range(NC):
        slab = rest[j].astype(F32)
        bcdt_g[j * SMALL:(j + 1) * SMALL] = slab[:SMALL, :wide]
        tail = slab[SMALL:SMALL + 24]
        small[j] = tail[0:4] + tail[4:8] + tail[8:12]
        gain[0:4] += tail[12:16] + tail[16:20] + tail[20:24]


def finish(zx, mix, qkv, o, ff, rest, bcdt_width):
    thin, feat = rest.shape[2], zx.shape[3]
    D = NC * feat
    lead = lambda a: pl.BlockSpec((1,) + a.shape[1:], lambda i: (i, 0, 0, 0))
    whole = lambda r, w: pl.BlockSpec((r, w), lambda i: (0, 0))
    sds = lambda *s: jax.ShapeDtypeStruct(s, F32)
    rows, half, part = 2 * zx.shape[2], 2 * mix.shape[2], ff.shape[2]
    return pl.pallas_call(
        finish_kernel,
        grid=(NC,),
        in_specs=[lead(zx), lead(mix), lead(qkv), lead(o), lead(ff), pl.BlockSpec((NC,) + rest.shape[1:], lambda i: (i, 0, 0))],
        out_specs=[whole(rows, NC * WIDE)] * 2 + [whole(rows, 2 * WIDE)] * 3 + [
            pl.BlockSpec((half, feat), lambda i: (i, 0)), pl.BlockSpec((half, feat), lambda i: (i // 2, 0)),
            pl.BlockSpec((part, feat), lambda i: (0, i)), pl.BlockSpec((part, feat), lambda i: (i, 0)),
            pl.BlockSpec((NC * SMALL, bcdt_width), lambda i: (i, 0)), pl.BlockSpec((NC, 4, thin), lambda i: (i, 0, 0)), whole(8, thin)],
        out_shape=[sds(rows, NC * WIDE)] * 2 + [sds(rows, 2 * WIDE)] * 3 + [
            sds(NC * half, feat), sds(2 * half, feat), sds(part, NC * feat), sds(NC * part, feat), sds(D, bcdt_width),
            sds(rest.shape[0], 4, thin), sds(8, thin)],
        compiler_params=pltpu.CompilerParams(vmem_limit_bytes=48 << 20, dimension_semantics=("arbitrary",)),
        cost_estimate=pl.CostEstimate(flops=1 << 20, bytes_accessed=24 << 20, transcendentals=0),
    )(zx, mix, qkv, o, ff, rest)


P = jax.sharding.PartitionSpec


def dot(a, b):
    return jnp.dot(a, b, preferred_element_type=F32)


def dot_t(a, b):
    return lax.dot_general(a, b, (((1,), (1,)), ((), ())), preferred_element_type=F32)


def t_dot(a, b):
    return lax.dot_general(a, b, (((0,), (0,)), ((), ())), preferred_element_type=F32)


def split_in(w):
    d, n = w.shape
    return w.reshape(d, NC, n // NC).transpose(1, 0, 2)


def halves_of(w):
    d, n = w.shape
    return w.reshape(d, 2, n // 2).transpose(1, 0, 2)


def whole_out(got):
    return got.transpose(1, 0, 2).reshape(got.shape[1], -1)


def split_grad(g):
    n, d = g.shape
    return g.astype(BF).reshape(n, NC, d // NC).transpose(1, 0, 2)


def place_block(piece, start, full_len, axis):
    shape = piece.shape[:axis] + (full_len,) + piece.shape[axis + 1:]
    return lax.dynamic_update_slice_in_dim(jnp.zeros(shape, piece.dtype), piece, start, axis)


def per_device(hidden_in, lengths, norm1_gain, z_weight, x_weight, bcdt_weight, conv_x_weight, conv_x_bias,
               conv_bc_weight, conv_bc_bias, a_log, d_skip, dt_bias, gate_gain, mix_out_weight, norm2_gain,
               q_weight, k_weight, v_weight, att_out_weight, norm3_gain, up_weight, down_weight, grad_output):
    r, c = lax.axis_index("rows"), lax.axis_index("cols")
    rows = lax.axis_size("rows")
    tok_rows, feat = hidden_in.shape
    T, D = tok_rows * rows, feat * NC
    S = T // (rows * NC)
    slab = r * NC + c
    inner = z_weight.shape[1] * rows
    wide = z_weight.shape[1] // NC
    heads_row = a_log.shape[0]
    heads = heads_row // NC
    n_heads = heads_row * rows
    seq_lens = lengths[0]
    places = jnp.arange(T, dtype=jnp.int32)
    one_f32, row8 = ((S, D), F32), ((8, D), F32)
    valid = (places < seq_lens[0] + seq_lens[1]).astype(F32)
    my_valid = lax.dynamic_slice_in_dim(valid, slab * S, S, 0)[:, None]
    pad = 128

    pair = "swap2" if lax.axis_size("dp") == 2 else "swap"

    def halved(a):
        return a.reshape(a.shape[0], 2, -1, a.shape[2]) if pair == "swap2" else a

    def joined(a):
        return a.reshape(a.shape[0], -1, a.shape[-1])

    zx_pieces = halved(jnp.concatenate([split_in(x_weight), split_in(z_weight)], axis=2))
    mix_pieces = halved(mix_out_weight.reshape(NC, -1, feat))
    bcdt_width = bcdt_weight.shape[1]
    bcdt_pad = -bcdt_width % 128
    bcdt_piece = jnp.pad(bcdt_weight, ((0, 0), (0, bcdt_pad))).reshape(2, feat // 2, -1)
    gain_piece = jnp.broadcast_to(jnp.pad(jnp.stack([norm1_gain, norm2_gain, norm3_gain]), ((0, 5), (0, 0)))[None], (2, 8, feat))
    here = lax.dynamic_slice_in_dim(valid, r * tok_rows, tok_rows, 0)[:, None]
    grad = (grad_output.astype(F32) * here).astype(BF).reshape(NC, S, feat)
    hidden_all, g3, h0, w_zx, mix_got, w_bcdt, gains = entry(
        0, hidden_in, grad, (pair, pair, "bcast2", "bcast2"), (zx_pieces, mix_pieces, bcdt_piece, gain_piece))
    g3_mine = lax.dynamic_slice_in_dim(g3, slab * S, S, 0)
    w_mix = whole_out(joined(mix_got))
    gains = gains[:, 0, :3].transpose(1, 0, 2).reshape(3, D)
    w_bcdt, w_zx = w_bcdt.reshape(D, -1), w_zx.reshape(D, 2 * wide)
    w_dt = jnp.pad(lax.dynamic_slice_in_dim(w_bcdt, 2 * STATE + slab * heads, heads, 1), ((0, 0), (0, 128 - heads)))
    w_in = jnp.concatenate([w_bcdt[:, :2 * STATE], w_zx, w_dt], axis=1)
    few = pair == "swap2"
    twice = lambda a: a if few else jnp.repeat(a, NC // 2, axis=0)
    one_way = "swaph" if few else "swap"
    qkv_pieces = halved(twice(jnp.concatenate([halves_of(q_weight), halves_of(k_weight), halves_of(v_weight)], axis=2)))
    o_pieces = halved(twice(att_out_weight.reshape(2, -1, feat)))

    mine = lambda a, n: lax.dynamic_slice_in_dim(a, c * n, n, a.ndim - 1)
    cw = jnp.concatenate([conv_bc_weight, mine(conv_x_weight, wide)], axis=1)
    cw = jnp.concatenate([cw, jnp.concatenate([conv_bc_bias, mine(conv_x_bias, wide)])[None], jnp.zeros((3, MIX), F32)])
    wide_row = lambda a: jnp.pad(a, (0, 256 - a.shape[0]))[None]
    pv = jnp.concatenate([wide_row(mine(gate_gain, wide)), wide_row(jnp.repeat(mine(d_skip, heads), HEAD_DIM)),
                          wide_row(mine(dt_bias, heads)), wide_row(-jnp.exp(mine(a_log, heads))), jnp.zeros((4, 256), F32)])
    u1, proj, mixg, squares, y, states, qkv_split = mixer_fwd(
        6, seq_lens, hidden_all.reshape(rows, NC, tok_rows, feat), gains[0:1], w_bcdt, w_zx, w_dt, cw, pv,
        (one_way,), (qkv_pieces,))
    att3 = qkv_pieces.shape[-1]
    u2, h1, mix_out, gate_scale, qkv, qkv_got, o_split, down_split = link(
        1, mixg, w_mix, functools.partial(mid_mixer, inner), (h0, gains[1:2]), (one_f32, one_f32, ((S, 128), F32)), side=squares,
        w2_kind="rider", post=post_plain, post_out=(((T, att3), BF),), early=("spread",), early_in=(qkv_split,), late=((one_way, None), (one_way, None)),
        late_in=(o_pieces, halved(down_weight.reshape(NC, -1, feat))))
    w_qkv = qkv_got.reshape(D, -1)
    att = att3 // 3

    attended, att_exact, lse, up_split, o_got = att_fwd(
        7, seq_lens, qkv, (one_way, "spread"), (halved(split_in(up_weight)), o_split))
    w_o = whole_out(joined(o_got))
    hidden_units = up_weight.shape[1] // NC
    u3, h2, act, hid, up_got, down_got = link(
        2, attended, w_o, mid_attention, (h1, gains[2:3]), (one_f32,), w2_kind="rider", post=post_gelu,
        post_out=(((T, hidden_units), F32), ((T, hidden_units), BF)), early=("spread",), early_in=(up_split,),
        late=(("spread", None),), late_in=(down_split,))
    w_up, w_down = up_got.reshape(D, -1), whole_out(joined(down_got))
    gelu_back = jax.vjp(functools.partial(jax.nn.gelu, approximate=True), act)[1]

    reduce = "reduce" if few else "swap"

    def added(pieces, got):
        if not few:
            return lax.psum(pieces, "dp")
        own = lax.dynamic_index_in_dim(pieces, lax.axis_index("dp"), 1, False)
        return (own.astype(F32) + got[0].astype(F32)).astype(BF)

    x_kinds = lambda n: ("half",) * n if few else ()
    x_arrays = lambda *arrays: arrays if few else ()
    d_act = gelu_back(dot_t(g3, w_down))[0].astype(BF)
    down_pieces = halved(split_grad(t_dot(hid, g3)))
    up_pieces = halved(t_dot(u3, d_act).astype(BF).reshape(NC, feat, -1))
    g2, dh2, gain3_rows, d_att, *got = link(
        3, d_act, w_up, mid_ff_back, (h2, gains[2:3], g3_mine), (one_f32, row8), w1_t=True, w2=w_o, w2_kind="in_t", post=post_plain,
        post_out=(((T, att), BF),), early=x_kinds(2), early_in=x_arrays(down_pieces, up_pieces))
    ff_sum = jnp.concatenate([added(down_pieces, got[:1]), added(up_pieces, got[1:])], axis=1)
    o_pieces = halved(split_grad(t_dot(attended, g2)))
    d_qkv, ff_split = att_bwd(8, seq_lens, qkv, d_att, att_exact, lse, ("swap",), (ff_sum,))
    qkv_pieces = halved(t_dot(u2, d_qkv).astype(BF).reshape(NC, feat, -1))
    g1_ext, dh1, gain2_rows, d_mix, ff_back, *got = link(
        4, d_qkv, w_qkv, functools.partial(mid_att_back, inner), (h1, gains[1:2], dh2, mix_out, gate_scale), (one_f32, row8), w1_t=True,
        w2=w_mix, w2_kind="in_t", post=post_plain, post_out=(((T, wide), F32),), extra=128,
        early=("spread",) + x_kinds(2), early_in=(ff_split,) + x_arrays(o_pieces, qkv_pieces))
    o_sum, qkv_sum = added(o_pieces, got[:1]), added(qkv_pieces, got[1:])
    g1 = g1_ext[:, :D]
    mix_pieces = halved(split_grad(t_dot(mixg, g1)))
    d_in, tap_grads, row_grads, o_split, qkv_split = mixer_bwd(
        9, seq_lens, proj, cw, pv, y, states, d_mix, g1_ext, ("swap", "swap"), (o_sum, qkv_sum))
    cbw_grad, cxw_grad = tap_grads[:CONV, :2 * STATE], tap_grads[:CONV, 2 * STATE:]
    cbb_grad, cxb_grad = tap_grads[CONV, :2 * STATE], tap_grads[CONV, 2 * STATE:]
    gate_gain_grad, dt_bias_grad, a_log_grad = row_grads[0, :wide], row_grads[2, :heads], row_grads[3, :heads]
    d_skip_grad = row_grads[1, :wide].reshape(heads, HEAD_DIM).sum(1)
    in_grad = t_dot(u1, d_in)
    zx_pieces = halved(in_grad[:, 2 * STATE:2 * STATE + 2 * wide].astype(BF).reshape(NC, feat, -1))
    slabs = rows * NC
    dt_grads = place_block(in_grad[:, 2 * STATE + 2 * wide:2 * STATE + 2 * wide + heads].astype(BF), slab * heads, bcdt_width + bcdt_pad - 2 * STATE, 1)
    bcdt_part = jnp.concatenate([in_grad[:, :2 * STATE].astype(BF), dt_grads], axis=1).reshape(slabs, SMALL, -1)
    misc = jnp.concatenate([cbw_grad.reshape(-1), cbb_grad] + [
        place_block(a, slab * heads, n_heads, 0) for a in (a_log_grad, d_skip_grad, dt_bias_grad)])
    n_misc = misc.shape[0]
    small = jnp.concatenate([gain2_rows[:1], gain3_rows[:1], place_block(cxw_grad, slab * wide, inner, 1).reshape(-1, D),
                             place_block(cxb_grad, slab * wide, inner, 0).reshape(-1, D),
                             place_block(gate_gain_grad, slab * wide, inner, 0).reshape(-1, D), jnp.pad(misc, (0, D - n_misc))[None]])
    thin = bcdt_width + bcdt_pad
    four = D // thin
    small = jnp.pad(small, ((0, slabs - small.shape[0]), (0, 0))).reshape(slabs, four, thin)
    small_hi = small.astype(BF)
    small_lo = (small - small_hi.astype(F32)).astype(BF)
    side = jnp.concatenate([bcdt_part, small_hi, small_lo, jnp.zeros((slabs, S - SMALL - 2 * four, thin), BF)], axis=1)
    rest_all, _, _, _, zx_back, mix_back, o_back, qkv_back, in_got, out_got = link(
        5, d_in, w_in, mid_mixer_back, (h0, gains[0:1], dh1), (((NC, S, feat), BF), row8), w1_t=True, side=side.reshape(T, thin), small=thin,
        early=(reduce, reduce, "spread", "spread"), early_in=(zx_pieces, mix_pieces, o_split, qkv_split), late=(("swap", 0),),
        more_sum=(hid, w_down), after=after_output, after_in=(h2, jnp.broadcast_to(my_valid, (S, 128))), after_out=(((NC, S, feat), BF),))
    output = out_got.reshape(NC * S, feat)
    four_d = lambda a: a if few else a.reshape(NC, 2, -1, a.shape[-1])
    if not few:
        n = ff_back.shape[1] // 2
        ff_back = jnp.concatenate([four_d(ff_back[:, :n]), four_d(ff_back[:, n:])], axis=2)
        zx_back, mix_back = lax.psum(zx_back, "dp"), lax.psum(mix_back, "dp")
    (x_grad, z_grad, q_grad, k_grad, v_grad, mix_grad, o_grad, up_grad, down_grad, bcdt_grad, small, gain1) = finish(
        four_d(zx_back), four_d(mix_back), four_d(qkv_back), four_d(o_back), ff_back, rest_all.reshape(slabs, S, thin), bcdt_width)
    small, gain1_grad = small.reshape(slabs, D), gain1[:4].reshape(D)
    per_inner = inner // D
    edges = [2 + CONV * per_inner, 2 + (CONV + 1) * per_inner, 2 + (CONV + 2) * per_inner]
    cxw_sum = small[2:edges[0]].reshape(CONV, inner)
    cxb_sum, gate_gain_sum = small[edges[0]:edges[1]].reshape(-1), small[edges[1]:edges[2]].reshape(-1)
    misc = small[edges[2]]
    cbw_sum, cbb_sum = misc[:CONV * 2 * STATE].reshape(CONV, 2 * STATE), misc[CONV * 2 * STATE:(CONV + 1) * 2 * STATE]
    a_log_sum, d_skip_sum, dt_bias_sum = jnp.split(misc[n_misc - 3 * n_heads:n_misc], 3)
    input_grad = in_got.reshape(NC * S, feat).astype(F32)
    return (output, input_grad, gain1_grad, z_grad, x_grad, bcdt_grad, cxw_sum, cxb_sum, cbw_sum, cbb_sum, a_log_sum, d_skip_sum,
            dt_bias_sum, gate_gain_sum, mix_grad, small[0], q_grad, k_grad, v_grad, o_grad, small[1], up_grad, down_grad)


def solution(mesh):
    assert mesh.shape["rows"] == 4 and mesh.shape["cols"] == NC
    token = P(("dp", "rows"), "cols")
    w_in, w_out = P("cols", "rows"), P("rows", "cols")
    row, col, whole = P("rows"), P("cols"), P()
    placed = (token, P("dp", None), col, w_in, w_in, P("cols", None), P(None, "rows"), row, whole, whole, row, row, row, row,
              w_out, col, w_in, w_in, w_in, w_out, col, w_in, w_out, token)
    given = (token, token, whole, w_in, w_in, whole, whole, whole, whole, whole, whole, whole, whole, whole, w_out, whole,
             w_in, w_in, w_in, w_out, whole, w_in, w_out)
    return jax.shard_map(per_device, mesh=mesh, in_specs=placed, out_specs=given, check_vma=False)
```

```python
import functools
import jax, jax.numpy as jnp
from jax import lax
from jax.experimental import pallas as pl
from jax.experimental.pallas import tpu as pltpu
MESH = pl.DeviceIdType.MESH
NC = 4
F32, BF = jnp.float32, jnp.bfloat16


def copy_to(src, dst, send, recv, dev):
    return pltpu.make_async_remote_copy(src_ref=src, dst_ref=dst, send_sem=send, recv_sem=recv, device_id=dev, device_id_type=MESH)


def greet(r, c, kinds=(), partners=True):
    barrier = pltpu.get_barrier_semaphore()
    all_cols = any(kind not in ("dp", "half", "spread") for kind in kinds)
    count = 0
    if partners:
        pl.semaphore_signal(barrier, inc=1, device_id={"rows": r ^ 1}, device_id_type=MESH)
        pl.semaphore_signal(barrier, inc=1, device_id={"rows": r ^ 2}, device_id_type=MESH)
        count = 2
    if all_cols:
        for s in range(1, NC):
            pl.semaphore_signal(barrier, inc=1, device_id={"cols": lax.rem(c + s, NC)}, device_id_type=MESH)
        count += NC - 1
    elif partners:
        @pl.when(c > 0)
        def _():
            pl.semaphore_signal(barrier, inc=1, device_id={"cols": c - 1}, device_id_type=MESH)

        @pl.when(c < NC - 1)
        def _():
            pl.semaphore_signal(barrier, inc=1, device_id={"cols": c + 1}, device_id_type=MESH)
        count = count + jnp.where(c > 0, 1, 0) + jnp.where(c < NC - 1, 1, 0)
    if any(kind in ("dp", "swap2", "half", "spread", "reduce") for kind in kinds):
        groups = lax.axis_size("dp")
        for s in range(1, groups):
            pl.semaphore_signal(barrier, inc=1, device_id={"dp": lax.rem(lax.axis_index("dp") + s, groups)}, device_id_type=MESH)
        count = count + groups - 1
    pl.semaphore_wait(barrier, count)


class Riders:
    def __init__(self, kinds, ins, outs, send, recv, loc, *held):
        r, c, g = lax.axis_index("rows"), lax.axis_index("cols"), lax.axis_index("dp")
        groups = lax.axis_size("dp")
        self.remote, self.local, self.late, self.sums = [], [], [], []
        held = iter(held)
        for e, kind in enumerate(kinds):
            src, dst = ins[e], outs[e]
            if kind == "half":
                self.remote.append(copy_to(src.at[:, 1 - g], dst, send.at[e, 0], recv.at[e, 0], {"dp": 1 - g}))
                continue
            if kind == "spread":
                place = dst.at[:, g] if groups == 2 else dst
                self.local.append(pltpu.make_async_copy(src, place, loc.at[e]))
                if groups == 2:
                    self.remote.append(copy_to(src, place, send.at[e, 0], recv.at[e, 0], {"dp": 1 - g}))
                continue
            if kind == "swaph":
                few = src.shape[0] != NC
                piece = lambda to, few=few, src=src: src.at[to >> 1 if few else to, g]
                for s in range(1, NC):
                    to = lax.rem(c + s, NC)
                    self.remote.append(copy_to(piece(to), dst.at[c], send.at[e, s - 1], recv.at[e, s - 1], {"cols": to}))
                self.local.append(pltpu.make_async_copy(piece(c), dst.at[c], loc.at[e]))
                continue
            if kind == "dp":
                for s in range(1, groups):
                    self.remote.append(copy_to(src, dst.at[s - 1], send.at[e, s - 1], recv.at[e, s - 1], {"dp": lax.rem(g + s, groups)}))
                continue
            if kind == "swap":
                for s in range(1, NC):
                    to = lax.rem(c + s, NC)
                    self.remote.append(copy_to(src.at[to], dst.at[c], send.at[e, s - 1], recv.at[e, s - 1], {"cols": to}))
                self.local.append(pltpu.make_async_copy(src.at[c], dst.at[c], loc.at[e]))
                continue
            half = r & 1 if kind == "bcast2" else g
            other = {"rows": r ^ 1} if kind == "bcast2" else {"dp": 1 - g}
            pairs = []
            if kind == "reduce":
                own, got = next(held), next(held)
                first = copy_to(src.at[:, 1 - g], got, send.at[e, 2 * NC - 1], recv.at[e, 2 * NC - 1], other)
                self.sums.append((first, pltpu.make_async_copy(src.at[:, g], own, loc.at[e]), own, got, pairs))
                piece = lambda to, own=own: own.at[to]
                keep = pltpu.make_async_copy(own.at[c], dst.at[c, g], loc.at[e])
                pairs.append((None, keep, copy_to(own.at[c], dst.at[c, g], send.at[e, NC - 1], recv.at[e, NC - 1], other)))
            elif kind == "swap2":
                few = src.shape[0] != NC
                piece = lambda to, few=few, src=src, half=half: src.at[to >> 1 if few else to, half]
                self.local.append(pltpu.make_async_copy(src.at[c >> 1 if few else c], dst.at[c], loc.at[e]))
            else:
                piece = lambda to, src=src, half=half: src.at[half]
                self.local.append(pltpu.make_async_copy(src, dst.at[c], loc.at[e]))
            for s in range(1, NC):
                to, came = lax.rem(c + s, NC), lax.rem(c + NC - s, NC)
                first = copy_to(piece(to), dst.at[c, half], send.at[e, s - 1], recv.at[e, s - 1], {"cols": to})
                pairs.append((first, None, copy_to(dst.at[came, half], dst.at[came, half], send.at[e, NC + s - 1], recv.at[e, NC + s - 1], other)))
            if kind != "reduce":
                self.late.extend(pairs)

    def start(self):
        for first, keep, own, got, pairs in self.sums:
            first.start()
            keep.start()
        for first, _, _ in self.late:
            first.start()
        for one in self.remote + self.local:
            one.start()

    def add(self):
        for first, keep, own, got, pairs in self.sums:
            keep.wait()
            first.wait()
            own[...] = (own[...].astype(F32) + got[...].astype(F32)).astype(BF)
            for one, local, second in pairs:
                if one is None:
                    local.start()
                    second.start()
                else:
                    one.start()

    def relay(self):
        for first, _, second in self.late + [p for one in self.sums for p in one[4] if p[0] is not None]:
            first.wait_recv()
            second.start()

    def finish(self):
        for one in self.remote + self.local:
            one.wait()
        for first, local, second in self.late + [p for one in self.sums for p in one[4]]:
            if first is None:
                local.wait()
            else:
                first.wait_send()
            second.wait()


def rider_parts(kinds, arrays):
    groups = lax.axis_size("dp")
    shapes = []
    for kind, a in zip(kinds, arrays):
        if kind == "swap2":
            a = jax.ShapeDtypeStruct((NC,) + a.shape[1:], a.dtype)
        if kind in ("half", "swaph"):
            a = jax.ShapeDtypeStruct((NC,) + a.shape[2:], a.dtype)
        if kind == "spread":
            a = jax.ShapeDtypeStruct((NC,) + (2,) * (groups == 2) + a.shape[1:], a.dtype)
        lead = {"swap": (), "swap2": (), "half": (), "swaph": (), "spread": (), "reduce": (), "bcast2": (NC,), "dp": (groups - 1,)}[kind]
        shapes.append(jax.ShapeDtypeStruct(lead + a.shape, a.dtype))
    n, most = len(kinds), max(2 * NC, groups)
    sems = [pltpu.SemaphoreType.DMA((n, most)), pltpu.SemaphoreType.DMA((n, most)), pltpu.SemaphoreType.DMA((n,))] if n else []
    for kind, a in zip(kinds, arrays):
        if kind == "reduce":
            sems += [pltpu.VMEM(a.shape[:1] + a.shape[2:], a.dtype)] * 2
    return shapes, sems


SMALL = 96


def sum_groups(x_ref, others, held, dp_s, dp_r, n):
    g, groups = lax.axis_index("dp"), lax.axis_size("dp")
    copies = [copy_to(x_ref, others.at[s - 1], dp_s.at[s - 1], dp_r.at[s - 1], {"dp": lax.rem(g + s, groups)}) for s in range(1, groups)]
    for one in copies:
        one.start()

    def settle():
        total = x_ref[...]
        for s, one in enumerate(copies):
            one.wait()
            total = total + others[s]
        part = (lax.broadcasted_iota(jnp.int32, total.shape, 0) - SMALL) // n
        rest = total - total.astype(BF).astype(F32)
        rest2 = rest - rest.astype(BF).astype(F32)
        second, third = (part == 1) | (part == 4), (part == 2) | (part == 5)
        held[...] = jnp.where(second, rest, jnp.where(third, rest2, total)).astype(BF)
    return settle


def ridden(kernel, n_in, n_out, kinds):
    n = len(kinds)

    def run(*refs):
        ins, rest = refs[:n_in], refs[n_in + n:]
        outs, tail = rest[:n_out], rest[n_out + n:]
        riding = Riders(kinds, refs[n_in:n_in + n], rest[n_out:n_out + n], *tail[-3:])
        step = pl.program_id(0)

        @pl.when(step == 0)
        def _():
            greet(lax.axis_index("rows"), lax.axis_index("cols"), kinds, False)
            riding.start()
        kernel(*ins, *outs, *tail[:-3])

        @pl.when(step == pl.num_programs(0) - 1)
        def _():
            riding.finish()
    return run


def ridden_call(kernel, cid, grid, ins, in_specs, outs, out_specs, scratch, flops, kinds, arrays):
    shapes, sems = rider_parts(kinds, arrays)
    any_space = [pl.BlockSpec(memory_space=pl.ANY)] * len(kinds)
    return pl.pallas_call(
        ridden(kernel, len(ins), len(outs), tuple(kinds)),
        grid=(grid,),
        in_specs=list(in_specs) + any_space,
        out_specs=list(out_specs) + any_space,
        out_shape=[jax.ShapeDtypeStruct(*o) for o in outs] + shapes,
        scratch_shapes=list(scratch) + sems,
        compiler_params=pltpu.CompilerParams(collective_id=cid, has_side_effects=True, vmem_limit_bytes=56 << 20,
                                             dimension_semantics=("arbitrary",)),
        cost_estimate=pl.CostEstimate(flops=flops, bytes_accessed=24 << 20, transcendentals=4 << 20),
    )(*ins, *arrays)


HEAD_DIM = 64
STATE = 128
CONV = 4
SPAN = 256
WIDE = 192
MIX = 2 * STATE + WIDE


def mm(a, b, ca=1, cb=0):
    return lax.dot_general(a.astype(BF), b.astype(BF), (((ca,), (cb,)), ((), ())), preferred_element_type=F32)


def by_parts(a, mask, ca, cb, parts, mask_first=False):
    total = None
    for _ in range(parts):
        high = a.astype(BF)
        one = mm(mask, high, ca, cb) if mask_first else mm(high, mask, ca, cb)
        total = one if total is None else total + one
        a = a - high.astype(F32)
    return total


def seg_at(place, l0, l1):
    return jnp.where(place < 0, -1, jnp.where(place >= l0, 1, 0) + jnp.where(place >= l0 + l1, 1, 0))


def sigmoid(x):
    return 1.0 / (1.0 + jnp.exp(-x))


def by_head(a, lane):
    return jnp.where(lane < HEAD_DIM, a[:, 0:1], jnp.where(lane < 2 * HEAD_DIM, a[:, 1:2], a[:, 2:3]))


def head_sums(a):
    i = lax.broadcasted_iota(jnp.int32, (WIDE, 128), 0)
    j = lax.broadcasted_iota(jnp.int32, (WIDE, 128), 1)
    return by_parts(a, jnp.where(i // HEAD_DIM == j, 1.0, 0.0), 1, 0, 2)


class Block:
    def __init__(self, blk, lens, proj, before, cw, pv):
        self.l0, self.l1 = lens[0], lens[1]
        self.start = blk * SPAN
        v = proj[:, :MIX]
        self.place = self.start + lax.broadcasted_iota(jnp.int32, (SPAN, 1), 0)
        self.seg = seg_at(self.place, self.l0, self.l1)
        ext = jnp.concatenate([before[:, :MIX], v], axis=0)
        acc = cw[4:5] + cw[3:4] * v
        self.shifted = [v]
        for s in range(1, CONV):
            keep = jnp.where(seg_at(self.place - s, self.l0, self.l1) == self.seg, 1.0, 0.0)
            moved = ext[8 - s:8 - s + SPAN] * keep
            self.shifted.append(moved)
            acc = acc + cw[3 - s:4 - s] * moved
        self.acc = acc
        self.gate = sigmoid(acc)
        act = acc * self.gate
        self.b, self.c, self.x = act[:, :STATE], act[:, STATE:2 * STATE], act[:, 2 * STATE:]
        self.z = proj[:, MIX:MIX + WIDE]
        self.zs = sigmoid(self.z)
        self.raw = proj[:, MIX + WIDE:] + pv[2:3, :128]
        self.dt = jnp.maximum(self.raw, 0.0) + jnp.log1p(jnp.exp(-jnp.abs(self.raw)))
        self.rate = pv[3:4, :128] * self.dt
        i = lax.broadcasted_iota(jnp.int32, (SPAN, SPAN), 0)
        j = lax.broadcasted_iota(jnp.int32, (SPAN, SPAN), 1)
        self.low = jnp.where(j <= i, 1.0, 0.0).astype(F32)
        self.cum = by_parts(self.rate, self.low, 1, 0, 3, True)
        self.cum_t = self.cum.T
        seg_row = seg_at(self.start + lax.broadcasted_iota(jnp.int32, (1, SPAN), 1), self.l0, self.l1)
        self.allowed = (j <= i) & (seg_row == self.seg)
        self.scores = mm(self.c, self.b, 1, 1)
        self.lane = lax.broadcasted_iota(jnp.int32, (SPAN, WIDE), 1)
        self.w = self.x * by_head(self.dt, self.lane)
        prior = seg_at(self.start - 1, self.l0, self.l1)
        last = seg_at(self.start + SPAN - 1, self.l0, self.l1)
        end = self.cum[SPAN - 1:SPAN]
        self.e = by_head(jnp.exp(self.cum), self.lane) * jnp.where(self.seg == prior, 1.0, 0.0)
        self.tail = by_head(jnp.exp(end - self.cum), self.lane) * jnp.where(self.seg == last, 1.0, 0.0)
        self.through = jnp.exp(end) * jnp.where(last == prior, 1.0, 0.0)
        row = lax.broadcasted_iota(jnp.int32, (WIDE, 1), 0)
        self.through_rows = jnp.where(row < HEAD_DIM, self.through[:, 0:1],
                                      jnp.where(row < 2 * HEAD_DIM, self.through[:, 1:2], self.through[:, 2:3]))

    def decay(self, h):
        return jnp.exp(jnp.where(self.allowed, self.cum[:, h:h + 1] - self.cum_t[h:h + 1, :], -1e30))

    def of_head(self, a, h):
        return jnp.where(self.lane // HEAD_DIM == h, a, 0.0)


def mixer_fwd_kernel(lens, hidden, gain, w_bc, w_xz, w_dt, cw, pv, u_out, proj_out, mixg, squares, y_out, states, state, before):
    blk = pl.program_id(0)

    @pl.when(blk == 0)
    def _():
        state[...] = jnp.zeros_like(state)
        before[...] = jnp.zeros_like(before)
    parts = [hidden[0, i].astype(F32) for i in range(NC)]
    feat = parts[0].shape[1]
    squares_in = sum(jnp.sum(p * p, axis=1, keepdims=True) for p in parts)
    scale = lax.rsqrt(squares_in / (NC * feat) + 1e-05)
    for i, p in enumerate(parts):
        at = slice(i * feat, (i + 1) * feat)
        u_out[:, at] = (p * scale * gain[:, at]).astype(BF)
    u = u_out[...]
    proj = jnp.concatenate([mm(u, w_bc[:, :2 * STATE]), mm(u, w_xz[...]), mm(u, w_dt[...])], axis=1)
    proj_out[...] = proj
    k = Block(blk, lens, proj, before[...], cw[...], pv[...])
    before[...] = proj[SPAN - 8:]
    s_in = state[...]
    states[0] = s_in
    y = mm(k.c, s_in, 1, 1) * k.e
    for h in range(3):
        y = y + mm(k.scores * k.decay(h), k.of_head(k.w, h))
    y = y + pv[1:2, :WIDE] * k.x
    state[...] = k.through_rows * s_in + mm(k.tail * k.w, k.b, 0, 0)
    y_out[...] = y
    gated = y * k.z * k.zs
    mixg[...] = (gated * pv[0:1, :WIDE]).astype(BF)
    squares[...] = jnp.broadcast_to(jnp.sum(gated * gated, axis=1, keepdims=True), squares.shape).astype(BF)


def mixer_bwd_kernel(lens, proj, before, cw, pv, y_ref, states, d_mix, extra, d_in, taps, rows, d_state, later):
    step = pl.program_id(0)
    blk = pl.num_programs(0) - 1 - step

    @pl.when(step == 0)
    def _():
        d_state[...] = jnp.zeros_like(d_state)
        later[...] = jnp.zeros_like(later)
        taps[...] = jnp.zeros_like(taps)
        rows[...] = jnp.zeros_like(rows)
    k = Block(blk, lens, proj[...], before[...], cw[...], pv[...])
    y, dm, s_in, ds = y_ref[...], d_mix[...], states[0], d_state[...]
    tilt = extra[:, 0:1].astype(F32) + extra[:, 64:65].astype(F32)
    silu_z = k.z * k.zs
    gated = y * silu_z
    d_gated = dm * pv[0:1, :WIDE] - gated * tilt
    d_z = d_gated * y * (k.zs * (1.0 + k.z * (1.0 - k.zs)))
    dy = d_gated * silu_z
    zeros = jnp.zeros((SPAN, 128), F32)
    lane = lax.broadcasted_iota(jnp.int32, (SPAN, 128), 1)
    top = lax.broadcasted_iota(jnp.int32, (128, SPAN), 0)
    d_cum, cols = zeros, jnp.zeros((128, SPAN), F32)
    d_scores = jnp.zeros((SPAN, SPAN), F32)
    dw = jnp.zeros((SPAN, WIDE), F32)
    for h in range(3):
        decay = k.decay(h)
        mixing = k.scores * decay
        dyh = k.of_head(dy, h).astype(BF)
        d_mixing = mm(dyh, k.w, 1, 1)
        d_scores = d_scores + d_mixing * decay
        moved = d_mixing * mixing
        d_cum = jnp.where(lane == h, jnp.sum(moved, axis=1, keepdims=True), d_cum)
        cols = jnp.where(top == h, jnp.sum(moved, axis=0, keepdims=True), cols)
        dw = dw + mm(mixing, dyh, 0, 0)
    e_dy, tail_w = k.e * dy, k.tail * k.w
    back = mm(k.b, ds, 1, 1)
    dw = dw + k.tail * back
    d_c = mm(d_scores, k.b) + mm(e_dy, s_in)
    d_b = mm(d_scores, k.c, 0, 0) + mm(tail_w, ds)
    through_state = mm(k.c, s_in, 1, 1) * k.e
    left = head_sums(tail_w * back)
    d_cum = d_cum - cols.T + head_sums(dy * through_state) - left
    own = jnp.sum(ds * s_in, axis=1, keepdims=True)
    of_row = lax.broadcasted_iota(jnp.int32, (WIDE, 128), 0) // HEAD_DIM
    own = jnp.sum(jnp.where(of_row == lax.broadcasted_iota(jnp.int32, (WIDE, 128), 1), own, 0.0), axis=0, keepdims=True)
    at_end = jnp.sum(left, axis=0, keepdims=True) + k.through * own
    is_last = lax.broadcasted_iota(jnp.int32, (SPAN, 128), 0) == SPAN - 1
    d_cum = d_cum + jnp.where(is_last, at_end, 0.0)
    d_rate = by_parts(d_cum, k.low, 0, 0, 3, True)
    d_dt = head_sums(dw * k.x) + d_rate * pv[3:4, :128]
    d_raw = jnp.where(lane < 3, d_dt * sigmoid(k.raw), 0.0)
    d_x = dw * by_head(k.dt, k.lane) + pv[1:2, :WIDE] * dy
    d_pre = jnp.concatenate([d_b, d_c, d_x], axis=1) * (k.gate * (1.0 + k.acc * (1.0 - k.gate)))
    wide_rows = [jnp.sum(gated * dm, axis=0, keepdims=True), jnp.sum(dy * k.x, axis=0, keepdims=True)]
    thin_rows = [jnp.sum(d_raw, axis=0, keepdims=True), jnp.sum(d_rate * k.rate, axis=0, keepdims=True)]
    for i, one in enumerate(wide_rows):
        rows[i:i + 1, :WIDE] += one
    for i, one in enumerate(thin_rows):
        rows[2 + i:3 + i, :128] += one
    for s in range(CONV):
        taps[3 - s:4 - s] += jnp.sum(d_pre * k.shifted[s], axis=0, keepdims=True)
    taps[4:5] += jnp.sum(d_pre, axis=0, keepdims=True)
    ext = jnp.concatenate([d_pre, later[...]], axis=0)
    place = k.start + lax.broadcasted_iota(jnp.int32, (SPAN + 8, 1), 0)
    seg = seg_at(place, k.l0, k.l1)
    d_v = cw[3:4] * d_pre
    for s in range(1, CONV):
        keep = jnp.where(seg_at(place - s, k.l0, k.l1) == seg, 1.0, 0.0)
        d_v = d_v + cw[3 - s:4 - s] * (ext * keep)[s:s + SPAN]
    later[...] = d_pre[:8]
    d_in[...] = jnp.concatenate([d_v, d_z, d_raw], axis=1).astype(BF)
    d_state[...] = k.through_rows * ds + mm(e_dy, k.c, 0, 0)


def mixer_specs(n, order):
    block = lambda width: pl.BlockSpec((SPAN, width), lambda i: (order(i), 0))
    whole = lambda shape: pl.BlockSpec(shape, lambda i: (0, 0))
    before = pl.BlockSpec((8, MIX + WIDE + 128), lambda i: (jnp.maximum(order(i) * (SPAN // 8) - 1, 0), 0))
    return block, whole, [pl.BlockSpec(memory_space=pltpu.SMEM), block(MIX + WIDE + 128), before, whole((8, MIX)), whole((8, 256))]


def mixer_fwd(cid, lens, hidden, gain, w_bc, w_xz, w_dt, cw, pv, kinds, arrays):
    _, _, tok, feat = hidden.shape
    T, D = hidden.shape[0] * tok, NC * feat
    n, per = T // SPAN, tok // SPAN
    block, whole, _ = mixer_specs(n, lambda i: i)
    cols = MIX + WIDE + 128
    return ridden_call(
        mixer_fwd_kernel, cid, n, (lens, hidden, gain, w_bc, w_xz, w_dt, cw, pv),
        [pl.BlockSpec(memory_space=pltpu.SMEM), pl.BlockSpec((1, NC, SPAN, feat), lambda i: (i // per, 0, i % per, 0)),
         whole((1, D)), whole(w_bc.shape), whole(w_xz.shape), whole(w_dt.shape), whole((8, MIX)), whole((8, 256))],
        [((T, D), BF), ((T, cols), F32), ((T, WIDE), BF), ((T, 128), BF), ((T, WIDE), F32), ((n, WIDE, STATE), F32)],
        [block(D), block(cols), block(WIDE), block(128), block(WIDE), pl.BlockSpec((1, WIDE, STATE), lambda i: (i, 0, 0))],
        [pltpu.VMEM((WIDE, STATE), F32), pltpu.VMEM((8, cols), F32)], 8 << 30, kinds, arrays)


def mixer_bwd(cid, lens, proj, cw, pv, y, states, d_mix, g1_ext, kinds, arrays):
    T = proj.shape[0]
    n = T // SPAN
    order = lambda i: n - 1 - i
    block, whole, first = mixer_specs(n, order)
    at = g1_ext.shape[1] // 128 - 1
    return ridden_call(
        mixer_bwd_kernel, cid, n, (lens, proj, proj, cw, pv, y, states, d_mix, g1_ext),
        first + [block(WIDE), pl.BlockSpec((1, WIDE, STATE), lambda i: (order(i), 0, 0)), block(WIDE),
                 pl.BlockSpec((SPAN, 128), lambda i: (order(i), at))],
        [((T, MIX + WIDE + 128), BF), ((8, MIX), F32), ((8, 256), F32)],
        [block(MIX + WIDE + 128), whole((8, MIX)), whole((8, 256))],
        [pltpu.VMEM((WIDE, STATE), F32), pltpu.VMEM((8, MIX), F32)], 12 << 30, kinds, arrays)


AHEAD_DIM = 64
SCALE = AHEAD_DIM ** (-0.5)
LOW = -1e30


def att_allowed(lens, i, j, n, flip):
    a, b = lax.broadcasted_iota(jnp.int32, (n, 1), 0), lax.broadcasted_iota(jnp.int32, (1, n), 1)
    qp, kp = (i * n + b, j * n + a) if flip else (i * n + a, j * n + b)
    return (kp <= qp) & (seg_at(kp, lens[0], lens[1]) == seg_at(qp, lens[0], lens[1]))


def att_fwd_kernel(lens, qkv, attended, o_ref, lse):
    i = pl.program_id(0)
    n = o_ref.shape[0]
    lane = lax.broadcasted_iota(jnp.int32, (n, WIDE), 1)
    thin = lax.broadcasted_iota(jnp.int32, (n, 128), 1)
    mine = jnp.where((i == 0) | (i == 3), 0, 1) == lax.rem(lax.axis_index("cols"), 2)

    @pl.when(jnp.logical_not(mine))
    def _():
        attended[...] = jnp.zeros_like(attended)
        o_ref[...] = jnp.zeros_like(o_ref)
        lse[...] = jnp.zeros_like(lse)

    @pl.when(mine)
    def _():
        q = qkv[pl.ds(i * n, n), :WIDE] * jnp.asarray(SCALE, BF)
        heads = [jnp.where(lane // AHEAD_DIM == h, q, jnp.zeros_like(q)) for h in range(3)]

        def body(j, carry):
            tops, sums, acc = carry
            k, v = qkv[pl.ds(j * n, n), WIDE:2 * WIDE], qkv[pl.ds(j * n, n), 2 * WIDE:]
            allowed = att_allowed(lens, i, j, n, False)
            new_tops, new_sums = [], []
            for h in range(3):
                s = jnp.where(allowed, mm(heads[h], k, 1, 1), LOW)
                top = jnp.maximum(tops[h], jnp.max(s, axis=1, keepdims=True))
                p = jnp.exp(s - top)
                fade = jnp.exp(tops[h] - top)
                new_tops.append(top)
                new_sums.append(sums[h] * fade + jnp.sum(p, axis=1, keepdims=True))
                acc = jnp.where(lane // AHEAD_DIM == h, acc * fade + mm(p, v), acc)
            return tuple(new_tops), tuple(new_sums), acc

        zero = jnp.zeros((n, 1), F32)
        start = (tuple(zero + LOW for _ in range(3)), (zero,) * 3, jnp.zeros((n, WIDE), F32))
        tops, sums, acc = lax.fori_loop(0, i + 1, body, start)
        pick = lambda a: jnp.where(lane < AHEAD_DIM, a[0], jnp.where(lane < 2 * AHEAD_DIM, a[1], a[2]))
        out = acc / pick(sums)
        o_ref[...] = out
        attended[...] = out.astype(BF)
        logs = [t + jnp.log(s) for t, s in zip(tops, sums)]
        lse[...] = jnp.where(thin == 0, logs[0], jnp.where(thin == 1, logs[1], logs[2]))


def att_bwd_kernel(lens, qkv, d_att, o_ref, lse, d_qkv, dk, dv):
    i = pl.program_id(0)
    n = lse.shape[0]
    lane = lax.broadcasted_iota(jnp.int32, (n, WIDE), 1)
    mine = jnp.where((i == 0) | (i == 3), 0, 1) == lax.rem(lax.axis_index("cols"), 2)

    @pl.when(i == 0)
    def _():
        dk[...] = jnp.zeros_like(dk)
        dv[...] = jnp.zeros_like(dv)

    @pl.when(jnp.logical_not(mine))
    def _():
        d_qkv[pl.ds(i * n, n), :WIDE] = jnp.zeros((n, WIDE), BF)

    @pl.when(mine)
    def _():
        q = qkv[pl.ds(i * n, n), :WIDE]
        do = d_att[...]
        delta = head_sums(o_ref[...] * do.astype(F32)).T
        logs = lse[...].T
        none = jnp.zeros_like(q)
        qs = [jnp.where(lane // AHEAD_DIM == h, q, none) for h in range(3)]
        dos = [jnp.where(lane // AHEAD_DIM == h, do, none) for h in range(3)]

        def body(j, dq):
            at = pl.ds(j * n, n)
            k, v = qkv[at, WIDE:2 * WIDE], qkv[at, 2 * WIDE:]
            allowed = att_allowed(lens, i, j, n, True)
            for h in range(3):
                s = mm(k, qs[h], 1, 1) * SCALE
                p = jnp.exp(jnp.where(allowed, s, LOW) - logs[h:h + 1])
                ds = (p * (mm(v, dos[h], 1, 1) - delta[h:h + 1]) * SCALE).astype(BF)
                dv[at, :] += mm(p, dos[h])
                dk[at, :] += mm(ds, qs[h])
                dq = jnp.where(lane // AHEAD_DIM == h, dq + mm(ds, k, 0, 0), dq)
            return dq

        dq = lax.fori_loop(0, i + 1, body, jnp.zeros((n, WIDE), F32))
        d_qkv[pl.ds(i * n, n), :WIDE] = dq.astype(BF)

    @pl.when(i == pl.num_programs(0) - 1)
    def _():
        d_qkv[:, WIDE:2 * WIDE] = dk[...].astype(BF)
        d_qkv[:, 2 * WIDE:] = dv[...].astype(BF)


def att_call(kernel, cid, lens, qkv, blocked, outs, out_specs, scratch, kinds, arrays):
    T = qkv.shape[0]
    specs = [pl.BlockSpec(memory_space=pltpu.SMEM), pl.BlockSpec((T, 3 * WIDE), lambda i: (0, 0))]
    specs += [pl.BlockSpec((T // 4, a.shape[1]), lambda i: (i, 0)) for a in blocked]
    return ridden_call(kernel, cid, 4, (lens, qkv) + blocked, specs, outs, out_specs, scratch, 8 << 30, kinds, arrays)


def att_fwd(cid, lens, qkv, kinds, arrays):
    T = qkv.shape[0]
    block = lambda w: pl.BlockSpec((T // 4, w), lambda i: (i, 0))
    return att_call(att_fwd_kernel, cid, lens, qkv, (), [((T, WIDE), BF), ((T, WIDE), F32), ((T, 128), F32)],
                    [block(WIDE), block(WIDE), block(128)], [], kinds, arrays)


def att_bwd(cid, lens, qkv, d_att, o, lse, kinds, arrays):
    T = qkv.shape[0]
    return att_call(att_bwd_kernel, cid, lens, qkv, (d_att, o, lse), [((T, 3 * WIDE), BF)],
                    [pl.BlockSpec((T, 3 * WIDE), lambda i: (0, 0))], [pltpu.VMEM((T, WIDE), F32), pltpu.VMEM((T, WIDE), F32)], kinds, arrays)


VMEM, ANY = pltpu.VMEM, pl.ANY


HALVES = 2


class Sum:
    def __init__(self, r, c, partial, bufs):
        self.r, self.c, self.partial = r, c, partial
        self.yy, self.kk = r >> 1, r & 1
        (self.part, self.p_out, self.k_buf, self.y_out, self.y_buf, self.z_out, self.r_buf, self.l_buf,
         self.k_s, self.k_r, self.y_s, self.y_r, self.zr_s, self.zr_r, self.zl_s, self.zl_r) = bufs
        self.cut = self.part.shape[1] // HALVES

    @staticmethod
    def scratch(S, W):
        buf, sem = (lambda *n: VMEM(n + (S, W), BF)), (lambda n: pltpu.SemaphoreType.DMA((n,)))
        return [VMEM((NC, S, W), F32), buf(2, NC), buf(2, NC)] + [buf(NC)] * 5 + [sem(2 * NC), sem(2 * NC)] + [sem(HALVES * NC)] * 6

    def k_copy(self, y, cc):
        i = y * NC + cc
        return copy_to(self.p_out.at[y, cc], self.k_buf.at[y, cc], self.k_s.at[i], self.k_r.at[i], {"rows": self.r ^ 1})

    def piece(self, src, dst, send, recv, cc, h, to):
        at, i = pl.ds(h * self.cut, self.cut), cc * HALVES + h
        return copy_to(src.at[cc, at], dst.at[cc, at], send.at[i], recv.at[i], to)

    def y_copy(self, cc, h):
        return self.piece(self.y_out, self.y_buf, self.y_s, self.y_r, cc, h, {"rows": self.r ^ 2})

    def r_copy(self, cc, h):
        return self.piece(self.z_out, self.r_buf, self.zr_s, self.zr_r, cc, h, {"cols": self.c + 1})

    def l_copy(self, cc, h):
        return self.piece(self.z_out, self.l_buf, self.zl_s, self.zl_r, cc, h, {"cols": self.c - 1})

    def nth(self, j):
        return jnp.where(self.c < NC // 2, NC - 1 - j, j)

    def each(self, f):
        def body(j, carry):
            f(self.nth(j))
            return carry
        lax.fori_loop(0, NC, body, 0)

    def to_core(self):
        def half(i, carry):
            y = jnp.where(i == 0, 1 - self.yy, self.yy)

            def one(cc):
                self.p_out[y, cc] = self.partial(y * 2 + (1 - self.kk), cc).astype(BF)
                self.k_copy(y, cc).start()
            self.each(one)
            return carry
        lax.fori_loop(0, 2, half, 0)

    def to_y(self):
        def one(cc):
            mine = self.partial((1 - self.yy) * 2 + self.kk, cc)
            self.k_copy(1 - self.yy, cc).wait_recv()
            self.y_out[cc] = (mine + self.k_buf[1 - self.yy, cc].astype(F32)).astype(BF)
            self.y_copy(cc, 0).start()
        self.each(one)
        for h in range(1, HALVES):
            self.each(lambda cc: self.y_copy(cc, h).start())

    def own(self):
        def one(cc):
            mine = self.partial(self.r, cc)
            self.k_copy(self.yy, cc).wait_recv()
            self.part[cc] = mine + self.k_buf[self.yy, cc].astype(F32)
        self.each(one)

    def step(self, j, h):
        c, cc = self.c, self.nth(j)
        at = pl.ds(h * self.cut, self.cut)
        self.y_copy(cc, h).wait_recv()
        self.part[cc, at] += self.y_buf[cc, at].astype(F32)

        @pl.when(cc > c)
        def _():
            @pl.when(c > 0)
            def _():
                self.r_copy(cc, h).wait_recv()
                self.part[cc, at] += self.r_buf[cc, at].astype(F32)
            self.z_out[cc, at] = self.part[cc, at].astype(BF)
            self.r_copy(cc, h).start()

        @pl.when(cc < c)
        def _():
            @pl.when(c < NC - 1)
            def _():
                self.l_copy(cc, h).wait_recv()
                self.part[cc, at] += self.l_buf[cc, at].astype(F32)
            self.z_out[cc, at] = self.part[cc, at].astype(BF)
            self.l_copy(cc, h).start()

    def last(self, total, h):
        c, at = self.c, pl.ds(h * self.cut, self.cut)
        total[at] = self.part[c, at]

        @pl.when(c > 0)
        def _():
            self.r_copy(c, h).wait_recv()
            total[at] += self.r_buf[c, at].astype(F32)

        @pl.when(c < NC - 1)
        def _():
            self.l_copy(c, h).wait_recv()
            total[at] += self.l_buf[c, at].astype(F32)

    def finish(self):
        def one(cc):
            self.k_copy(0, cc).wait_send()
            self.k_copy(1, cc).wait_send()
            for h in range(HALVES):
                self.y_copy(cc, h).wait_send()

                @pl.when(cc > self.c)
                def _():
                    self.r_copy(cc, h).wait_send()

                @pl.when(cc < self.c)
                def _():
                    self.l_copy(cc, h).wait_send()
        self.each(one)


class Gather:
    def __init__(self, r, c, out, S, sems, use=None):
        self.r, self.c, self.out, self.S, self.use = r, c, out, S, use
        self.recv, self.zr_s, self.zl_s, self.y_s, self.k_s = sems

    @staticmethod
    def scratch():
        return [pltpu.SemaphoreType.DMA((HALVES * n,)) for n in (4 * NC, NC, NC, NC, 2 * NC)]

    def slab(self, rr, cc):
        return self.out.at[pl.ds(pl.multiple_of((rr * NC + cc) * self.S, 16), self.S)]

    def move(self, rr, cc, h, sem, to):
        cut = self.S // HALVES
        ref = self.out.at[pl.ds(pl.multiple_of((rr * NC + cc) * self.S + h * cut, 16), cut)]
        return copy_to(ref, ref, sem, self.recv.at[(rr * NC + cc) * HALVES + h], to)

    def right(self, cc, h):
        return self.move(self.r, cc, h, self.zr_s.at[cc * HALVES + h], {"cols": self.c + 1})

    def left(self, cc, h):
        return self.move(self.r, cc, h, self.zl_s.at[cc * HALVES + h], {"cols": self.c - 1})

    def y_copy(self, cc, h):
        return self.move(self.r, cc, h, self.y_s.at[cc * HALVES + h], {"rows": self.r ^ 2})

    def k_copy(self, rr, cc, h):
        return self.move(rr, cc, h, self.k_s.at[((rr >> 1) * NC + cc) * HALVES + h], {"rows": self.r ^ 1})

    def got(self, rr, cc, h):
        self.k_copy(rr, cc, h).wait_recv()

    def pass_on(self, cc, h):
        c = self.c

        @pl.when((cc <= c) & (c < NC - 1))
        def _():
            self.right(cc, h).start()

        @pl.when((cc >= c) & (c > 0))
        def _():
            self.left(cc, h).start()
        self.y_copy(cc, h).start()
        self.k_copy(self.r, cc, h).start()

    def begin(self):
        for h in range(HALVES):
            self.pass_on(self.c, h)

    def sides(self, off, f):
        for s in (-1, 1):
            cc = self.c + s * off
            fits = (cc >= 0) & (cc < NC) & (off < NC)
            if s == 1:
                fits = fits & (off > 0)

            @pl.when(fits)
            def _():
                f(cc)

    def forward(self, d, halves=range(HALVES)):
        for h in halves:
            def along(cc):
                self.got(self.r, cc, h)
                self.pass_on(cc, h)

            def across(cc):
                self.got(self.r ^ 2, cc, h)
                self.k_copy(self.r ^ 2, cc, h).start()
            self.sides(d, along)
            self.sides(d - 1, across)

    def uses(self, d):
        def one(i, carry):
            kind, s = i >> 1, (i & 1) * 2 - 1
            off = d - jnp.where(kind == 0, 0, jnp.where(kind == 3, 2, 1))
            rr = self.r ^ jnp.where(kind == 0, 0, jnp.where(kind == 1, 2, jnp.where(kind == 2, 1, 3)))
            cc = self.c + s * off
            fits = (off >= 0) & (off < NC) & (cc >= 0) & (cc < NC) & ((s < 0) | (off > 0))

            @pl.when(fits)
            def _():
                @pl.when(kind >= 2)
                def _():
                    for h in range(HALVES):
                        self.got(rr, cc, h)
                if self.use is not None:
                    self.use(rr, cc)
            return carry
        lax.fori_loop(0, 8, one, 0)

    def finish(self):
        def body(cc, carry):
            for h in range(HALVES):
                self.y_copy(cc, h).wait_send()
                self.k_copy(self.r, cc, h).wait_send()
                self.k_copy(self.r ^ 2, cc, h).wait_send()

                @pl.when((cc <= self.c) & (self.c < NC - 1))
                def _():
                    self.right(cc, h).wait_send()

                @pl.when((cc >= self.c) & (self.c > 0))
                def _():
                    self.left(cc, h).wait_send()
            return carry
        lax.fori_loop(0, NC, body, 0)


def link_call(kernel, cid, ins, in_spaces, outs, out_spaces, scratch, flops):
    return pl.pallas_call(
        kernel,
        out_shape=[jax.ShapeDtypeStruct(s, d) for s, d in outs],
        in_specs=[pl.BlockSpec(memory_space=s) for s in in_spaces],
        out_specs=[pl.BlockSpec(memory_space=s) for s in out_spaces],
        scratch_shapes=scratch,
        compiler_params=pltpu.CompilerParams(collective_id=cid, has_side_effects=True, vmem_limit_bytes=62 << 20),
        cost_estimate=pl.CostEstimate(flops=flops, bytes_accessed=96 << 20, transcendentals=0),
    )(*ins)


def entry_kernel(kinds, *refs):
    n = len(kinds)
    it = iter(refs)
    take = lambda k: [next(it) for _ in range(k)]
    hidden, grad = take(2)
    ins = take(n)
    hid_all, g_all, h0 = take(3)
    outs = take(n)
    got, = take(1)
    hid_sems, g_sems, swap_sems, sems = take(5), take(5), take(3), take(3)
    r, c = lax.axis_index("rows"), lax.axis_index("cols")
    greet(r, c, kinds)
    big, S = hidden.shape[0], got.shape[1]
    feat = hidden.shape[1]
    first = Gather(r, c, hid_all, big, hid_sems)
    second = Gather(r, c, g_all, S, g_sems)
    swap = Riders(("swap",), (grad,), (got,), *swap_sems)
    riding = Riders(kinds, ins, outs, *sems)
    hid_all[pl.ds(pl.multiple_of((r * NC + c) * big, 16), big), :] = hidden[...]
    first.begin()
    swap.start()
    for d in range(1, NC):
        first.forward(d)
        if d == 1:
            riding.start()
        first.uses(d)
        if d == 2:
            swap.finish()
            for i in range(NC):
                g_all[pl.ds(pl.multiple_of((r * NC + c) * S, 16), S), i * feat:(i + 1) * feat] = got[i]
            second.begin()
        if d == 3:
            riding.relay()
            second.forward(1)
            second.uses(1)
    for i in range(NC):
        h0[:, i * feat:(i + 1) * feat] = hid_all[pl.ds(pl.multiple_of((r * NC + i) * big + c * S, 16), S), :]
    for d in range(NC, NC + 2):
        first.forward(d)
        first.uses(d)
        second.forward(d - 2)
        second.uses(d - 2)
    for d in range(NC, NC + 2):
        second.forward(d)
        second.uses(d)
    first.finish()
    second.finish()
    riding.finish()


def entry(cid, hidden, grad, kinds, arrays):
    big, feat = hidden.shape
    S, D = big // NC, feat * NC
    shapes, sems = rider_parts(kinds, arrays)
    _, swap_sems = rider_parts(("swap",), (grad,))
    outs = [((4 * NC * big, feat), BF), ((4 * NC * S, D), BF), ((S, D), BF)] + [(s.shape, s.dtype) for s in shapes]
    scratch = [VMEM(grad.shape, BF)] + Gather.scratch() + Gather.scratch() + swap_sems + sems
    return link_call(functools.partial(entry_kernel, tuple(kinds)), cid, [hidden, grad] + list(arrays), [VMEM] + [ANY] * (1 + len(kinds)),
                     outs, [VMEM] * 3 + [ANY] * len(kinds), scratch, 1 << 20)


def link_kernel(spec, *refs):
    it = iter(refs)
    take = lambda n: [next(it) for _ in range(n)]
    maybe = lambda key, n=1: take(n) if spec[key] else [None] * n
    a, w1 = take(2)
    side, = maybe("side")
    mid_in = take(spec["n_mid"])
    w2, = take(1) if spec["w2"] in ("in", "in_t") else [None]
    a2, v2 = maybe("more_sum", 2)
    after_in = take(spec["n_after"])
    early_in = take(len(spec["early"]))
    late_in = take(sum(src is None for _, src in spec["late"]))
    u_all = next(it)
    mid_out = take(spec["n_mid_out"])
    post_out = take(spec["n_post"])
    after_out = take(spec["n_after_out"])
    early_out, late_out = take(len(spec["early"])), take(len(spec["late"]))
    final_out = take(len(after_out))
    total, = take(1)
    sum_bufs, gather_sems = take(16), take(5)
    sum2_bufs = take(17) if spec["more_sum"] else []
    small = take(6) if spec["small"] else None
    early_sems, late_sems, final_sems = take(spec["n_early_sems"]), take(spec["n_late_sems"]), take(3 * (len(after_out) > 0))
    r, c = lax.axis_index("rows"), lax.axis_index("cols")
    S, W = total.shape
    D = w1.shape[0] if spec["w1_t"] else w1.shape[1]
    late_kinds = tuple(kind for kind, _ in spec["late"])
    greet(r, c, spec["early"] + late_kinds + (("dp",) if spec["small"] else ()))
    none = [None] * 3
    early = Riders(spec["early"], early_in, early_out, *(early_sems or none))
    late_in = iter(late_in)
    sources = [next(late_in) if src is None else mid_out[src] for _, src in spec["late"]]
    late = Riders(late_kinds, sources, late_out, *(late_sems or none))
    final = Riders(("swap",) * len(after_out), after_out, final_out, *(final_sems or none))
    rows_of = lambda rr, cc: pl.ds(pl.multiple_of((rr * NC + cc) * S, 16), S)

    def partial(rr, cc):
        p = mm(a[rows_of(rr, cc), :], w1[...], 1, 1 if spec["w1_t"] else 0)
        return p if side is None else jnp.concatenate([p, side[rows_of(rr, cc), :].astype(F32)], axis=1)

    def use(rr, cc):
        w = early_out[0][...].reshape(D, -1) if spec["w2"] == "rider" else w2[...]
        u = u_all[rows_of(rr, cc), :D] if u_all.shape[1] > D else u_all[rows_of(rr, cc), :]
        spec["post"](mm(u, w, 1, 1 if spec["w2"] == "in_t" else 0), rows_of(rr, cc), post_out)

    summing = Sum(r, c, partial, sum_bufs)
    gather = Gather(r, c, u_all, S, gather_sems, use if spec["w2"] else None)
    summing2 = None
    summing.to_core()
    early.start()
    summing.to_y()
    if spec["more_sum"]:
        summing2 = Sum(r, c, lambda rr, cc: mm(a2[rows_of(rr, cc), :], v2[...]), sum2_bufs[:16])
    summing.own()
    def advance(h):
        at = pl.ds(h * (S // HALVES), S // HALVES)
        off = pl.multiple_of((r * NC + c) * S + h * (S // HALVES), 16)
        u_all[pl.ds(off, S // HALVES), :] = spec["mid"](total, mid_in, mid_out, at, h)
        gather.pass_on(c, h)

    for h in range(HALVES):
        for j in range(NC):
            summing.step(j, h)
            if h == 0 and j == 1:
                if spec["small"]:
                    early.add()
                if summing2:
                    summing2.to_core()
            if not spec["small"] and j == 1:
                for g in range(h):
                    gather.forward(h - g, (g,))
        summing.last(total, h)
        if not spec["small"]:
            advance(h)
        if h == 0:
            if summing2:
                summing2.to_y()
                summing2.own()
            if not spec["small"]:
                early.add()
    if spec["small"]:
        mine, others, held, dp_s, dp_r, loc = small
        spec["mid"](total, mid_in, mid_out, mine)
        settle = sum_groups(mine, others, held, dp_s, dp_r, 4)
        late.start()
        settle()
        place = pltpu.make_async_copy(held, gather.slab(r, c), loc)
        place.start()
        place.wait()
        gather.begin()
        early.relay()
    else:
        late.start()
    if spec["w2"] == "rider":
        early.relay()
        early.finish()
    if spec["w2"]:
        use(r, c)
    for d in range(1, NC + 2):
        if summing2 and d <= NC:
            for h in range(HALVES):
                summing2.step(d - 1, h)
        if spec["small"]:
            gather.forward(d)
        else:
            for g in reversed(range(HALVES)):
                if HALVES - 1 - g + d <= NC:
                    gather.forward(HALVES - 1 - g + d, (g,))
        gather.uses(d)
        if d == 2 and spec["w2"] != "rider" and not spec["small"]:
            early.relay()
    gather.finish()
    summing.finish()
    if summing2:
        for h in range(HALVES):
            summing2.last(sum2_bufs[16], h)
        spec["after"](sum2_bufs[16], after_in, after_out)
        final.start()
        summing2.finish()
        final.finish()
    late.add()
    late.relay()
    if spec["w2"] != "rider":
        early.finish()
    late.finish()


def link(cid, a, w1, mid, mid_in, mid_out, *, w1_t=False, side=None, w2=None, w2_kind=None, post=None, post_out=(), early=(), early_in=(),
         late=(), late_in=(), extra=0, small=0, more_sum=None, after=None, after_in=(), after_out=()):
    T = a.shape[0]
    D = w1.shape[0] if w1_t else w1.shape[1]
    S = T // (4 * NC)
    W = D + (0 if side is None else side.shape[1])
    width = small or D + extra
    early_shapes, early_sems = rider_parts(early, early_in)
    late_it = iter(late_in)
    late_arrays = [next(late_it) if src is None else jax.ShapeDtypeStruct(*mid_out[src]) for _, src in late]
    late_shapes, late_sems = rider_parts(tuple(k for k, _ in late), late_arrays)
    final_shapes, final_sems = rider_parts(("swap",) * len(after_out), [jax.ShapeDtypeStruct(*o) for o in after_out])
    spec = dict(w1_t=w1_t, side=side is not None, mid=mid, n_mid=len(mid_in), n_mid_out=len(mid_out), w2=w2_kind, post=post,
                n_post=len(post_out), early=tuple(early), late=tuple(late), small=small, more_sum=more_sum is not None,
                after=after, n_after=len(after_in), n_after_out=len(after_out), n_early_sems=len(early_sems), n_late_sems=len(late_sems))
    ins = [a, w1] + ([side] if side is not None else []) + list(mid_in) + ([w2] if w2 is not None else [])
    ins += list(more_sum or ()) + list(after_in)
    riding = list(early_in) + list(late_in)
    in_spaces = [VMEM] * len(ins) + [ANY] * len(riding)
    ins += riding
    outs = [((T, width), BF)] + list(mid_out) + list(post_out)
    outs += list(after_out)
    out_spaces = [VMEM] * len(outs) + [ANY] * len(early_shapes + late_shapes + final_shapes)
    if w2_kind == "rider":
        out_spaces[len(outs)] = VMEM
    outs += [(s.shape, s.dtype) for s in early_shapes + late_shapes + final_shapes]
    scratch = [VMEM((S, W), F32)] + Sum.scratch(S, W) + Gather.scratch()
    if more_sum is not None:
        scratch += Sum.scratch(S, D) + [VMEM((S, D), F32)]
    if small:
        groups = lax.axis_size("dp")
        scratch += [VMEM((S, small), F32), VMEM((groups - 1, S, small), F32), VMEM((S, small), BF), pltpu.SemaphoreType.DMA((groups - 1,)),
                    pltpu.SemaphoreType.DMA((groups - 1,)), pltpu.SemaphoreType.DMA]
    scratch += early_sems + late_sems + final_sems
    return link_call(functools.partial(link_kernel, spec), cid, ins, in_spaces, outs, out_spaces, scratch, 8 << 30)


EPS = 1e-05


def norm_scale(x):
    return lax.rsqrt(jnp.mean(x * x, axis=1, keepdims=True) + EPS)


def norm_grad(x, gain, up, gain_grad, h):
    s = norm_scale(x)
    own = jnp.sum(x * s * up, axis=0, keepdims=True)
    gain_grad[0:1] = own if h == 0 else gain_grad[0:1] + own
    tilted = up * gain
    return s * tilted - x * (s * s * s * jnp.mean(x * tilted, axis=1, keepdims=True))


def mid_mixer(inner, total, ins, outs, at, h):
    h0, gain = ins
    h1, mix_out, gate_scale = outs
    D = h0.shape[1]
    s = lax.rsqrt(total[at, D:D + 1] / inner + EPS)
    out = total[at, :D] * s
    mix_out[at] = out
    gate_scale[at] = jnp.broadcast_to(s, (out.shape[0], gate_scale.shape[1]))
    x = h0[at].astype(F32) + out
    h1[at] = x
    return (x * norm_scale(x) * gain[...]).astype(BF)


def mid_attention(total, ins, outs, at, h):
    h1, gain = ins
    x = h1[at] + total[at]
    outs[0][at] = x
    return (x * norm_scale(x) * gain[...]).astype(BF)


def mid_ff_back(total, ins, outs, at, h):
    h2, gain, grad = ins
    dh2, gain_grad = outs
    d = grad[at].astype(F32) + norm_grad(h2[at], gain[...], total[at], gain_grad, h)
    dh2[at] = d
    return d.astype(BF)


def mid_att_back(inner, total, ins, outs, at, h):
    h1, gain, dh2, mix_out, gate_scale = ins
    dh1, gain_grad = outs
    d = dh2[at] + norm_grad(h1[at], gain[...], total[at], gain_grad, h)
    dh1[at] = d
    s = gate_scale[at, 0:1]
    tilt = s * s * jnp.sum(d * mix_out[at], axis=1, keepdims=True) / inner
    high = tilt.astype(BF).astype(F32)
    lane = lax.broadcasted_iota(jnp.int32, (d.shape[0], 128), 1)
    return jnp.concatenate([d * s, jnp.where(lane < 64, high, tilt - high)], axis=1).astype(BF)


def mid_mixer_back(total, ins, outs, small):
    h0, gain, dh1 = ins
    in_slab, gain_grad = outs
    D = h0.shape[1]
    thin = small.shape[1]
    four = D // thin
    d = dh1[...] + norm_grad(h0[...].astype(F32), gain[...], total[:, :D], gain_grad, 0)
    feat = D // NC
    for i in range(NC):
        in_slab[i] = d[:, i * feat:(i + 1) * feat].astype(BF)
    rest = total[:, D:]
    small[...] = jnp.zeros_like(small)
    small[:SMALL] = rest[:SMALL]
    own = rest[SMALL:SMALL + four] + rest[SMALL + four:SMALL + 2 * four]
    row = gain_grad[0:1]
    for i in range(3):
        small[SMALL + i * four:SMALL + (i + 1) * four] = own
        for j in range(four):
            at = SMALL + (3 + i) * four + j
            small[at:at + 1] = row[:, j * thin:(j + 1) * thin]


def after_output(total, ins, outs):
    h2, valid = ins
    x = (h2[...] + total[...]) * valid[:, 0:1]
    feat = x.shape[1] // NC
    for i in range(NC):
        outs[0][i] = x[:, i * feat:(i + 1) * feat].astype(BF)


def post_plain(p, at, outs):
    outs[0][at, :] = p.astype(outs[0].dtype)


def post_gelu(p, at, outs):
    outs[0][at, :] = p
    outs[1][at, :] = (0.5 * p * (1.0 + jnp.tanh(0.7978845608028654 * (p + 0.044715 * (p * p * p))))).astype(BF)


def finish_kernel(zx, mix, qkv, o, ff, rest, x_g, z_g, q_g, k_g, v_g, mix_g, o_g, up_g, down_g, bcdt_g, small, gain):
    i = pl.program_id(0)
    rows, part = zx.shape[2], ff.shape[2] // 2
    for h in range(2):
        at = slice(h * rows, (h + 1) * rows)
        piece = zx[0, h].astype(F32)
        x_new, z_new = piece[:, :WIDE], piece[:, WIDE:]
        three = qkv[0, h].astype(F32)
        for j in range(NC):
            @pl.when(i == j)
            def _():
                x_g[at, j * WIDE:(j + 1) * WIDE] = x_new
                z_g[at, j * WIDE:(j + 1) * WIDE] = z_new
                to = slice((j // 2) * WIDE, (j // 2 + 1) * WIDE)
                for n, out in enumerate((q_g, k_g, v_g)):
                    new = three[:, n * WIDE:(n + 1) * WIDE]
                    out[at, to] = new if j % 2 == 0 else out[at, to] + new
        half = mix.shape[2]
        mix_g[h * half:(h + 1) * half] = mix[0, h].astype(F32)
        o_at = slice(h * half, (h + 1) * half)

        @pl.when(i % 2 == 0)
        def _():
            o_g[o_at] = o[0, h].astype(F32)

        @pl.when(i % 2 == 1)
        def _():
            o_g[o_at] += o[0, h].astype(F32)
        down_g[h * part:(h + 1) * part] = ff[0, h, :part].astype(F32)
        up_g[h * part:(h + 1) * part] = ff[0, h, part:].astype(F32)
    wide = bcdt_g.shape[1]

    @pl.when(i == 0)
    def _():
        gain[...] = jnp.zeros_like(gain)
    for j in range(NC):
        slab = rest[j].astype(F32)
        bcdt_g[j * SMALL:(j + 1) * SMALL] = slab[:SMALL, :wide]
        tail = slab[SMALL:SMALL + 24]
        small[j] = tail[0:4] + tail[4:8] + tail[8:12]
        gain[0:4] += tail[12:16] + tail[16:20] + tail[20:24]


def finish(zx, mix, qkv, o, ff, rest, bcdt_width):
    thin, feat = rest.shape[2], zx.shape[3]
    D = NC * feat
    lead = lambda a: pl.BlockSpec((1,) + a.shape[1:], lambda i: (i, 0, 0, 0))
    whole = lambda r, w: pl.BlockSpec((r, w), lambda i: (0, 0))
    sds = lambda *s: jax.ShapeDtypeStruct(s, F32)
    rows, half, part = 2 * zx.shape[2], 2 * mix.shape[2], ff.shape[2]
    return pl.pallas_call(
        finish_kernel,
        grid=(NC,),
        in_specs=[lead(zx), lead(mix), lead(qkv), lead(o), lead(ff), pl.BlockSpec((NC,) + rest.shape[1:], lambda i: (i, 0, 0))],
        out_specs=[whole(rows, NC * WIDE)] * 2 + [whole(rows, 2 * WIDE)] * 3 + [
            pl.BlockSpec((half, feat), lambda i: (i, 0)), pl.BlockSpec((half, feat), lambda i: (i // 2, 0)),
            pl.BlockSpec((part, feat), lambda i: (0, i)), pl.BlockSpec((part, feat), lambda i: (i, 0)),
            pl.BlockSpec((NC * SMALL, bcdt_width), lambda i: (i, 0)), pl.BlockSpec((NC, 4, thin), lambda i: (i, 0, 0)), whole(8, thin)],
        out_shape=[sds(rows, NC * WIDE)] * 2 + [sds(rows, 2 * WIDE)] * 3 + [
            sds(NC * half, feat), sds(2 * half, feat), sds(part, NC * feat), sds(NC * part, feat), sds(D, bcdt_width),
            sds(rest.shape[0], 4, thin), sds(8, thin)],
        compiler_params=pltpu.CompilerParams(vmem_limit_bytes=62 << 20, dimension_semantics=("arbitrary",)),
        cost_estimate=pl.CostEstimate(flops=1 << 20, bytes_accessed=24 << 20, transcendentals=0),
    )(zx, mix, qkv, o, ff, rest)


def side_kernel(in_grad, taps, rows, gain2, gain3, zx, side, small):
    i = pl.program_id(0)
    slab = lax.axis_index("rows") * NC + lax.axis_index("cols")
    thin = side.shape[2]
    lane = lax.broadcasted_iota(jnp.int32, (1, thin), 1)

    @pl.when(i == 0)
    def _():
        small[...] = jnp.zeros_like(small)
        for n, g in enumerate((gain2, gain3)):
            for q in range(4):
                small[n, q:q + 1] = g[0:1, q * thin:(q + 1) * thin]

        def channels(first, v):
            both = jnp.concatenate([v, v], axis=1)
            small[first + (slab >> 3), pl.ds((slab & 7) >> 1, 1)] = jnp.where(lane // WIDE == (slab & 1), both, 0.0)

        def heads(at, v):
            placed = sum(jnp.where(lane == slab * 3 + h, v[:, h:h + 1], 0.0) for h in range(3))
            small[15, at:at + 1] = placed
        none = jnp.zeros((1, thin - 2 * STATE), F32)
        for t in range(CONV):
            channels(2 + 2 * t, taps[t:t + 1, 2 * STATE:])
            small[14, t:t + 1] = jnp.concatenate([taps[t:t + 1, :2 * STATE], none], axis=1)
        channels(10, taps[CONV:CONV + 1, 2 * STATE:])
        channels(12, rows[0:1, :WIDE])
        small[15, 0:1] = jnp.concatenate([taps[CONV:CONV + 1, :2 * STATE], none], axis=1)
        heads(1, rows[3:4, :128])
        heads(2, head_sums(jnp.broadcast_to(rows[1:2, :WIDE], (8, WIDE)))[0:1])
        heads(3, rows[2:3, :128])
    p = in_grad[...]
    half = p.shape[0] // 2
    for h in range(2):
        zx[0, h] = p[h * half:(h + 1) * half, 2 * STATE:2 * STATE + 2 * WIDE].astype(BF)
    at = lax.broadcasted_iota(jnp.int32, (p.shape[0], 128), 1)
    dts = sum(jnp.where(at == slab * 3 + h, p[:, MIX + WIDE + h:MIX + WIDE + h + 1], 0.0) for h in range(3))
    state = jnp.concatenate([p[:, :2 * STATE], dts], axis=1).astype(BF)
    for j in range(NC):
        side[j, :SMALL] = state[j * SMALL:(j + 1) * SMALL]
        own = small[i * NC + j]
        rest = own - own.astype(BF).astype(F32)
        side[j, SMALL:] = jnp.concatenate([own, rest, jnp.zeros((side.shape[1] - SMALL - 8, thin), F32)], axis=0).astype(BF)


def side_columns(in_grad, taps, rows, gain2, gain3, S):
    D, cols = in_grad.shape
    feat, thin = D // NC, cols - 2 * WIDE
    whole = lambda a: pl.BlockSpec(a.shape, lambda i: (0, 0))
    return pl.pallas_call(
        side_kernel,
        grid=(NC,),
        in_specs=[pl.BlockSpec((feat, cols), lambda i: (i, 0)), whole(taps), whole(rows), whole(gain2), whole(gain3)],
        out_specs=[pl.BlockSpec((1, 2, feat // 2, 2 * WIDE), lambda i: (i, 0, 0, 0)), pl.BlockSpec((NC, S, thin), lambda i: (i, 0, 0))],
        out_shape=[jax.ShapeDtypeStruct((NC, 2, feat // 2, 2 * WIDE), BF), jax.ShapeDtypeStruct((4 * NC, S, thin), BF)],
        scratch_shapes=[pltpu.VMEM((4 * NC, 4, thin), F32)],
        compiler_params=pltpu.CompilerParams(vmem_limit_bytes=32 << 20, dimension_semantics=("arbitrary",)),
        cost_estimate=pl.CostEstimate(flops=1 << 20, bytes_accessed=8 << 20, transcendentals=0),
    )(in_grad, taps, rows, gain2, gain3)


P = jax.sharding.PartitionSpec


def dot(a, b):
    return jnp.dot(a, b, preferred_element_type=F32)


def dot_t(a, b):
    return lax.dot_general(a, b, (((1,), (1,)), ((), ())), preferred_element_type=F32)


def t_dot(a, b):
    return lax.dot_general(a, b, (((0,), (0,)), ((), ())), preferred_element_type=F32)


def split_in(w):
    d, n = w.shape
    return w.reshape(d, NC, n // NC).transpose(1, 0, 2)


def halves_of(w):
    d, n = w.shape
    return w.reshape(d, 2, n // 2).transpose(1, 0, 2)


def whole_out(got):
    return got.transpose(1, 0, 2).reshape(got.shape[1], -1)


def split_grad(g):
    n, d = g.shape
    return g.astype(BF).reshape(n, NC, d // NC).transpose(1, 0, 2)


def per_device(hidden_in, lengths, norm1_gain, z_weight, x_weight, bcdt_weight, conv_x_weight, conv_x_bias,
               conv_bc_weight, conv_bc_bias, a_log, d_skip, dt_bias, gate_gain, mix_out_weight, norm2_gain,
               q_weight, k_weight, v_weight, att_out_weight, norm3_gain, up_weight, down_weight, grad_output):
    r, c = lax.axis_index("rows"), lax.axis_index("cols")
    rows = lax.axis_size("rows")
    tok_rows, feat = hidden_in.shape
    T, D = tok_rows * rows, feat * NC
    S = T // (rows * NC)
    slab = r * NC + c
    inner = z_weight.shape[1] * rows
    wide = z_weight.shape[1] // NC
    heads_row = a_log.shape[0]
    heads = heads_row // NC
    n_heads = heads_row * rows
    seq_lens = lengths[0]
    places = jnp.arange(T, dtype=jnp.int32)
    one_f32, row8 = ((S, D), F32), ((8, D), F32)
    valid = (places < seq_lens[0] + seq_lens[1]).astype(F32)
    my_valid = lax.dynamic_slice_in_dim(valid, slab * S, S, 0)[:, None]
    pad = 128

    pair = "swap2" if lax.axis_size("dp") == 2 else "swap"

    def halved(a):
        return a.reshape(a.shape[0], 2, -1, a.shape[2]) if pair == "swap2" else a

    def joined(a):
        return a.reshape(a.shape[0], -1, a.shape[-1])

    zx_pieces = halved(jnp.concatenate([split_in(x_weight), split_in(z_weight)], axis=2))
    mix_pieces = halved(mix_out_weight.reshape(NC, -1, feat))
    bcdt_width = bcdt_weight.shape[1]
    bcdt_pad = -bcdt_width % 128
    bcdt_piece = jnp.pad(bcdt_weight, ((0, 0), (0, bcdt_pad))).reshape(2, feat // 2, -1)
    gain_piece = jnp.broadcast_to(jnp.pad(jnp.stack([norm1_gain, norm2_gain, norm3_gain]), ((0, 5), (0, 0)))[None], (2, 8, feat))
    here = lax.dynamic_slice_in_dim(valid, r * tok_rows, tok_rows, 0)[:, None]
    grad = (grad_output.astype(F32) * here).astype(BF).reshape(NC, S, feat)
    hidden_all, g3, h0, w_zx, mix_got, w_bcdt, gains = entry(
        0, hidden_in, grad, (pair, pair, "bcast2", "bcast2"), (zx_pieces, mix_pieces, bcdt_piece, gain_piece))
    g3_mine = lax.dynamic_slice_in_dim(g3, slab * S, S, 0)
    w_mix = whole_out(joined(mix_got))
    gains = gains[:, 0, :3].transpose(1, 0, 2).reshape(3, D)
    w_bcdt, w_zx = w_bcdt.reshape(D, -1), w_zx.reshape(D, 2 * wide)
    w_dt = jnp.pad(lax.dynamic_slice_in_dim(w_bcdt, 2 * STATE + slab * heads, heads, 1), ((0, 0), (0, 128 - heads)))
    w_in = jnp.concatenate([w_bcdt[:, :2 * STATE], w_zx, w_dt], axis=1)
    few = pair == "swap2"
    twice = lambda a: a if few else jnp.repeat(a, NC // 2, axis=0)
    one_way = "swaph" if few else "swap"
    qkv_pieces = halved(twice(jnp.concatenate([halves_of(q_weight), halves_of(k_weight), halves_of(v_weight)], axis=2)))
    o_pieces = halved(twice(att_out_weight.reshape(2, -1, feat)))

    mine = lambda a, n: lax.dynamic_slice_in_dim(a, c * n, n, a.ndim - 1)
    cw = jnp.concatenate([conv_bc_weight, mine(conv_x_weight, wide)], axis=1)
    cw = jnp.concatenate([cw, jnp.concatenate([conv_bc_bias, mine(conv_x_bias, wide)])[None], jnp.zeros((3, MIX), F32)])
    wide_row = lambda a: jnp.pad(a, (0, 256 - a.shape[0]))[None]
    pv = jnp.concatenate([wide_row(mine(gate_gain, wide)), wide_row(jnp.repeat(mine(d_skip, heads), HEAD_DIM)),
                          wide_row(mine(dt_bias, heads)), wide_row(-jnp.exp(mine(a_log, heads))), jnp.zeros((4, 256), F32)])
    u1, proj, mixg, squares, y, states, qkv_split = mixer_fwd(
        6, seq_lens, hidden_all.reshape(rows, NC, tok_rows, feat), gains[0:1], w_bcdt, w_zx, w_dt, cw, pv,
        (one_way,), (qkv_pieces,))
    att3 = qkv_pieces.shape[-1]
    u2, h1, mix_out, gate_scale, qkv, qkv_got, o_split, down_split = link(
        1, mixg, w_mix, functools.partial(mid_mixer, inner), (h0, gains[1:2]), (one_f32, one_f32, ((S, 128), F32)), side=squares,
        w2_kind="rider", post=post_plain, post_out=(((T, att3), BF),), early=("spread",), early_in=(qkv_split,), late=((one_way, None), (one_way, None)),
        late_in=(o_pieces, halved(down_weight.reshape(NC, -1, feat))))
    w_qkv = qkv_got.reshape(D, -1)
    att = att3 // 3

    attended, att_exact, lse, up_split, o_got = att_fwd(
        7, seq_lens, qkv, (one_way, "spread"), (halved(split_in(up_weight)), o_split))
    w_o = whole_out(joined(o_got))
    hidden_units = up_weight.shape[1] // NC
    u3, h2, act, hid, up_got, down_got = link(
        2, attended, w_o, mid_attention, (h1, gains[2:3]), (one_f32,), w2_kind="rider", post=post_gelu,
        post_out=(((T, hidden_units), F32), ((T, hidden_units), BF)), early=("spread",), early_in=(up_split,),
        late=(("spread", None),), late_in=(down_split,))
    w_up, w_down = up_got.reshape(D, -1), whole_out(joined(down_got))
    gelu_back = jax.vjp(functools.partial(jax.nn.gelu, approximate=True), act)[1]

    reduce = "reduce" if few else "swap"

    def added(pieces, got):
        if not few:
            return lax.psum(pieces, "dp")
        own = lax.dynamic_index_in_dim(pieces, lax.axis_index("dp"), 1, False)
        return (own.astype(F32) + got[0].astype(F32)).astype(BF)

    x_kinds = lambda n: ("half",) * n if few else ()
    x_arrays = lambda *arrays: arrays if few else ()
    d_act = gelu_back(dot_t(g3, w_down))[0].astype(BF)
    down_pieces = halved(split_grad(t_dot(hid, g3)))
    up_pieces = halved(t_dot(u3, d_act).astype(BF).reshape(NC, feat, -1))
    g2, dh2, gain3_rows, d_att, *got = link(
        3, d_act, w_up, mid_ff_back, (h2, gains[2:3], g3_mine), (one_f32, row8), w1_t=True, w2=w_o, w2_kind="in_t", post=post_plain,
        post_out=(((T, att), BF),), early=x_kinds(2), early_in=x_arrays(down_pieces, up_pieces))
    ff_sum = jnp.concatenate([added(down_pieces, got[:1]), added(up_pieces, got[1:])], axis=1)
    o_pieces = halved(split_grad(t_dot(attended, g2)))
    d_qkv, ff_split = att_bwd(8, seq_lens, qkv, d_att, att_exact, lse, ("swap",), (ff_sum,))
    qkv_pieces = halved(t_dot(u2, d_qkv).astype(BF).reshape(NC, feat, -1))
    g1_ext, dh1, gain2_rows, d_mix, ff_back, *got = link(
        4, d_qkv, w_qkv, functools.partial(mid_att_back, inner), (h1, gains[1:2], dh2, mix_out, gate_scale), (one_f32, row8), w1_t=True,
        w2=w_mix, w2_kind="in_t", post=post_plain, post_out=(((T, wide), F32),), extra=128,
        early=("spread",) + x_kinds(2), early_in=(ff_split,) + x_arrays(o_pieces, qkv_pieces))
    o_sum, qkv_sum = added(o_pieces, got[:1]), added(qkv_pieces, got[1:])
    g1 = g1_ext[:, :D]
    mix_pieces = halved(split_grad(t_dot(mixg, g1)))
    d_in, tap_grads, row_grads, o_split, qkv_split = mixer_bwd(
        9, seq_lens, proj, cw, pv, y, states, d_mix, g1_ext, ("swap", "swap"), (o_sum, qkv_sum))
    in_grad = t_dot(u1, d_in)
    slabs, thin = rows * NC, bcdt_width + bcdt_pad
    four = D // thin
    zx_pieces, side = side_columns(in_grad, tap_grads, row_grads, gain2_rows, gain3_rows, S)
    zx_pieces = zx_pieces if few else zx_pieces.reshape(NC, feat, -1)
    rest_all, _, _, _, zx_back, mix_back, o_back, qkv_back, in_got, out_got = link(
        5, d_in, w_in, mid_mixer_back, (h0, gains[0:1], dh1), (((NC, S, feat), BF), row8), w1_t=True, side=side.reshape(T, thin), small=thin,
        early=(reduce, reduce, "spread", "spread"), early_in=(zx_pieces, mix_pieces, o_split, qkv_split), late=(("swap", 0),),
        more_sum=(hid, w_down), after=after_output, after_in=(h2, jnp.broadcast_to(my_valid, (S, 128))), after_out=(((NC, S, feat), BF),))
    output = out_got.reshape(NC * S, feat)
    four_d = lambda a: a if few else a.reshape(NC, 2, -1, a.shape[-1])
    if not few:
        n = ff_back.shape[1] // 2
        ff_back = jnp.concatenate([four_d(ff_back[:, :n]), four_d(ff_back[:, n:])], axis=2)
        zx_back, mix_back = lax.psum(zx_back, "dp"), lax.psum(mix_back, "dp")
    (x_grad, z_grad, q_grad, k_grad, v_grad, mix_grad, o_grad, up_grad, down_grad, bcdt_grad, small, gain1) = finish(
        four_d(zx_back), four_d(mix_back), four_d(qkv_back), four_d(o_back), ff_back, rest_all.reshape(slabs, S, thin), bcdt_width)
    gain1_grad = gain1[:4].reshape(D)
    cxw_sum = small[2:10].reshape(CONV, inner)
    cxb_sum, gate_gain_sum = small[10:12].reshape(-1), small[12:14].reshape(-1)
    cbw_sum, cbb_sum = small[14, :, :2 * STATE], small[15, 0, :2 * STATE]
    a_log_sum, d_skip_sum, dt_bias_sum = small[15, 1, :n_heads], small[15, 2, :n_heads], small[15, 3, :n_heads]
    input_grad = in_got.reshape(NC * S, feat).astype(F32)
    return (output, input_grad, gain1_grad, z_grad, x_grad, bcdt_grad, cxw_sum, cxb_sum, cbw_sum, cbb_sum, a_log_sum, d_skip_sum,
            dt_bias_sum, gate_gain_sum, mix_grad, small[0].reshape(D), q_grad, k_grad, v_grad, o_grad, small[1].reshape(D), up_grad, down_grad)


def solution(mesh):
    assert mesh.shape["rows"] == 4 and mesh.shape["cols"] == NC
    token = P(("dp", "rows"), "cols")
    w_in, w_out = P("cols", "rows"), P("rows", "cols")
    row, col, whole = P("rows"), P("cols"), P()
    placed = (token, P("dp", None), col, w_in, w_in, P("cols", None), P(None, "rows"), row, whole, whole, row, row, row, row,
              w_out, col, w_in, w_in, w_in, w_out, col, w_in, w_out, token)
    given = (token, token, whole, w_in, w_in, whole, whole, whole, whole, whole, whole, whole, whole, whole, w_out, whole,
             w_in, w_in, w_in, w_out, whole, w_in, w_out)
    return jax.shard_map(per_device, mesh=mesh, in_specs=placed, out_specs=given, check_vma=False)
```

```python
import functools
import jax, jax.numpy as jnp
from jax import lax
from jax.experimental import pallas as pl
from jax.experimental.pallas import tpu as pltpu
MESH = pl.DeviceIdType.MESH
NC = 4
F32, BF = jnp.float32, jnp.bfloat16


def copy_to(src, dst, send, recv, dev):
    return pltpu.make_async_remote_copy(src_ref=src, dst_ref=dst, send_sem=send, recv_sem=recv, device_id=dev, device_id_type=MESH)


def greet(r, c, kinds=(), partners=True):
    barrier = pltpu.get_barrier_semaphore()
    all_cols = any(kind not in ("dp", "half", "spread") for kind in kinds)
    count = 0
    if partners:
        pl.semaphore_signal(barrier, inc=1, device_id={"rows": r ^ 1}, device_id_type=MESH)
        pl.semaphore_signal(barrier, inc=1, device_id={"rows": r ^ 2}, device_id_type=MESH)
        count = 2
    if all_cols:
        for s in range(1, NC):
            pl.semaphore_signal(barrier, inc=1, device_id={"cols": lax.rem(c + s, NC)}, device_id_type=MESH)
        count += NC - 1
    elif partners:
        @pl.when(c > 0)
        def _():
            pl.semaphore_signal(barrier, inc=1, device_id={"cols": c - 1}, device_id_type=MESH)

        @pl.when(c < NC - 1)
        def _():
            pl.semaphore_signal(barrier, inc=1, device_id={"cols": c + 1}, device_id_type=MESH)
        count = count + jnp.where(c > 0, 1, 0) + jnp.where(c < NC - 1, 1, 0)
    if any(kind in ("dp", "swap2", "half", "spread", "reduce") for kind in kinds):
        groups = lax.axis_size("dp")
        for s in range(1, groups):
            pl.semaphore_signal(barrier, inc=1, device_id={"dp": lax.rem(lax.axis_index("dp") + s, groups)}, device_id_type=MESH)
        count = count + groups - 1
    pl.semaphore_wait(barrier, count)


class Riders:
    def __init__(self, kinds, ins, outs, send, recv, loc, *held):
        r, c, g = lax.axis_index("rows"), lax.axis_index("cols"), lax.axis_index("dp")
        groups = lax.axis_size("dp")
        self.remote, self.local, self.late, self.sums = [], [], [], []
        held = iter(held)
        for e, kind in enumerate(kinds):
            src, dst = ins[e], outs[e]
            if kind == "half":
                self.remote.append(copy_to(src.at[:, 1 - g], dst, send.at[e, 0], recv.at[e, 0], {"dp": 1 - g}))
                continue
            if kind == "spread":
                place = dst.at[:, g] if groups == 2 else dst
                self.local.append(pltpu.make_async_copy(src, place, loc.at[e]))
                if groups == 2:
                    self.remote.append(copy_to(src, place, send.at[e, 0], recv.at[e, 0], {"dp": 1 - g}))
                continue
            if kind == "swaph":
                few = src.shape[0] != NC
                piece = lambda to, few=few, src=src: src.at[to >> 1 if few else to, g]
                for s in range(1, NC):
                    to = lax.rem(c + s, NC)
                    self.remote.append(copy_to(piece(to), dst.at[c], send.at[e, s - 1], recv.at[e, s - 1], {"cols": to}))
                self.local.append(pltpu.make_async_copy(piece(c), dst.at[c], loc.at[e]))
                continue
            if kind == "dp":
                for s in range(1, groups):
                    self.remote.append(copy_to(src, dst.at[s - 1], send.at[e, s - 1], recv.at[e, s - 1], {"dp": lax.rem(g + s, groups)}))
                continue
            if kind == "swap":
                for s in range(1, NC):
                    to = lax.rem(c + s, NC)
                    self.remote.append(copy_to(src.at[to], dst.at[c], send.at[e, s - 1], recv.at[e, s - 1], {"cols": to}))
                self.local.append(pltpu.make_async_copy(src.at[c], dst.at[c], loc.at[e]))
                continue
            half = r & 1 if kind == "bcast2" else g
            other = {"rows": r ^ 1} if kind == "bcast2" else {"dp": 1 - g}
            pairs = []
            if kind == "reduce":
                own, got = next(held), next(held)
                first = copy_to(src.at[:, 1 - g], got, send.at[e, 2 * NC - 1], recv.at[e, 2 * NC - 1], other)
                self.sums.append((first, pltpu.make_async_copy(src.at[:, g], own, loc.at[e]), own, got, pairs))
                piece = lambda to, own=own: own.at[to]
                keep = pltpu.make_async_copy(own.at[c], dst.at[c, g], loc.at[e])
                pairs.append((None, keep, copy_to(own.at[c], dst.at[c, g], send.at[e, NC - 1], recv.at[e, NC - 1], other)))
            elif kind == "swap2":
                few = src.shape[0] != NC
                piece = lambda to, few=few, src=src, half=half: src.at[to >> 1 if few else to, half]
                self.local.append(pltpu.make_async_copy(src.at[c >> 1 if few else c], dst.at[c], loc.at[e]))
            else:
                piece = lambda to, src=src, half=half: src.at[half]
                self.local.append(pltpu.make_async_copy(src, dst.at[c], loc.at[e]))
            for s in range(1, NC):
                to, came = lax.rem(c + s, NC), lax.rem(c + NC - s, NC)
                first = copy_to(piece(to), dst.at[c, half], send.at[e, s - 1], recv.at[e, s - 1], {"cols": to})
                pairs.append((first, None, copy_to(dst.at[came, half], dst.at[came, half], send.at[e, NC + s - 1], recv.at[e, NC + s - 1], other)))
            if kind != "reduce":
                self.late.extend(pairs)

    def start(self):
        for first, keep, own, got, pairs in self.sums:
            first.start()
            keep.start()
        for first, _, _ in self.late:
            first.start()
        for one in self.remote + self.local:
            one.start()

    def add(self):
        for first, keep, own, got, pairs in self.sums:
            keep.wait()
            first.wait()
            own[...] = (own[...].astype(F32) + got[...].astype(F32)).astype(BF)
            for one, local, second in pairs:
                if one is None:
                    local.start()
                    second.start()
                else:
                    one.start()

    def relay(self):
        for first, _, second in self.late + [p for one in self.sums for p in one[4] if p[0] is not None]:
            first.wait_recv()
            second.start()

    def finish(self):
        for one in self.remote + self.local:
            one.wait()
        for first, local, second in self.late + [p for one in self.sums for p in one[4]]:
            if first is None:
                local.wait()
            else:
                first.wait_send()
            second.wait()


def rider_parts(kinds, arrays):
    groups = lax.axis_size("dp")
    shapes = []
    for kind, a in zip(kinds, arrays):
        if kind == "swap2":
            a = jax.ShapeDtypeStruct((NC,) + a.shape[1:], a.dtype)
        if kind in ("half", "swaph"):
            a = jax.ShapeDtypeStruct((NC,) + a.shape[2:], a.dtype)
        if kind == "spread":
            a = jax.ShapeDtypeStruct((NC,) + (2,) * (groups == 2) + a.shape[1:], a.dtype)
        lead = {"swap": (), "swap2": (), "half": (), "swaph": (), "spread": (), "reduce": (), "bcast2": (NC,), "dp": (groups - 1,)}[kind]
        shapes.append(jax.ShapeDtypeStruct(lead + a.shape, a.dtype))
    n, most = len(kinds), max(2 * NC, groups)
    sems = [pltpu.SemaphoreType.DMA((n, most)), pltpu.SemaphoreType.DMA((n, most)), pltpu.SemaphoreType.DMA((n,))] if n else []
    for kind, a in zip(kinds, arrays):
        if kind == "reduce":
            sems += [pltpu.VMEM(a.shape[:1] + a.shape[2:], a.dtype)] * 2
    return shapes, sems


SMALL = 96


def sum_groups(x_ref, others, held, dp_s, dp_r, n):
    g, groups = lax.axis_index("dp"), lax.axis_size("dp")
    copies = [copy_to(x_ref, others.at[s - 1], dp_s.at[s - 1], dp_r.at[s - 1], {"dp": lax.rem(g + s, groups)}) for s in range(1, groups)]
    for one in copies:
        one.start()

    def settle():
        total = x_ref[...]
        for s, one in enumerate(copies):
            one.wait()
            total = total + others[s]
        part = (lax.broadcasted_iota(jnp.int32, total.shape, 0) - SMALL) // n
        rest = total - total.astype(BF).astype(F32)
        rest2 = rest - rest.astype(BF).astype(F32)
        second, third = (part == 1) | (part == 4), (part == 2) | (part == 5)
        held[...] = jnp.where(second, rest, jnp.where(third, rest2, total)).astype(BF)
    return settle


def ridden(kernel, n_in, n_out, kinds):
    n = len(kinds)

    def run(*refs):
        ins, rest = refs[:n_in], refs[n_in + n:]
        outs, tail = rest[:n_out], rest[n_out + n:]
        riding = Riders(kinds, refs[n_in:n_in + n], rest[n_out:n_out + n], *tail[-3:])
        step = pl.program_id(0)

        @pl.when(step == 0)
        def _():
            greet(lax.axis_index("rows"), lax.axis_index("cols"), kinds, False)
            riding.start()
        kernel(*ins, *outs, *tail[:-3])

        @pl.when(step == pl.num_programs(0) - 1)
        def _():
            riding.finish()
    return run


def ridden_call(kernel, cid, grid, ins, in_specs, outs, out_specs, scratch, flops, kinds, arrays):
    shapes, sems = rider_parts(kinds, arrays)
    any_space = [pl.BlockSpec(memory_space=pl.ANY)] * len(kinds)
    return pl.pallas_call(
        ridden(kernel, len(ins), len(outs), tuple(kinds)),
        grid=(grid,),
        in_specs=list(in_specs) + any_space,
        out_specs=list(out_specs) + any_space,
        out_shape=[jax.ShapeDtypeStruct(*o) for o in outs] + shapes,
        scratch_shapes=list(scratch) + sems,
        compiler_params=pltpu.CompilerParams(collective_id=cid, has_side_effects=True, vmem_limit_bytes=56 << 20,
                                             dimension_semantics=("arbitrary",)),
        cost_estimate=pl.CostEstimate(flops=flops, bytes_accessed=24 << 20, transcendentals=4 << 20),
    )(*ins, *arrays)


HEAD_DIM = 64
STATE = 128
CONV = 4
SPAN = 256
WIDE = 192
MIX = 2 * STATE + WIDE


def mm(a, b, ca=1, cb=0):
    return lax.dot_general(a.astype(BF), b.astype(BF), (((ca,), (cb,)), ((), ())), preferred_element_type=F32)


def by_parts(a, mask, ca, cb, parts, mask_first=False):
    total = None
    for _ in range(parts):
        high = a.astype(BF)
        one = mm(mask, high, ca, cb) if mask_first else mm(high, mask, ca, cb)
        total = one if total is None else total + one
        a = a - high.astype(F32)
    return total


def seg_at(place, l0, l1):
    return jnp.where(place < 0, -1, jnp.where(place >= l0, 1, 0) + jnp.where(place >= l0 + l1, 1, 0))


def sigmoid(x):
    return 1.0 / (1.0 + jnp.exp(-x))


def by_head(a, lane):
    return jnp.where(lane < HEAD_DIM, a[:, 0:1], jnp.where(lane < 2 * HEAD_DIM, a[:, 1:2], a[:, 2:3]))


def head_sums(a):
    i = lax.broadcasted_iota(jnp.int32, (WIDE, 128), 0)
    j = lax.broadcasted_iota(jnp.int32, (WIDE, 128), 1)
    return by_parts(a, jnp.where(i // HEAD_DIM == j, 1.0, 0.0), 1, 0, 2)


class Block:
    def __init__(self, blk, lens, proj, before, cw, pv):
        self.l0, self.l1 = lens[0], lens[1]
        self.start = blk * SPAN
        v = proj[:, :MIX]
        self.place = self.start + lax.broadcasted_iota(jnp.int32, (SPAN, 1), 0)
        self.seg = seg_at(self.place, self.l0, self.l1)
        ext = jnp.concatenate([before[:, :MIX], v], axis=0)
        acc = cw[4:5] + cw[3:4] * v
        self.shifted = [v]
        for s in range(1, CONV):
            keep = jnp.where(seg_at(self.place - s, self.l0, self.l1) == self.seg, 1.0, 0.0)
            moved = ext[8 - s:8 - s + SPAN] * keep
            self.shifted.append(moved)
            acc = acc + cw[3 - s:4 - s] * moved
        self.acc = acc
        self.gate = sigmoid(acc)
        act = acc * self.gate
        self.b, self.c, self.x = act[:, :STATE], act[:, STATE:2 * STATE], act[:, 2 * STATE:]
        self.z = proj[:, MIX:MIX + WIDE]
        self.zs = sigmoid(self.z)
        self.raw = proj[:, MIX + WIDE:] + pv[2:3, :128]
        self.dt = jnp.maximum(self.raw, 0.0) + jnp.log1p(jnp.exp(-jnp.abs(self.raw)))
        self.rate = pv[3:4, :128] * self.dt
        i = lax.broadcasted_iota(jnp.int32, (SPAN, SPAN), 0)
        j = lax.broadcasted_iota(jnp.int32, (SPAN, SPAN), 1)
        self.low = jnp.where(j <= i, 1.0, 0.0).astype(F32)
        self.cum = by_parts(self.rate, self.low, 1, 0, 3, True)
        self.cum_t = self.cum.T
        seg_row = seg_at(self.start + lax.broadcasted_iota(jnp.int32, (1, SPAN), 1), self.l0, self.l1)
        self.allowed = (j <= i) & (seg_row == self.seg)
        self.scores = mm(self.c, self.b, 1, 1)
        self.lane = lax.broadcasted_iota(jnp.int32, (SPAN, WIDE), 1)
        self.w = self.x * by_head(self.dt, self.lane)
        prior = seg_at(self.start - 1, self.l0, self.l1)
        last = seg_at(self.start + SPAN - 1, self.l0, self.l1)
        end = self.cum[SPAN - 1:SPAN]
        self.e = by_head(jnp.exp(self.cum), self.lane) * jnp.where(self.seg == prior, 1.0, 0.0)
        self.tail = by_head(jnp.exp(end - self.cum), self.lane) * jnp.where(self.seg == last, 1.0, 0.0)
        self.through = jnp.exp(end) * jnp.where(last == prior, 1.0, 0.0)
        row = lax.broadcasted_iota(jnp.int32, (WIDE, 1), 0)
        self.through_rows = jnp.where(row < HEAD_DIM, self.through[:, 0:1],
                                      jnp.where(row < 2 * HEAD_DIM, self.through[:, 1:2], self.through[:, 2:3]))

    def decay(self, h):
        return jnp.exp(jnp.where(self.allowed, self.cum[:, h:h + 1] - self.cum_t[h:h + 1, :], -1e30))

    def of_head(self, a, h):
        return jnp.where(self.lane // HEAD_DIM == h, a, 0.0)


def mixer_fwd_kernel(lens, hidden, gain, w_bc, w_xz, w_dt, cw, pv, u_out, proj_out, mixg, squares, y_out, states, state, before):
    blk = pl.program_id(0)

    @pl.when(blk == 0)
    def _():
        state[...] = jnp.zeros_like(state)
        before[...] = jnp.zeros_like(before)
    parts = [hidden[0, i].astype(F32) for i in range(NC)]
    feat = parts[0].shape[1]
    squares_in = sum(jnp.sum(p * p, axis=1, keepdims=True) for p in parts)
    scale = lax.rsqrt(squares_in / (NC * feat) + 1e-05)
    for i, p in enumerate(parts):
        at = slice(i * feat, (i + 1) * feat)
        u_out[:, at] = (p * scale * gain[:, at]).astype(BF)
    u = u_out[...]
    proj = jnp.concatenate([mm(u, w_bc[:, :2 * STATE]), mm(u, w_xz[...]), mm(u, w_dt[...])], axis=1)
    proj_out[...] = proj
    k = Block(blk, lens, proj, before[...], cw[...], pv[...])
    before[...] = proj[SPAN - 8:]
    s_in = state[...]
    states[0] = s_in
    y = mm(k.c, s_in, 1, 1) * k.e
    for h in range(3):
        y = y + mm(k.scores * k.decay(h), k.of_head(k.w, h))
    y = y + pv[1:2, :WIDE] * k.x
    state[...] = k.through_rows * s_in + mm(k.tail * k.w, k.b, 0, 0)
    y_out[...] = y
    gated = y * k.z * k.zs
    mixg[...] = (gated * pv[0:1, :WIDE]).astype(BF)
    squares[...] = jnp.broadcast_to(jnp.sum(gated * gated, axis=1, keepdims=True), squares.shape).astype(BF)


def mixer_bwd_kernel(lens, proj, before, cw, pv, y_ref, states, d_mix, extra, d_in, taps, rows, d_state, later):
    step = pl.program_id(0)
    blk = pl.num_programs(0) - 1 - step

    @pl.when(step == 0)
    def _():
        d_state[...] = jnp.zeros_like(d_state)
        later[...] = jnp.zeros_like(later)
        taps[...] = jnp.zeros_like(taps)
        rows[...] = jnp.zeros_like(rows)
    k = Block(blk, lens, proj[...], before[...], cw[...], pv[...])
    y, dm, s_in, ds = y_ref[...], d_mix[...], states[0], d_state[...]
    tilt = extra[:, 0:1].astype(F32) + extra[:, 64:65].astype(F32)
    silu_z = k.z * k.zs
    gated = y * silu_z
    d_gated = dm * pv[0:1, :WIDE] - gated * tilt
    d_z = d_gated * y * (k.zs * (1.0 + k.z * (1.0 - k.zs)))
    dy = d_gated * silu_z
    zeros = jnp.zeros((SPAN, 128), F32)
    lane = lax.broadcasted_iota(jnp.int32, (SPAN, 128), 1)
    top = lax.broadcasted_iota(jnp.int32, (128, SPAN), 0)
    d_cum, cols = zeros, jnp.zeros((128, SPAN), F32)
    d_scores = jnp.zeros((SPAN, SPAN), F32)
    dw = jnp.zeros((SPAN, WIDE), F32)
    for h in range(3):
        decay = k.decay(h)
        mixing = k.scores * decay
        dyh = k.of_head(dy, h).astype(BF)
        d_mixing = mm(dyh, k.w, 1, 1)
        d_scores = d_scores + d_mixing * decay
        moved = d_mixing * mixing
        d_cum = jnp.where(lane == h, jnp.sum(moved, axis=1, keepdims=True), d_cum)
        cols = jnp.where(top == h, jnp.sum(moved, axis=0, keepdims=True), cols)
        dw = dw + mm(mixing, dyh, 0, 0)
    e_dy, tail_w = k.e * dy, k.tail * k.w
    back = mm(k.b, ds, 1, 1)
    dw = dw + k.tail * back
    d_c = mm(d_scores, k.b) + mm(e_dy, s_in)
    d_b = mm(d_scores, k.c, 0, 0) + mm(tail_w, ds)
    through_state = mm(k.c, s_in, 1, 1) * k.e
    left = head_sums(tail_w * back)
    d_cum = d_cum - cols.T + head_sums(dy * through_state) - left
    own = jnp.sum(ds * s_in, axis=1, keepdims=True)
    of_row = lax.broadcasted_iota(jnp.int32, (WIDE, 128), 0) // HEAD_DIM
    own = jnp.sum(jnp.where(of_row == lax.broadcasted_iota(jnp.int32, (WIDE, 128), 1), own, 0.0), axis=0, keepdims=True)
    at_end = jnp.sum(left, axis=0, keepdims=True) + k.through * own
    is_last = lax.broadcasted_iota(jnp.int32, (SPAN, 128), 0) == SPAN - 1
    d_cum = d_cum + jnp.where(is_last, at_end, 0.0)
    d_rate = by_parts(d_cum, k.low, 0, 0, 3, True)
    d_dt = head_sums(dw * k.x) + d_rate * pv[3:4, :128]
    d_raw = jnp.where(lane < 3, d_dt * sigmoid(k.raw), 0.0)
    d_x = dw * by_head(k.dt, k.lane) + pv[1:2, :WIDE] * dy
    d_pre = jnp.concatenate([d_b, d_c, d_x], axis=1) * (k.gate * (1.0 + k.acc * (1.0 - k.gate)))
    wide_rows = [jnp.sum(gated * dm, axis=0, keepdims=True), jnp.sum(dy * k.x, axis=0, keepdims=True)]
    thin_rows = [jnp.sum(d_raw, axis=0, keepdims=True), jnp.sum(d_rate * k.rate, axis=0, keepdims=True)]
    for i, one in enumerate(wide_rows):
        rows[i:i + 1, :WIDE] += one
    for i, one in enumerate(thin_rows):
        rows[2 + i:3 + i, :128] += one
    for s in range(CONV):
        taps[3 - s:4 - s] += jnp.sum(d_pre * k.shifted[s], axis=0, keepdims=True)
    taps[4:5] += jnp.sum(d_pre, axis=0, keepdims=True)
    ext = jnp.concatenate([d_pre, later[...]], axis=0)
    place = k.start + lax.broadcasted_iota(jnp.int32, (SPAN + 8, 1), 0)
    seg = seg_at(place, k.l0, k.l1)
    d_v = cw[3:4] * d_pre
    for s in range(1, CONV):
        keep = jnp.where(seg_at(place - s, k.l0, k.l1) == seg, 1.0, 0.0)
        d_v = d_v + cw[3 - s:4 - s] * (ext * keep)[s:s + SPAN]
    later[...] = d_pre[:8]
    d_in[...] = jnp.concatenate([d_v, d_z, d_raw], axis=1).astype(BF)
    d_state[...] = k.through_rows * ds + mm(e_dy, k.c, 0, 0)


def mixer_specs(n, order):
    block = lambda width: pl.BlockSpec((SPAN, width), lambda i: (order(i), 0))
    whole = lambda shape: pl.BlockSpec(shape, lambda i: (0, 0))
    before = pl.BlockSpec((8, MIX + WIDE + 128), lambda i: (jnp.maximum(order(i) * (SPAN // 8) - 1, 0), 0))
    return block, whole, [pl.BlockSpec(memory_space=pltpu.SMEM), block(MIX + WIDE + 128), before, whole((8, MIX)), whole((8, 256))]


def mixer_fwd(cid, lens, hidden, gain, w_bc, w_xz, w_dt, cw, pv, kinds, arrays):
    _, _, tok, feat = hidden.shape
    T, D = hidden.shape[0] * tok, NC * feat
    n, per = T // SPAN, tok // SPAN
    block, whole, _ = mixer_specs(n, lambda i: i)
    cols = MIX + WIDE + 128
    return ridden_call(
        mixer_fwd_kernel, cid, n, (lens, hidden, gain, w_bc, w_xz, w_dt, cw, pv),
        [pl.BlockSpec(memory_space=pltpu.SMEM), pl.BlockSpec((1, NC, SPAN, feat), lambda i: (i // per, 0, i % per, 0)),
         whole((1, D)), whole(w_bc.shape), whole(w_xz.shape), whole(w_dt.shape), whole((8, MIX)), whole((8, 256))],
        [((T, D), BF), ((T, cols), F32), ((T, WIDE), BF), ((T, 128), BF), ((T, WIDE), F32), ((n, WIDE, STATE), F32)],
        [block(D), block(cols), block(WIDE), block(128), block(WIDE), pl.BlockSpec((1, WIDE, STATE), lambda i: (i, 0, 0))],
        [pltpu.VMEM((WIDE, STATE), F32), pltpu.VMEM((8, cols), F32)], 8 << 30, kinds, arrays)


def mixer_bwd(cid, lens, proj, cw, pv, y, states, d_mix, g1_ext, kinds, arrays):
    T = proj.shape[0]
    n = T // SPAN
    order = lambda i: n - 1 - i
    block, whole, first = mixer_specs(n, order)
    at = g1_ext.shape[1] // 128 - 1
    return ridden_call(
        mixer_bwd_kernel, cid, n, (lens, proj, proj, cw, pv, y, states, d_mix, g1_ext),
        first + [block(WIDE), pl.BlockSpec((1, WIDE, STATE), lambda i: (order(i), 0, 0)), block(WIDE),
                 pl.BlockSpec((SPAN, 128), lambda i: (order(i), at))],
        [((T, MIX + WIDE + 128), BF), ((8, MIX), F32), ((8, 256), F32)],
        [block(MIX + WIDE + 128), whole((8, MIX)), whole((8, 256))],
        [pltpu.VMEM((WIDE, STATE), F32), pltpu.VMEM((8, MIX), F32)], 12 << 30, kinds, arrays)


AHEAD_DIM = 64
SCALE = AHEAD_DIM ** (-0.5)
LOW = -1e30


def att_allowed(lens, i, j, n, flip):
    a, b = lax.broadcasted_iota(jnp.int32, (n, 1), 0), lax.broadcasted_iota(jnp.int32, (1, n), 1)
    qp, kp = (i * n + b, j * n + a) if flip else (i * n + a, j * n + b)
    return (kp <= qp) & (seg_at(kp, lens[0], lens[1]) == seg_at(qp, lens[0], lens[1]))


def att_fwd_kernel(lens, qkv, attended, o_ref, lse):
    i = pl.program_id(0)
    n = o_ref.shape[0]
    lane = lax.broadcasted_iota(jnp.int32, (n, WIDE), 1)
    thin = lax.broadcasted_iota(jnp.int32, (n, 128), 1)
    mine = jnp.where((i == 0) | (i == 3), 0, 1) == lax.rem(lax.axis_index("cols"), 2)

    @pl.when(jnp.logical_not(mine))
    def _():
        attended[...] = jnp.zeros_like(attended)
        o_ref[...] = jnp.zeros_like(o_ref)
        lse[...] = jnp.zeros_like(lse)

    @pl.when(mine)
    def _():
        q = qkv[pl.ds(i * n, n), :WIDE] * jnp.asarray(SCALE, BF)
        heads = [jnp.where(lane // AHEAD_DIM == h, q, jnp.zeros_like(q)) for h in range(3)]

        def body(j, carry):
            tops, sums, acc = carry
            k, v = qkv[pl.ds(j * n, n), WIDE:2 * WIDE], qkv[pl.ds(j * n, n), 2 * WIDE:]
            allowed = att_allowed(lens, i, j, n, False)
            new_tops, new_sums = [], []
            for h in range(3):
                s = jnp.where(allowed, mm(heads[h], k, 1, 1), LOW)
                top = jnp.maximum(tops[h], jnp.max(s, axis=1, keepdims=True))
                p = jnp.exp(s - top)
                fade = jnp.exp(tops[h] - top)
                new_tops.append(top)
                new_sums.append(sums[h] * fade + jnp.sum(p, axis=1, keepdims=True))
                acc = jnp.where(lane // AHEAD_DIM == h, acc * fade + mm(p, v), acc)
            return tuple(new_tops), tuple(new_sums), acc

        zero = jnp.zeros((n, 1), F32)
        start = (tuple(zero + LOW for _ in range(3)), (zero,) * 3, jnp.zeros((n, WIDE), F32))
        tops, sums, acc = lax.fori_loop(0, i + 1, body, start)
        pick = lambda a: jnp.where(lane < AHEAD_DIM, a[0], jnp.where(lane < 2 * AHEAD_DIM, a[1], a[2]))
        out = acc / pick(sums)
        o_ref[...] = out
        attended[...] = out.astype(BF)
        logs = [t + jnp.log(s) for t, s in zip(tops, sums)]
        lse[...] = jnp.where(thin == 0, logs[0], jnp.where(thin == 1, logs[1], logs[2]))


def att_bwd_kernel(lens, qkv, d_att, o_ref, lse, d_qkv, dk, dv):
    i = pl.program_id(0)
    n = lse.shape[0]
    lane = lax.broadcasted_iota(jnp.int32, (n, WIDE), 1)
    mine = jnp.where((i == 0) | (i == 3), 0, 1) == lax.rem(lax.axis_index("cols"), 2)

    @pl.when(i == 0)
    def _():
        dk[...] = jnp.zeros_like(dk)
        dv[...] = jnp.zeros_like(dv)

    @pl.when(jnp.logical_not(mine))
    def _():
        d_qkv[pl.ds(i * n, n), :WIDE] = jnp.zeros((n, WIDE), BF)

    @pl.when(mine)
    def _():
        q = qkv[pl.ds(i * n, n), :WIDE]
        do = d_att[...]
        delta = head_sums(o_ref[...] * do.astype(F32)).T
        logs = lse[...].T
        none = jnp.zeros_like(q)
        qs = [jnp.where(lane // AHEAD_DIM == h, q, none) for h in range(3)]
        dos = [jnp.where(lane // AHEAD_DIM == h, do, none) for h in range(3)]

        def body(j, dq):
            at = pl.ds(j * n, n)
            k, v = qkv[at, WIDE:2 * WIDE], qkv[at, 2 * WIDE:]
            allowed = att_allowed(lens, i, j, n, True)
            for h in range(3):
                s = mm(k, qs[h], 1, 1) * SCALE
                p = jnp.exp(jnp.where(allowed, s, LOW) - logs[h:h + 1])
                ds = (p * (mm(v, dos[h], 1, 1) - delta[h:h + 1]) * SCALE).astype(BF)
                dv[at, :] += mm(p, dos[h])
                dk[at, :] += mm(ds, qs[h])
                dq = jnp.where(lane // AHEAD_DIM == h, dq + mm(ds, k, 0, 0), dq)
            return dq

        dq = lax.fori_loop(0, i + 1, body, jnp.zeros((n, WIDE), F32))
        d_qkv[pl.ds(i * n, n), :WIDE] = dq.astype(BF)

    @pl.when(i == pl.num_programs(0) - 1)
    def _():
        d_qkv[:, WIDE:2 * WIDE] = dk[...].astype(BF)
        d_qkv[:, 2 * WIDE:] = dv[...].astype(BF)


def att_call(kernel, cid, lens, qkv, blocked, outs, out_specs, scratch, kinds, arrays):
    T = qkv.shape[0]
    specs = [pl.BlockSpec(memory_space=pltpu.SMEM), pl.BlockSpec((T, 3 * WIDE), lambda i: (0, 0))]
    specs += [pl.BlockSpec((T // 4, a.shape[1]), lambda i: (i, 0)) for a in blocked]
    return ridden_call(kernel, cid, 4, (lens, qkv) + blocked, specs, outs, out_specs, scratch, 8 << 30, kinds, arrays)


def att_fwd(cid, lens, qkv, kinds, arrays):
    T = qkv.shape[0]
    block = lambda w: pl.BlockSpec((T // 4, w), lambda i: (i, 0))
    return att_call(att_fwd_kernel, cid, lens, qkv, (), [((T, WIDE), BF), ((T, WIDE), F32), ((T, 128), F32)],
                    [block(WIDE), block(WIDE), block(128)], [], kinds, arrays)


def att_bwd(cid, lens, qkv, d_att, o, lse, kinds, arrays):
    T = qkv.shape[0]
    return att_call(att_bwd_kernel, cid, lens, qkv, (d_att, o, lse), [((T, 3 * WIDE), BF)],
                    [pl.BlockSpec((T, 3 * WIDE), lambda i: (0, 0))], [pltpu.VMEM((T, WIDE), F32), pltpu.VMEM((T, WIDE), F32)], kinds, arrays)


VMEM, ANY = pltpu.VMEM, pl.ANY


HALVES = 2


class Sum:
    def __init__(self, r, c, partial, bufs):
        self.r, self.c, self.partial = r, c, partial
        self.yy, self.kk = r >> 1, r & 1
        (self.part, self.p_out, self.k_buf, self.y_out, self.y_buf, self.z_out, self.r_buf, self.l_buf,
         self.k_s, self.k_r, self.y_s, self.y_r, self.zr_s, self.zr_r, self.zl_s, self.zl_r) = bufs
        self.cut = self.part.shape[1] // HALVES

    @staticmethod
    def scratch(S, W):
        buf, sem = (lambda *n: VMEM(n + (S, W), BF)), (lambda n: pltpu.SemaphoreType.DMA((n,)))
        return [VMEM((NC, S, W), F32), buf(2, NC), buf(2, NC)] + [buf(NC)] * 5 + [sem(2 * NC), sem(2 * NC)] + [sem(HALVES * NC)] * 6

    def k_copy(self, y, cc):
        i = y * NC + cc
        return copy_to(self.p_out.at[y, cc], self.k_buf.at[y, cc], self.k_s.at[i], self.k_r.at[i], {"rows": self.r ^ 1})

    def piece(self, src, dst, send, recv, cc, h, to):
        at, i = pl.ds(h * self.cut, self.cut), cc * HALVES + h
        return copy_to(src.at[cc, at], dst.at[cc, at], send.at[i], recv.at[i], to)

    def y_copy(self, cc, h):
        return self.piece(self.y_out, self.y_buf, self.y_s, self.y_r, cc, h, {"rows": self.r ^ 2})

    def r_copy(self, cc, h):
        return self.piece(self.z_out, self.r_buf, self.zr_s, self.zr_r, cc, h, {"cols": self.c + 1})

    def l_copy(self, cc, h):
        return self.piece(self.z_out, self.l_buf, self.zl_s, self.zl_r, cc, h, {"cols": self.c - 1})

    def nth(self, j):
        return jnp.where(self.c < NC // 2, NC - 1 - j, j)

    def each(self, f):
        def body(j, carry):
            f(self.nth(j))
            return carry
        lax.fori_loop(0, NC, body, 0)

    def to_core(self):
        def half(i, carry):
            y = jnp.where(i == 0, 1 - self.yy, self.yy)

            def one(cc):
                self.p_out[y, cc] = self.partial(y * 2 + (1 - self.kk), cc).astype(BF)
                self.k_copy(y, cc).start()
            self.each(one)
            return carry
        lax.fori_loop(0, 2, half, 0)

    def to_y(self):
        def one(cc):
            mine = self.partial((1 - self.yy) * 2 + self.kk, cc)
            self.k_copy(1 - self.yy, cc).wait_recv()
            self.y_out[cc] = (mine + self.k_buf[1 - self.yy, cc].astype(F32)).astype(BF)
            self.y_copy(cc, 0).start()
        self.each(one)
        for h in range(1, HALVES):
            self.each(lambda cc: self.y_copy(cc, h).start())

    def own(self):
        def one(cc):
            mine = self.partial(self.r, cc)
            self.k_copy(self.yy, cc).wait_recv()
            self.part[cc] = mine + self.k_buf[self.yy, cc].astype(F32)
        self.each(one)

    def step(self, j, h):
        c, cc = self.c, self.nth(j)
        at = pl.ds(h * self.cut, self.cut)
        self.y_copy(cc, h).wait_recv()
        self.part[cc, at] += self.y_buf[cc, at].astype(F32)

        @pl.when(cc > c)
        def _():
            @pl.when(c > 0)
            def _():
                self.r_copy(cc, h).wait_recv()
                self.part[cc, at] += self.r_buf[cc, at].astype(F32)
            self.z_out[cc, at] = self.part[cc, at].astype(BF)
            self.r_copy(cc, h).start()

        @pl.when(cc < c)
        def _():
            @pl.when(c < NC - 1)
            def _():
                self.l_copy(cc, h).wait_recv()
                self.part[cc, at] += self.l_buf[cc, at].astype(F32)
            self.z_out[cc, at] = self.part[cc, at].astype(BF)
            self.l_copy(cc, h).start()

    def last(self, total, h):
        c, at = self.c, pl.ds(h * self.cut, self.cut)
        total[at] = self.part[c, at]

        @pl.when(c > 0)
        def _():
            self.r_copy(c, h).wait_recv()
            total[at] += self.r_buf[c, at].astype(F32)

        @pl.when(c < NC - 1)
        def _():
            self.l_copy(c, h).wait_recv()
            total[at] += self.l_buf[c, at].astype(F32)

    def finish(self):
        def one(cc):
            self.k_copy(0, cc).wait_send()
            self.k_copy(1, cc).wait_send()
            for h in range(HALVES):
                self.y_copy(cc, h).wait_send()

                @pl.when(cc > self.c)
                def _():
                    self.r_copy(cc, h).wait_send()

                @pl.when(cc < self.c)
                def _():
                    self.l_copy(cc, h).wait_send()
        self.each(one)


class Gather:
    def __init__(self, r, c, out, S, sems, use=None):
        self.r, self.c, self.out, self.S, self.use = r, c, out, S, use
        self.recv, self.zr_s, self.zl_s, self.y_s, self.k_s = sems

    @staticmethod
    def scratch():
        return [pltpu.SemaphoreType.DMA((HALVES * n,)) for n in (4 * NC, NC, NC, NC, 2 * NC)]

    def slab(self, rr, cc):
        return self.out.at[pl.ds(pl.multiple_of((rr * NC + cc) * self.S, 16), self.S)]

    def move(self, rr, cc, h, sem, to):
        cut = self.S // HALVES
        ref = self.out.at[pl.ds(pl.multiple_of((rr * NC + cc) * self.S + h * cut, 16), cut)]
        return copy_to(ref, ref, sem, self.recv.at[(rr * NC + cc) * HALVES + h], to)

    def right(self, cc, h):
        return self.move(self.r, cc, h, self.zr_s.at[cc * HALVES + h], {"cols": self.c + 1})

    def left(self, cc, h):
        return self.move(self.r, cc, h, self.zl_s.at[cc * HALVES + h], {"cols": self.c - 1})

    def y_copy(self, cc, h):
        return self.move(self.r, cc, h, self.y_s.at[cc * HALVES + h], {"rows": self.r ^ 2})

    def k_copy(self, rr, cc, h):
        return self.move(rr, cc, h, self.k_s.at[((rr >> 1) * NC + cc) * HALVES + h], {"rows": self.r ^ 1})

    def got(self, rr, cc, h):
        self.k_copy(rr, cc, h).wait_recv()

    def pass_on(self, cc, h):
        c = self.c

        @pl.when((cc <= c) & (c < NC - 1))
        def _():
            self.right(cc, h).start()

        @pl.when((cc >= c) & (c > 0))
        def _():
            self.left(cc, h).start()
        self.y_copy(cc, h).start()
        self.k_copy(self.r, cc, h).start()

    def begin(self):
        for h in range(HALVES):
            self.pass_on(self.c, h)

    def sides(self, off, f):
        for s in (-1, 1):
            cc = self.c + s * off
            fits = (cc >= 0) & (cc < NC) & (off < NC)
            if s == 1:
                fits = fits & (off > 0)

            @pl.when(fits)
            def _():
                f(cc)

    def forward(self, d, halves=range(HALVES)):
        for h in halves:
            def along(cc):
                self.got(self.r, cc, h)
                self.pass_on(cc, h)

            def across(cc):
                self.got(self.r ^ 2, cc, h)
                self.k_copy(self.r ^ 2, cc, h).start()
            self.sides(d, along)
            self.sides(d - 1, across)

    def uses(self, d):
        def one(i, carry):
            kind, s = i >> 1, (i & 1) * 2 - 1
            off = d - jnp.where(kind == 0, 0, jnp.where(kind == 3, 2, 1))
            rr = self.r ^ jnp.where(kind == 0, 0, jnp.where(kind == 1, 2, jnp.where(kind == 2, 1, 3)))
            cc = self.c + s * off
            fits = (off >= 0) & (off < NC) & (cc >= 0) & (cc < NC) & ((s < 0) | (off > 0))

            @pl.when(fits)
            def _():
                @pl.when(kind >= 2)
                def _():
                    for h in range(HALVES):
                        self.got(rr, cc, h)
                if self.use is not None:
                    self.use(rr, cc)
            return carry
        lax.fori_loop(0, 8, one, 0)

    def finish(self):
        def body(cc, carry):
            for h in range(HALVES):
                self.y_copy(cc, h).wait_send()
                self.k_copy(self.r, cc, h).wait_send()
                self.k_copy(self.r ^ 2, cc, h).wait_send()

                @pl.when((cc <= self.c) & (self.c < NC - 1))
                def _():
                    self.right(cc, h).wait_send()

                @pl.when((cc >= self.c) & (self.c > 0))
                def _():
                    self.left(cc, h).wait_send()
            return carry
        lax.fori_loop(0, NC, body, 0)


def link_call(kernel, cid, ins, in_spaces, outs, out_spaces, scratch, flops):
    return pl.pallas_call(
        kernel,
        out_shape=[jax.ShapeDtypeStruct(s, d) for s, d in outs],
        in_specs=[pl.BlockSpec(memory_space=s) for s in in_spaces],
        out_specs=[pl.BlockSpec(memory_space=s) for s in out_spaces],
        scratch_shapes=scratch,
        compiler_params=pltpu.CompilerParams(collective_id=cid, has_side_effects=True, vmem_limit_bytes=62 << 20),
        cost_estimate=pl.CostEstimate(flops=flops, bytes_accessed=96 << 20, transcendentals=0),
    )(*ins)


def entry_kernel(kinds, *refs):
    n = len(kinds)
    it = iter(refs)
    take = lambda k: [next(it) for _ in range(k)]
    hidden, grad = take(2)
    ins = take(n)
    hid_all, g_all, h0 = take(3)
    outs = take(n)
    got, = take(1)
    hid_sems, g_sems, swap_sems, sems = take(5), take(5), take(3), take(3)
    r, c = lax.axis_index("rows"), lax.axis_index("cols")
    greet(r, c, kinds)
    big, S = hidden.shape[0], got.shape[1]
    feat = hidden.shape[1]
    first = Gather(r, c, hid_all, big, hid_sems)
    second = Gather(r, c, g_all, S, g_sems)
    swap = Riders(("swap",), (grad,), (got,), *swap_sems)
    riding = Riders(kinds, ins, outs, *sems)
    hid_all[pl.ds(pl.multiple_of((r * NC + c) * big, 16), big), :] = hidden[...]
    first.begin()
    swap.start()
    for d in range(1, NC):
        first.forward(d)
        if d == 1:
            riding.start()
        first.uses(d)
        if d == 2:
            swap.finish()
            for i in range(NC):
                g_all[pl.ds(pl.multiple_of((r * NC + c) * S, 16), S), i * feat:(i + 1) * feat] = got[i]
            second.begin()
        if d == 3:
            riding.relay()
            second.forward(1)
            second.uses(1)
    for i in range(NC):
        h0[:, i * feat:(i + 1) * feat] = hid_all[pl.ds(pl.multiple_of((r * NC + i) * big + c * S, 16), S), :]
    for d in range(NC, NC + 2):
        first.forward(d)
        first.uses(d)
        second.forward(d - 2)
        second.uses(d - 2)
    for d in range(NC, NC + 2):
        second.forward(d)
        second.uses(d)
    first.finish()
    second.finish()
    riding.finish()


def entry(cid, hidden, grad, kinds, arrays):
    big, feat = hidden.shape
    S, D = big // NC, feat * NC
    shapes, sems = rider_parts(kinds, arrays)
    _, swap_sems = rider_parts(("swap",), (grad,))
    outs = [((4 * NC * big, feat), BF), ((4 * NC * S, D), BF), ((S, D), BF)] + [(s.shape, s.dtype) for s in shapes]
    scratch = [VMEM(grad.shape, BF)] + Gather.scratch() + Gather.scratch() + swap_sems + sems
    return link_call(functools.partial(entry_kernel, tuple(kinds)), cid, [hidden, grad] + list(arrays), [VMEM] + [ANY] * (1 + len(kinds)),
                     outs, [VMEM] * 3 + [ANY] * len(kinds), scratch, 1 << 20)


def link_kernel(spec, *refs):
    it = iter(refs)
    take = lambda n: [next(it) for _ in range(n)]
    maybe = lambda key, n=1: take(n) if spec[key] else [None] * n
    a, w1 = take(2)
    side, = maybe("side")
    mid_in = take(spec["n_mid"])
    w2, = take(1) if spec["w2"] in ("in", "in_t") else [None]
    a2, v2 = maybe("more_sum", 2)
    after_in = take(spec["n_after"])
    early_in = take(len(spec["early"]))
    late_in = take(sum(src is None for _, src in spec["late"]))
    u_all = next(it)
    mid_out = take(spec["n_mid_out"])
    post_out = take(spec["n_post"])
    after_out = take(spec["n_after_out"])
    early_out, late_out = take(len(spec["early"])), take(len(spec["late"]))
    final_out = take(len(after_out))
    total, = take(1)
    sum_bufs, gather_sems = take(16), take(5)
    sum2_bufs = take(17) if spec["more_sum"] else []
    small = take(6) if spec["small"] else None
    early_sems, late_sems, final_sems = take(spec["n_early_sems"]), take(spec["n_late_sems"]), take(3 * (len(after_out) > 0))
    r, c = lax.axis_index("rows"), lax.axis_index("cols")
    S, W = total.shape
    D = w1.shape[0] if spec["w1_t"] else w1.shape[1]
    late_kinds = tuple(kind for kind, _ in spec["late"])
    greet(r, c, spec["early"] + late_kinds + (("dp",) if spec["small"] else ()))
    none = [None] * 3
    early = Riders(spec["early"], early_in, early_out, *(early_sems or none))
    late_in = iter(late_in)
    sources = [next(late_in) if src is None else mid_out[src] for _, src in spec["late"]]
    late = Riders(late_kinds, sources, late_out, *(late_sems or none))
    final = Riders(("swap",) * len(after_out), after_out, final_out, *(final_sems or none))
    rows_of = lambda rr, cc: pl.ds(pl.multiple_of((rr * NC + cc) * S, 16), S)

    def partial(rr, cc):
        p = mm(a[rows_of(rr, cc), :], w1[...], 1, 1 if spec["w1_t"] else 0)
        return p if side is None else jnp.concatenate([p, side[rows_of(rr, cc), :].astype(F32)], axis=1)

    def use(rr, cc):
        w = early_out[0][...].reshape(D, -1) if spec["w2"] == "rider" else w2[...]
        u = u_all[rows_of(rr, cc), :D] if u_all.shape[1] > D else u_all[rows_of(rr, cc), :]
        spec["post"](mm(u, w, 1, 1 if spec["w2"] == "in_t" else 0), rows_of(rr, cc), post_out)

    summing = Sum(r, c, partial, sum_bufs)
    gather = Gather(r, c, u_all, S, gather_sems, use if spec["w2"] else None)
    summing2 = None
    summing.to_core()
    early.start()
    summing.to_y()
    if spec["more_sum"]:
        summing2 = Sum(r, c, lambda rr, cc: mm(a2[rows_of(rr, cc), :], v2[...]), sum2_bufs[:16])
    summing.own()
    def advance(h):
        at = pl.ds(h * (S // HALVES), S // HALVES)
        off = pl.multiple_of((r * NC + c) * S + h * (S // HALVES), 16)
        u_all[pl.ds(off, S // HALVES), :] = spec["mid"](total, mid_in, mid_out, at, h)
        gather.pass_on(c, h)

    for h in range(HALVES):
        for j in range(NC):
            summing.step(j, h)
            if h == 0 and j == 1:
                if spec["small"]:
                    early.add()
                if summing2:
                    summing2.to_core()
            if not spec["small"] and j == 1:
                for g in range(h):
                    gather.forward(h - g, (g,))
        summing.last(total, h)
        if not spec["small"]:
            advance(h)
        if h == 0:
            if summing2:
                summing2.to_y()
                summing2.own()
            if not spec["small"]:
                early.add()
    if spec["small"]:
        mine, others, held, dp_s, dp_r, loc = small
        spec["mid"](total, mid_in, mid_out, mine)
        settle = sum_groups(mine, others, held, dp_s, dp_r, 4)
        late.start()
        settle()
        place = pltpu.make_async_copy(held, gather.slab(r, c), loc)
        place.start()
        place.wait()
        gather.begin()
        early.relay()
    else:
        late.start()
    if spec["w2"] == "rider":
        early.relay()
        early.finish()
    if spec["w2"]:
        use(r, c)
    for d in range(1, NC + 2):
        if summing2 and d <= NC:
            for h in range(HALVES):
                summing2.step(d - 1, h)
        if spec["small"]:
            gather.forward(d)
        else:
            for g in reversed(range(HALVES)):
                if HALVES - 1 - g + d <= NC:
                    gather.forward(HALVES - 1 - g + d, (g,))
        gather.uses(d)
        if d == 2 and spec["w2"] != "rider" and not spec["small"]:
            early.relay()
    gather.finish()
    summing.finish()
    if summing2:
        for h in range(HALVES):
            summing2.last(sum2_bufs[16], h)
        spec["after"](sum2_bufs[16], after_in, after_out)
        final.start()
        summing2.finish()
        final.finish()
    late.add()
    late.relay()
    if spec["w2"] != "rider":
        early.finish()
    late.finish()


def link(cid, a, w1, mid, mid_in, mid_out, *, w1_t=False, side=None, w2=None, w2_kind=None, post=None, post_out=(), early=(), early_in=(),
         late=(), late_in=(), extra=0, small=0, more_sum=None, after=None, after_in=(), after_out=()):
    T = a.shape[0]
    D = w1.shape[0] if w1_t else w1.shape[1]
    S = T // (4 * NC)
    W = D + (0 if side is None else side.shape[1])
    width = small or D + extra
    early_shapes, early_sems = rider_parts(early, early_in)
    late_it = iter(late_in)
    late_arrays = [next(late_it) if src is None else jax.ShapeDtypeStruct(*mid_out[src]) for _, src in late]
    late_shapes, late_sems = rider_parts(tuple(k for k, _ in late), late_arrays)
    final_shapes, final_sems = rider_parts(("swap",) * len(after_out), [jax.ShapeDtypeStruct(*o) for o in after_out])
    spec = dict(w1_t=w1_t, side=side is not None, mid=mid, n_mid=len(mid_in), n_mid_out=len(mid_out), w2=w2_kind, post=post,
                n_post=len(post_out), early=tuple(early), late=tuple(late), small=small, more_sum=more_sum is not None,
                after=after, n_after=len(after_in), n_after_out=len(after_out), n_early_sems=len(early_sems), n_late_sems=len(late_sems))
    ins = [a, w1] + ([side] if side is not None else []) + list(mid_in) + ([w2] if w2 is not None else [])
    ins += list(more_sum or ()) + list(after_in)
    riding = list(early_in) + list(late_in)
    in_spaces = [VMEM] * len(ins) + [ANY] * len(riding)
    ins += riding
    outs = [((T, width), BF)] + list(mid_out) + list(post_out)
    outs += list(after_out)
    out_spaces = [VMEM] * len(outs) + [ANY] * len(early_shapes + late_shapes + final_shapes)
    if w2_kind == "rider":
        out_spaces[len(outs)] = VMEM
    outs += [(s.shape, s.dtype) for s in early_shapes + late_shapes + final_shapes]
    scratch = [VMEM((S, W), F32)] + Sum.scratch(S, W) + Gather.scratch()
    if more_sum is not None:
        scratch += Sum.scratch(S, D) + [VMEM((S, D), F32)]
    if small:
        groups = lax.axis_size("dp")
        scratch += [VMEM((S, small), F32), VMEM((groups - 1, S, small), F32), VMEM((S, small), BF), pltpu.SemaphoreType.DMA((groups - 1,)),
                    pltpu.SemaphoreType.DMA((groups - 1,)), pltpu.SemaphoreType.DMA]
    scratch += early_sems + late_sems + final_sems
    return link_call(functools.partial(link_kernel, spec), cid, ins, in_spaces, outs, out_spaces, scratch, 8 << 30)


EPS = 1e-05


def norm_scale(x):
    return lax.rsqrt(jnp.mean(x * x, axis=1, keepdims=True) + EPS)


def norm_grad(x, gain, up, gain_grad, h):
    s = norm_scale(x)
    own = jnp.sum(x * s * up, axis=0, keepdims=True)
    gain_grad[0:1] = own if h == 0 else gain_grad[0:1] + own
    tilted = up * gain
    return s * tilted - x * (s * s * s * jnp.mean(x * tilted, axis=1, keepdims=True))


def mid_mixer(inner, total, ins, outs, at, h):
    h0, gain = ins
    h1, mix_out, gate_scale = outs
    D = h0.shape[1]
    s = lax.rsqrt(total[at, D:D + 1] / inner + EPS)
    out = total[at, :D] * s
    mix_out[at] = out
    gate_scale[at] = jnp.broadcast_to(s, (out.shape[0], gate_scale.shape[1]))
    x = h0[at].astype(F32) + out
    h1[at] = x
    return (x * norm_scale(x) * gain[...]).astype(BF)


def mid_attention(total, ins, outs, at, h):
    h1, gain = ins
    x = h1[at] + total[at]
    outs[0][at] = x
    return (x * norm_scale(x) * gain[...]).astype(BF)


def mid_ff_back(total, ins, outs, at, h):
    h2, gain, grad = ins
    dh2, gain_grad = outs
    d = grad[at].astype(F32) + norm_grad(h2[at], gain[...], total[at], gain_grad, h)
    dh2[at] = d
    return d.astype(BF)


def mid_att_back(inner, total, ins, outs, at, h):
    h1, gain, dh2, mix_out, gate_scale = ins
    dh1, gain_grad = outs
    d = dh2[at] + norm_grad(h1[at], gain[...], total[at], gain_grad, h)
    dh1[at] = d
    s = gate_scale[at, 0:1]
    tilt = s * s * jnp.sum(d * mix_out[at], axis=1, keepdims=True) / inner
    high = tilt.astype(BF).astype(F32)
    lane = lax.broadcasted_iota(jnp.int32, (d.shape[0], 128), 1)
    return jnp.concatenate([d * s, jnp.where(lane < 64, high, tilt - high)], axis=1).astype(BF)


def mid_mixer_back(total, ins, outs, small):
    h0, gain, dh1 = ins
    in_slab, gain_grad = outs
    D = h0.shape[1]
    thin = small.shape[1]
    four = D // thin
    d = dh1[...] + norm_grad(h0[...].astype(F32), gain[...], total[:, :D], gain_grad, 0)
    feat = D // NC
    for i in range(NC):
        in_slab[i] = d[:, i * feat:(i + 1) * feat].astype(BF)
    rest = total[:, D:]
    small[...] = jnp.zeros_like(small)
    small[:SMALL] = rest[:SMALL]
    own = rest[SMALL:SMALL + four] + rest[SMALL + four:SMALL + 2 * four]
    row = gain_grad[0:1]
    for i in range(3):
        small[SMALL + i * four:SMALL + (i + 1) * four] = own
        for j in range(four):
            at = SMALL + (3 + i) * four + j
            small[at:at + 1] = row[:, j * thin:(j + 1) * thin]


def after_output(total, ins, outs):
    h2, valid = ins
    x = (h2[...] + total[...]) * valid[:, 0:1]
    feat = x.shape[1] // NC
    for i in range(NC):
        outs[0][i] = x[:, i * feat:(i + 1) * feat].astype(BF)


def post_plain(p, at, outs):
    outs[0][at, :] = p.astype(outs[0].dtype)


def post_gelu(p, at, outs):
    outs[0][at, :] = p
    outs[1][at, :] = (0.5 * p * (1.0 + jnp.tanh(0.7978845608028654 * (p + 0.044715 * (p * p * p))))).astype(BF)


def finish_kernel(zx, mix, qkv, o, ff, rest, x_g, z_g, q_g, k_g, v_g, mix_g, o_g, up_g, down_g, bcdt_g, gain2, gain3, cxw, cxb, gate, cbw, cbb, a_log, d_skip, dt_bias, gain1, gain):
    i = pl.program_id(0)
    rows, part = zx.shape[2], ff.shape[2] // 2
    for h in range(2):
        at = slice(h * rows, (h + 1) * rows)
        piece = zx[0, h].astype(F32)
        x_new, z_new = piece[:, :WIDE], piece[:, WIDE:]
        three = qkv[0, h].astype(F32)
        for j in range(NC):
            @pl.when(i == j)
            def _():
                x_g[at, j * WIDE:(j + 1) * WIDE] = x_new
                z_g[at, j * WIDE:(j + 1) * WIDE] = z_new
                to = slice((j // 2) * WIDE, (j // 2 + 1) * WIDE)
                for n, out in enumerate((q_g, k_g, v_g)):
                    new = three[:, n * WIDE:(n + 1) * WIDE]
                    out[at, to] = new if j % 2 == 0 else out[at, to] + new
        half = mix.shape[2]
        mix_g[h * half:(h + 1) * half] = mix[0, h].astype(F32)
        o_at = slice(h * half, (h + 1) * half)

        @pl.when(i % 2 == 0)
        def _():
            o_g[o_at] = o[0, h].astype(F32)

        @pl.when(i % 2 == 1)
        def _():
            o_g[o_at] += o[0, h].astype(F32)
        down_g[h * part:(h + 1) * part] = ff[0, h, :part].astype(F32)
        up_g[h * part:(h + 1) * part] = ff[0, h, part:].astype(F32)
    state = jnp.concatenate([rest[j, :SMALL].astype(F32) for j in range(NC)], axis=0)
    bcdt_g[...] = state.T[:bcdt_g.shape[0]]

    rows_new = []
    gain_new = jnp.zeros((4, rest.shape[2]), F32)
    for j in range(NC):
        tail = rest[j, SMALL:].astype(F32)
        rows_new.append(tail[0:4] + tail[4:8] + tail[8:12])
        gain_new = gain_new + tail[12:16] + tail[16:20] + tail[20:24]

    @pl.when(i == 0)
    def _():
        gain[...] = gain_new

    @pl.when(i > 0)
    def _():
        gain[...] += gain_new

    def line(out, at, four):
        for q in range(4):
            width = four.shape[1]
            out[0:1, at + q * width:at + (q + 1) * width] = four[q:q + 1]
    D = 4 * rest.shape[2]
    for step in range(NC):
        @pl.when(i == step)
        def _():
            for j in range(NC):
                n, new = step * NC + j, rows_new[j]
                if n < 2:
                    line((gain2, gain3)[n], 0, new)
                elif n < 10:
                    for q in range(4):
                        at = (n % 2) * D + q * new.shape[1]
                        cxw[(n - 2) // 2:(n - 2) // 2 + 1, at:at + new.shape[1]] = new[q:q + 1]
                elif n < 14:
                    line((cxb, gate)[(n - 10) // 2], (n % 2) * D, new)
                elif n == 14:
                    cbw[...] = new[:, :2 * STATE]
                else:
                    cbb[...] = new[0:1, :2 * STATE]
                    a_log[...] = new[1:2, :a_log.shape[1]]
                    d_skip[...] = new[2:3, :d_skip.shape[1]]
                    dt_bias[...] = new[3:4, :dt_bias.shape[1]]
            if step == NC - 1:
                line(gain1, 0, gain[...])


def finish(zx, mix, qkv, o, ff, rest, bcdt_width, inner, n_heads):
    thin, feat = rest.shape[2], zx.shape[3]
    D = NC * feat
    lead = lambda a: pl.BlockSpec((1,) + a.shape[1:], lambda i: (i, 0, 0, 0))
    whole = lambda r, w: pl.BlockSpec((r, w), lambda i: (0, 0))
    sds = lambda *s: jax.ShapeDtypeStruct(s, F32)
    small = [(1, D), (1, D), (CONV, inner), (1, inner), (1, inner), (CONV, 2 * STATE), (1, 2 * STATE)] + [(1, n_heads)] * 3 + [(1, D)]
    rows, half, part = 2 * zx.shape[2], 2 * mix.shape[2], ff.shape[2]
    return pl.pallas_call(
        finish_kernel,
        grid=(NC,),
        in_specs=[lead(zx), lead(mix), lead(qkv), lead(o), lead(ff), pl.BlockSpec((NC,) + rest.shape[1:], lambda i: (i, 0, 0))],
        out_specs=[whole(rows, NC * WIDE)] * 2 + [whole(rows, 2 * WIDE)] * 3 + [
            pl.BlockSpec((half, feat), lambda i: (i, 0)), pl.BlockSpec((half, feat), lambda i: (i // 2, 0)),
            pl.BlockSpec((part, feat), lambda i: (0, i)), pl.BlockSpec((part, feat), lambda i: (i, 0)),
            pl.BlockSpec((bcdt_width, NC * SMALL), lambda i: (0, i)), *[whole(*s) for s in small]],
        out_shape=[sds(rows, NC * WIDE)] * 2 + [sds(rows, 2 * WIDE)] * 3 + [
            sds(NC * half, feat), sds(2 * half, feat), sds(part, NC * feat), sds(NC * part, feat), sds(bcdt_width, D),
            *[sds(*s) for s in small]],
        scratch_shapes=[pltpu.VMEM((4, thin), F32)],
        compiler_params=pltpu.CompilerParams(vmem_limit_bytes=62 << 20, dimension_semantics=("arbitrary",)),
        cost_estimate=pl.CostEstimate(flops=1 << 20, bytes_accessed=24 << 20, transcendentals=0),
    )(zx, mix, qkv, o, ff, rest)


def side_kernel(in_grad, taps, rows, gain2, gain3, zx, side, small):
    i = pl.program_id(0)
    slab = lax.axis_index("rows") * NC + lax.axis_index("cols")
    thin = side.shape[2]
    lane = lax.broadcasted_iota(jnp.int32, (1, thin), 1)

    @pl.when(i == 0)
    def _():
        small[...] = jnp.zeros_like(small)
        for n, g in enumerate((gain2, gain3)):
            for q in range(4):
                small[n, q:q + 1] = g[0:1, q * thin:(q + 1) * thin]

        def channels(first, v):
            both = jnp.concatenate([v, v], axis=1)
            small[first + (slab >> 3), pl.ds((slab & 7) >> 1, 1)] = jnp.where(lane // WIDE == (slab & 1), both, 0.0)

        def heads(at, v):
            placed = sum(jnp.where(lane == slab * 3 + h, v[:, h:h + 1], 0.0) for h in range(3))
            small[15, at:at + 1] = placed
        none = jnp.zeros((1, thin - 2 * STATE), F32)
        for t in range(CONV):
            channels(2 + 2 * t, taps[t:t + 1, 2 * STATE:])
            small[14, t:t + 1] = jnp.concatenate([taps[t:t + 1, :2 * STATE], none], axis=1)
        channels(10, taps[CONV:CONV + 1, 2 * STATE:])
        channels(12, rows[0:1, :WIDE])
        small[15, 0:1] = jnp.concatenate([taps[CONV:CONV + 1, :2 * STATE], none], axis=1)
        heads(1, rows[3:4, :128])
        heads(2, head_sums(jnp.broadcast_to(rows[1:2, :WIDE], (8, WIDE)))[0:1])
        heads(3, rows[2:3, :128])
    p = in_grad[...]
    half = p.shape[0] // 2
    for h in range(2):
        zx[0, h] = p[h * half:(h + 1) * half, 2 * STATE:2 * STATE + 2 * WIDE].astype(BF)
    at = lax.broadcasted_iota(jnp.int32, (p.shape[0], 128), 1)
    dts = sum(jnp.where(at == slab * 3 + h, p[:, MIX + WIDE + h:MIX + WIDE + h + 1], 0.0) for h in range(3))
    state = jnp.concatenate([p[:, :2 * STATE], dts], axis=1).astype(BF)
    for j in range(NC):
        side[j, :SMALL] = state[j * SMALL:(j + 1) * SMALL]
        own = small[i * NC + j]
        rest = own - own.astype(BF).astype(F32)
        side[j, SMALL:] = jnp.concatenate([own, rest, jnp.zeros((side.shape[1] - SMALL - 8, thin), F32)], axis=0).astype(BF)


def side_columns(in_grad, taps, rows, gain2, gain3, S):
    D, cols = in_grad.shape
    feat, thin = D // NC, cols - 2 * WIDE
    whole = lambda a: pl.BlockSpec(a.shape, lambda i: (0, 0))
    return pl.pallas_call(
        side_kernel,
        grid=(NC,),
        in_specs=[pl.BlockSpec((feat, cols), lambda i: (i, 0)), whole(taps), whole(rows), whole(gain2), whole(gain3)],
        out_specs=[pl.BlockSpec((1, 2, feat // 2, 2 * WIDE), lambda i: (i, 0, 0, 0)), pl.BlockSpec((NC, S, thin), lambda i: (i, 0, 0))],
        out_shape=[jax.ShapeDtypeStruct((NC, 2, feat // 2, 2 * WIDE), BF), jax.ShapeDtypeStruct((4 * NC, S, thin), BF)],
        scratch_shapes=[pltpu.VMEM((4 * NC, 4, thin), F32)],
        compiler_params=pltpu.CompilerParams(vmem_limit_bytes=32 << 20, dimension_semantics=("arbitrary",)),
        cost_estimate=pl.CostEstimate(flops=1 << 20, bytes_accessed=8 << 20, transcendentals=0),
    )(in_grad, taps, rows, gain2, gain3)


P = jax.sharding.PartitionSpec


def dot(a, b):
    return jnp.dot(a, b, preferred_element_type=F32)


def dot_t(a, b):
    return lax.dot_general(a, b, (((1,), (1,)), ((), ())), preferred_element_type=F32)


def t_dot(a, b):
    return lax.dot_general(a, b, (((0,), (0,)), ((), ())), preferred_element_type=F32)


def split_in(w):
    d, n = w.shape
    return w.reshape(d, NC, n // NC).transpose(1, 0, 2)


def halves_of(w):
    d, n = w.shape
    return w.reshape(d, 2, n // 2).transpose(1, 0, 2)


def whole_out(got):
    return got.transpose(1, 0, 2).reshape(got.shape[1], -1)


def split_grad(g):
    n, d = g.shape
    return g.astype(BF).reshape(n, NC, d // NC).transpose(1, 0, 2)


def per_device(hidden_in, lengths, norm1_gain, z_weight, x_weight, bcdt_weight, conv_x_weight, conv_x_bias,
               conv_bc_weight, conv_bc_bias, a_log, d_skip, dt_bias, gate_gain, mix_out_weight, norm2_gain,
               q_weight, k_weight, v_weight, att_out_weight, norm3_gain, up_weight, down_weight, grad_output):
    r, c = lax.axis_index("rows"), lax.axis_index("cols")
    rows = lax.axis_size("rows")
    tok_rows, feat = hidden_in.shape
    T, D = tok_rows * rows, feat * NC
    S = T // (rows * NC)
    slab = r * NC + c
    inner = z_weight.shape[1] * rows
    wide = z_weight.shape[1] // NC
    heads_row = a_log.shape[0]
    heads = heads_row // NC
    n_heads = heads_row * rows
    seq_lens = lengths[0]
    places = jnp.arange(T, dtype=jnp.int32)
    one_f32, row8 = ((S, D), F32), ((8, D), F32)
    valid = (places < seq_lens[0] + seq_lens[1]).astype(F32)
    my_valid = lax.dynamic_slice_in_dim(valid, slab * S, S, 0)[:, None]
    pad = 128

    pair = "swap2" if lax.axis_size("dp") == 2 else "swap"

    def halved(a):
        return a.reshape(a.shape[0], 2, -1, a.shape[2]) if pair == "swap2" else a

    def joined(a):
        return a.reshape(a.shape[0], -1, a.shape[-1])

    zx_pieces = halved(jnp.concatenate([split_in(x_weight), split_in(z_weight)], axis=2))
    mix_pieces = halved(mix_out_weight.reshape(NC, -1, feat))
    bcdt_width = bcdt_weight.shape[1]
    bcdt_pad = -bcdt_width % 128
    bcdt_piece = jnp.pad(bcdt_weight, ((0, 0), (0, bcdt_pad))).reshape(2, feat // 2, -1)
    gain_piece = jnp.broadcast_to(jnp.pad(jnp.stack([norm1_gain, norm2_gain, norm3_gain]), ((0, 5), (0, 0)))[None], (2, 8, feat))
    here = lax.dynamic_slice_in_dim(valid, r * tok_rows, tok_rows, 0)[:, None]
    grad = (grad_output.astype(F32) * here).astype(BF).reshape(NC, S, feat)
    hidden_all, g3, h0, w_zx, mix_got, w_bcdt, gains = entry(
        0, hidden_in, grad, (pair, pair, "bcast2", "bcast2"), (zx_pieces, mix_pieces, bcdt_piece, gain_piece))
    g3_mine = lax.dynamic_slice_in_dim(g3, slab * S, S, 0)
    w_mix = whole_out(joined(mix_got))
    gains = gains[:, 0, :3].transpose(1, 0, 2).reshape(3, D)
    w_bcdt, w_zx = w_bcdt.reshape(D, -1), w_zx.reshape(D, 2 * wide)
    w_dt = jnp.pad(lax.dynamic_slice_in_dim(w_bcdt, 2 * STATE + slab * heads, heads, 1), ((0, 0), (0, 128 - heads)))
    w_in = jnp.concatenate([w_bcdt[:, :2 * STATE], w_zx, w_dt], axis=1)
    few = pair == "swap2"
    twice = lambda a: a if few else jnp.repeat(a, NC // 2, axis=0)
    one_way = "swaph" if few else "swap"
    qkv_pieces = halved(twice(jnp.concatenate([halves_of(q_weight), halves_of(k_weight), halves_of(v_weight)], axis=2)))
    o_pieces = halved(twice(att_out_weight.reshape(2, -1, feat)))

    mine = lambda a, n: lax.dynamic_slice_in_dim(a, c * n, n, a.ndim - 1)
    cw = jnp.concatenate([conv_bc_weight, mine(conv_x_weight, wide)], axis=1)
    cw = jnp.concatenate([cw, jnp.concatenate([conv_bc_bias, mine(conv_x_bias, wide)])[None], jnp.zeros((3, MIX), F32)])
    wide_row = lambda a: jnp.pad(a, (0, 256 - a.shape[0]))[None]
    pv = jnp.concatenate([wide_row(mine(gate_gain, wide)), wide_row(jnp.repeat(mine(d_skip, heads), HEAD_DIM)),
                          wide_row(mine(dt_bias, heads)), wide_row(-jnp.exp(mine(a_log, heads))), jnp.zeros((4, 256), F32)])
    u1, proj, mixg, squares, y, states, qkv_split = mixer_fwd(
        6, seq_lens, hidden_all.reshape(rows, NC, tok_rows, feat), gains[0:1], w_bcdt, w_zx, w_dt, cw, pv,
        (one_way,), (qkv_pieces,))
    att3 = qkv_pieces.shape[-1]
    u2, h1, mix_out, gate_scale, qkv, qkv_got, o_split, down_split = link(
        1, mixg, w_mix, functools.partial(mid_mixer, inner), (h0, gains[1:2]), (one_f32, one_f32, ((S, 128), F32)), side=squares,
        w2_kind="rider", post=post_plain, post_out=(((T, att3), BF),), early=("spread",), early_in=(qkv_split,), late=((one_way, None), (one_way, None)),
        late_in=(o_pieces, halved(down_weight.reshape(NC, -1, feat))))
    w_qkv = qkv_got.reshape(D, -1)
    att = att3 // 3

    attended, att_exact, lse, up_split, o_got = att_fwd(
        7, seq_lens, qkv, (one_way, "spread"), (halved(split_in(up_weight)), o_split))
    w_o = whole_out(joined(o_got))
    hidden_units = up_weight.shape[1] // NC
    u3, h2, act, hid, up_got, down_got = link(
        2, attended, w_o, mid_attention, (h1, gains[2:3]), (one_f32,), w2_kind="rider", post=post_gelu,
        post_out=(((T, hidden_units), F32), ((T, hidden_units), BF)), early=("spread",), early_in=(up_split,),
        late=(("spread", None),), late_in=(down_split,))
    w_up, w_down = up_got.reshape(D, -1), whole_out(joined(down_got))
    gelu_back = jax.vjp(functools.partial(jax.nn.gelu, approximate=True), act)[1]

    reduce = "reduce" if few else "swap"

    def added(pieces, got):
        if not few:
            return lax.psum(pieces, "dp")
        own = lax.dynamic_index_in_dim(pieces, lax.axis_index("dp"), 1, False)
        return (own.astype(F32) + got[0].astype(F32)).astype(BF)

    x_kinds = lambda n: ("half",) * n if few else ()
    x_arrays = lambda *arrays: arrays if few else ()
    d_act = gelu_back(dot_t(g3, w_down))[0].astype(BF)
    down_pieces = halved(split_grad(t_dot(hid, g3)))
    up_pieces = halved(t_dot(u3, d_act).astype(BF).reshape(NC, feat, -1))
    g2, dh2, gain3_rows, d_att, *got = link(
        3, d_act, w_up, mid_ff_back, (h2, gains[2:3], g3_mine), (one_f32, row8), w1_t=True, w2=w_o, w2_kind="in_t", post=post_plain,
        post_out=(((T, att), BF),), early=x_kinds(2), early_in=x_arrays(down_pieces, up_pieces))
    ff_sum = jnp.concatenate([added(down_pieces, got[:1]), added(up_pieces, got[1:])], axis=1)
    o_pieces = halved(split_grad(t_dot(attended, g2)))
    d_qkv, ff_split, *got = att_bwd(
        8, seq_lens, qkv, d_att, att_exact, lse, ("swap",) + x_kinds(1), (ff_sum,) + x_arrays(o_pieces))
    o_sum = added(o_pieces, got)
    qkv_pieces = halved(t_dot(u2, d_qkv).astype(BF).reshape(NC, feat, -1))
    g1_ext, dh1, gain2_rows, d_mix, ff_back, o_split, *got = link(
        4, d_qkv, w_qkv, functools.partial(mid_att_back, inner), (h1, gains[1:2], dh2, mix_out, gate_scale), (one_f32, row8), w1_t=True,
        w2=w_mix, w2_kind="in_t", post=post_plain, post_out=(((T, wide), F32),), extra=128,
        early=("spread", "swap") + x_kinds(1), early_in=(ff_split, o_sum) + x_arrays(qkv_pieces))
    qkv_sum = added(qkv_pieces, got)
    g1 = g1_ext[:, :D]
    mix_pieces = halved(split_grad(t_dot(mixg, g1)))
    d_in, tap_grads, row_grads, qkv_split = mixer_bwd(
        9, seq_lens, proj, cw, pv, y, states, d_mix, g1_ext, ("swap",), (qkv_sum,))
    in_grad = t_dot(u1, d_in)
    slabs, thin = rows * NC, bcdt_width + bcdt_pad
    four = D // thin
    zx_pieces, side = side_columns(in_grad, tap_grads, row_grads, gain2_rows, gain3_rows, S)
    zx_pieces = zx_pieces if few else zx_pieces.reshape(NC, feat, -1)
    rest_all, _, _, _, zx_back, mix_back, o_back, qkv_back, in_got, out_got = link(
        5, d_in, w_in, mid_mixer_back, (h0, gains[0:1], dh1), (((NC, S, feat), BF), row8), w1_t=True, side=side.reshape(T, thin), small=thin,
        early=(reduce, reduce, "spread", "spread"), early_in=(zx_pieces, mix_pieces, o_split, qkv_split), late=(("swap", 0),),
        more_sum=(hid, w_down), after=after_output, after_in=(h2, jnp.broadcast_to(my_valid, (S, 128))), after_out=(((NC, S, feat), BF),))
    output = out_got.reshape(NC * S, feat)
    four_d = lambda a: a if few else a.reshape(NC, 2, -1, a.shape[-1])
    if not few:
        n = ff_back.shape[1] // 2
        ff_back = jnp.concatenate([four_d(ff_back[:, :n]), four_d(ff_back[:, n:])], axis=2)
        zx_back, mix_back = lax.psum(zx_back, "dp"), lax.psum(mix_back, "dp")
    (x_grad, z_grad, q_grad, k_grad, v_grad, mix_grad, o_grad, up_grad, down_grad, bcdt_grad, gain2_sum, gain3_sum, cxw_sum, *lines) = finish(
        four_d(zx_back), four_d(mix_back), four_d(qkv_back), four_d(o_back), ff_back, rest_all.reshape(slabs, S, thin), bcdt_width,
        inner, n_heads)
    cxb_sum, gate_gain_sum, cbw_sum, cbb_sum, a_log_sum, d_skip_sum, dt_bias_sum, gain1_grad = lines
    bcdt_grad = bcdt_grad.T
    input_grad = in_got.reshape(NC * S, feat).astype(F32)
    return (output, input_grad, gain1_grad[0], z_grad, x_grad, bcdt_grad, cxw_sum, cxb_sum[0], cbw_sum, cbb_sum[0], a_log_sum[0],
            d_skip_sum[0], dt_bias_sum[0], gate_gain_sum[0], mix_grad, gain2_sum[0], q_grad, k_grad, v_grad, o_grad, gain3_sum[0],
            up_grad, down_grad)


def solution(mesh):
    assert mesh.shape["rows"] == 4 and mesh.shape["cols"] == NC
    token = P(("dp", "rows"), "cols")
    w_in, w_out = P("cols", "rows"), P("rows", "cols")
    row, col, whole = P("rows"), P("cols"), P()
    placed = (token, P("dp", None), col, w_in, w_in, P("cols", None), P(None, "rows"), row, whole, whole, row, row, row, row,
              w_out, col, w_in, w_in, w_in, w_out, col, w_in, w_out, token)
    given = (token, token, whole, w_in, w_in, whole, whole, whole, whole, whole, whole, whole, whole, whole, w_out, whole,
             w_in, w_in, w_in, w_out, whole, w_in, w_out)
    return jax.shard_map(per_device, mesh=mesh, in_specs=placed, out_specs=given, check_vma=False)
```
